32 devices in a mesh: dp: 8 (over z, x), sp: 4 (over y, core).
Axes of the slice: x: 2, y: 2, z: 4, core: 2. Of those that a mesh axis runs over, the one named last changes fastest.
Arguments:
- samples_hi: bfloat16 [8, 90, 180, 768], P('dp', None, 'sp'), may hold values from -6 to 6
- samples_lo: bfloat16 [32, 23, 45, 768], P(('dp', 'sp')), may hold values from -6 to 6
- cotan_hi: bfloat16 [8, 90, 180, 768], P('dp', None, 'sp'), may hold values from -6 to 6
- cotan_lo: bfloat16 [32, 23, 45, 768], P(('dp', 'sp')), may hold values from -6 to 6
- live_slots: int32 [32], P(('dp', 'sp')), may hold values 0 or 1
- spectral_w: float32 [3072, 96], P(('dp', 'sp')), may hold values from -0.4375 to 0.4375
- vectors: float32 [13, 768], P(None, ('dp', 'sp')), may hold values from 0.5 to 1.5
- weight_in: float32 [768, 3072], P(None, ('dp', 'sp')), may hold values from -0.21875 to 0.21875
- weight_out: float32 [3072, 768], P(('dp', 'sp')), may hold values from -0.109375 to 0.109375
- moment_spec: float32 [3072, 96], P(('dp', 'sp')), may hold values from -768 to 768
- moment_in: float32 [768, 3072], P(None, ('dp', 'sp')), may hold values from -768 to 768
- moment_out: float32 [3072, 768], P(('dp', 'sp')), may hold values from -768 to 768
- adam_first: float32 [13, 768], P(None, ('dp', 'sp')), may hold values from -128 to 128
- adam_second: float32 [13, 768], P(None, ('dp', 'sp')), may hold values from 16.272 to 65.088
Outputs:
- block_hi: bfloat16 [8, 90, 180, 768], P('dp', None, 'sp')
- block_lo: bfloat16 [32, 23, 45, 768], P(('dp', 'sp'))
- grad_hi: float32 [8, 90, 180, 768], P('dp', None, 'sp')
- grad_lo: float32 [32, 23, 45, 768], P(('dp', 'sp'))
- new_spectral: float32 [3072, 96], P(('dp', 'sp'))
- new_weight_in: float32 [768, 3072], P(None, ('dp', 'sp'))
- new_weight_out: float32 [3072, 768], P(('dp', 'sp'))
- new_moment_spec: float32 [3072, 96], P(('dp', 'sp'))
- new_moment_in: float32 [768, 3072], P(None, ('dp', 'sp'))
- new_moment_out: float32 [3072, 768], P(('dp', 'sp'))
- new_vectors: float32 [13, 768], P(None, ('dp', 'sp'))
- new_adam_first: float32 [13, 768], P(None, ('dp', 'sp'))
- new_adam_second: float32 [13, 768], P(None, ('dp', 'sp'))
The draws below stay inside these ranges and needn't reach their ends.
All inputs are finite; a program needn't handle non-finite values. No bound on the sum of `live_slots` on one device may be relied on, other than what follows from the above.
Results may differ from the reference program's by a relative error of at most 0.02.
Values may be sent and summed in bfloat16 or wider, within the bound.
A program may use at most 576 MiB of HBM per device.

```python
import math
import jax
import jax.numpy as jnp
from jax import lax

D = 768
FF = 3072
NB = 8
BS = 96
H = 90
W = 180
HL = 23
WL = 45
STEP = 10
NEWTON_STEPS = 5
NHI = 8
NLO = 32
TOK_ALL = 162720


def place_ends(entries, own_key, least, high):
    place = [jax.random.randint(jax.random.fold_in(own_key, axis), (), 0, length) for axis, length in enumerate(entries.shape)]
    longest = entries.shape.index(max(entries.shape))
    next_to = place[:longest] + [(place[longest] + 1) % entries.shape[longest]] + place[longest + 1:]
    return entries.at[tuple(place)].set(least).at[tuple(next_to)].set(high)


def shard_levels(stream_key, dims, pieces, least, largest):
    level = 1.0
    for dim, shards_of in pieces:
        steps = jax.random.uniform(jax.random.fold_in(jax.random.fold_in(stream_key, 6), dim), (shards_of,), jnp.float32, least / len(pieces), largest / len(pieces))
        level = level * jnp.repeat(jnp.exp(steps), dims[dim] // shards_of).reshape((-1,) + (1,) * (len(dims) - 1 - dim))
    return level


def centred(own_key, dims, deviation, reach, shards=(), kind=jnp.bfloat16):
    drawn = deviation * jax.random.normal(own_key, dims, jnp.float32)
    if shards:
        drawn = drawn * shard_levels(own_key, dims, shards, -0.22, 0.18)
    return jnp.clip(drawn, -reach, reach).astype(kind)


def setup_inputs(seed: int = 0) -> dict:
    streams_of = jax.random.split(jax.random.key(seed), 15)
    return {
        "samples_hi": centred(streams_of[0], (NHI, H, W, D), 1.0, 6.0, ((0, 8), (2, 4))),
        "samples_lo": centred(streams_of[1], (NLO, HL, WL, D), 1.0, 6.0, ((0, 32),)),
        "cotan_hi": centred(streams_of[2], (NHI, H, W, D), 1.0, 6.0, ((0, 8), (2, 4))),
        "cotan_lo": centred(streams_of[3], (NLO, HL, WL, D), 1.0, 6.0, ((0, 32),)),
        "live_slots": place_ends((jax.random.randint(streams_of[4], (NLO,), 0, 4) < 3).astype(jnp.int32), jax.random.fold_in(streams_of[4], 1), 0, 1),
        "spectral_w": centred(streams_of[5], (4 * NB * BS, BS), (2 * BS) ** -0.5, 0.4375, ((0, 32),), jnp.float32),
        "vectors": jnp.clip(0.5 + 1.0 * jax.random.uniform(streams_of[6], (13, D), jnp.float32) ** shard_levels(streams_of[6], (13, D), ((1, 32),), -0.2, 0.2), 0.5, 1.5),
        "weight_in": centred(streams_of[7], (D, FF), D ** -0.5, 0.21875, ((1, 32),), jnp.float32),
        "weight_out": centred(streams_of[8], (FF, D), FF ** -0.5, 0.109375, ((0, 32),), jnp.float32),
        "moment_spec": centred(streams_of[9], (4 * NB * BS, BS), (0.3 * TOK_ALL ** 0.5), 768.0, ((0, 32),), jnp.float32),
        "moment_in": centred(streams_of[10], (D, FF), (0.3 * TOK_ALL ** 0.5), 768.0, ((1, 32),), jnp.float32),
        "moment_out": centred(streams_of[11], (FF, D), (0.3 * TOK_ALL ** 0.5), 768.0, ((0, 32),), jnp.float32),
        "adam_first": centred(streams_of[12], (13, D), (0.05 * TOK_ALL ** 0.5), 128.0, ((1, 32),), jnp.float32),
        "adam_second": jnp.clip(jnp.exp(math.log(65.088) - 1.3862944 * jax.random.uniform(streams_of[13], (13, D), jnp.float32) ** shard_levels(streams_of[13], (13, D), ((1, 32),), -0.2, 0.2)), 16.272, 65.088),
    }


@jax.custom_vjp
def low(v):
    return lax.optimization_barrier(v.astype(jnp.bfloat16)).astype(jnp.float32)

@jax.custom_vjp
def low_back(v):
    return v

def low_keep(v):
    return (low(v), None)

def low_pass(kept, grad):
    return (grad,)

def back_keep(v):
    return (v, None)

def back_low(kept, grad):
    return (low(grad),)
low.defvjp(low_keep, low_pass)
low_back.defvjp(back_keep, back_low)
highest = lax.Precision.HIGHEST
epsilon = 1e-06
shrink_level = 0.01
shrink_sharp = 10.0
momentum = 0.95
newton_a = 3.4445
newton_b = -4.775
newton_c = 2.0315
muon_rate = 0.5
adam_rate = 0.3
decay = 0.01
beta_one = 0.9
beta_two = 0.999

def round_table(values):
    return lax.optimization_barrier(values.astype(jnp.bfloat16)).astype(jnp.float32)

def dft_pair(length):
    index = jnp.arange(length, dtype=jnp.int32)
    phase = index[:, None] * index[None, :] % length
    angle = phase.astype(jnp.float32) * (2.0 * math.pi / length)
    factor = 1.0 / math.sqrt(length)
    return (round_table(jnp.cos(angle) * factor), round_table(jnp.sin(angle) * factor))

def product(form, left, right):
    return jnp.einsum(form, left, right, precision=highest)

def layer_norm(values, gain, shift):
    center = values - lax.optimization_barrier(jnp.mean(values, axis=-1, keepdims=True))
    return center * lax.rsqrt(lax.optimization_barrier(jnp.mean(center * center, axis=-1, keepdims=True)) + epsilon) * gain + shift

def block_product(real_in, imag_in, weight_re, weight_im):
    real_out = product('nbi,bij->nbj', real_in, weight_re) - product('nbi,bij->nbj', imag_in, weight_im)
    imag_out = product('nbi,bij->nbj', real_in, weight_im) + product('nbi,bij->nbj', imag_in, weight_re)
    return (real_out, imag_out)

def forward_one(sample, params, tables):
    spectral_w, vectors, weight_in, weight_out = params
    cos_w, sin_w, cos_h, sin_h = tables
    biases = vectors[9:13].reshape(4, NB, BS)
    norm_one = layer_norm(sample, vectors[0], vectors[1])
    norm_low = low(norm_one)
    area_re = low(low_back(product('kw,hwd->khd', cos_w, norm_low)))
    area_im = low(low_back(-product('kw,hwd->khd', sin_w, norm_low)))
    four_re = low(low_back(product('mh,khd->kmd', cos_h, area_re) + product('mh,khd->kmd', sin_h, area_im)))
    four_im = low(low_back(product('mh,khd->kmd', cos_h, area_im) - product('mh,khd->kmd', sin_h, area_re)))
    shape = four_re.shape
    weights = low(spectral_w).reshape(2, 2, NB, BS, BS)
    first_re, first_im = block_product(four_re.reshape(-1, NB, BS), four_im.reshape(-1, NB, BS), weights[0, 0], weights[0, 1])
    first_re = low_back(first_re + biases[0])
    first_im = low_back(first_im + biases[1])
    act_re = low(jax.nn.gelu(first_re))
    act_im = low(jax.nn.gelu(first_im))
    second_re, second_im = block_product(act_re, act_im, weights[1, 0], weights[1, 1])
    second_re = low_back(second_re + biases[2])
    second_im = low_back(second_im + biases[3])
    shrunk_re = low(second_re - shrink_level * jnp.tanh(shrink_sharp * second_re)).reshape(shape)
    shrunk_im = low(second_im - shrink_level * jnp.tanh(shrink_sharp * second_im)).reshape(shape)
    back_re = low(low_back(product('mh,kmd->khd', cos_h, shrunk_re) - product('mh,kmd->khd', sin_h, shrunk_im)))
    back_im = low(low_back(product('mh,kmd->khd', cos_h, shrunk_im) + product('mh,kmd->khd', sin_h, shrunk_re)))
    filtered = low_back(product('kw,khd->hwd', cos_w, back_re) - product('kw,khd->hwd', sin_w, back_im))
    mixed = filtered + norm_one + sample
    norm_two = low(layer_norm(mixed, vectors[2], vectors[3]))
    hidden = low_back(product('hwd,df->hwf', norm_two, low(weight_in)) + vectors[5:9].reshape(FF))
    active = low(jax.nn.gelu(hidden))
    return mixed + (product('hwf,fd->hwd', active, low(weight_out)) + vectors[4])

def newton(matrix, left_side):
    current = matrix / (jnp.sqrt(jnp.sum(matrix * matrix)) + 1e-07)
    for newton_turn in range(NEWTON_STEPS):
        if left_side:
            gram = jnp.dot(current, current.T, precision=highest)
            once = jnp.dot(gram, current, precision=highest)
            twice = jnp.dot(gram, once, precision=highest)
        else:
            gram = jnp.dot(current.T, current, precision=highest)
            once = jnp.dot(current, gram, precision=highest)
            twice = jnp.dot(once, gram, precision=highest)
        current = newton_a * current + newton_b * once + newton_c * twice
    return current

def reference(samples_hi, samples_lo, cotan_hi, cotan_lo, live_slots, spectral_w, vectors, weight_in, weight_out, moment_spec, moment_in, moment_out, adam_first, adam_second):
    params = (spectral_w, vectors, weight_in, weight_out)
    tables_hi = dft_pair(W) + dft_pair(H)
    tables_lo = dft_pair(WL) + dft_pair(HL)

    def make_step(tables):

        def one_sample(totals, sample_pair):
            sample, cotangent = sample_pair
            result, pullback = jax.vjp(lambda part_x, part_p: forward_one(part_x, part_p, tables), sample.astype(jnp.float32), params)
            grad_sample, grad_params = pullback(cotangent)
            totals = jax.tree.map(lambda left, right: left + right, totals, grad_params)
            return (totals, (result.astype(jnp.bfloat16), grad_sample))
        return one_sample
    totals = jax.tree.map(jnp.zeros_like, params)
    totals, (block_hi, grad_hi) = lax.scan(make_step(tables_hi), totals, (samples_hi, cotan_hi.astype(jnp.float32)))
    live_weight = live_slots.astype(jnp.float32)[:, None, None, None]
    totals, (block_lo, grad_lo) = lax.scan(make_step(tables_lo), totals, (samples_lo, cotan_lo.astype(jnp.float32) * live_weight))
    grad_spec, grad_vectors, grad_in, grad_out = totals
    new_moment_spec = momentum * moment_spec + grad_spec
    new_moment_in = momentum * moment_in + grad_in
    new_moment_out = momentum * moment_out + grad_out
    dir_spec = grad_spec + momentum * new_moment_spec
    dir_in = grad_in + momentum * new_moment_in
    dir_out = grad_out + momentum * new_moment_out
    orth_in = newton(dir_in, True)
    orth_out = newton(dir_out, False)
    orth_spec = jax.vmap(lambda matrix: newton(matrix, False))(dir_spec.reshape(4 * NB, BS, BS)).reshape(4 * NB * BS, BS)
    keep = 1.0 - muon_rate * decay
    new_weight_in = weight_in * keep - muon_rate * orth_in
    new_weight_out = weight_out * keep - muon_rate * math.sqrt(max(1.0, FF / D)) * orth_out
    new_spectral = spectral_w * keep - muon_rate * orth_spec
    new_adam_first = beta_one * adam_first + (1.0 - beta_one) * grad_vectors
    new_adam_second = beta_two * adam_second + (1.0 - beta_two) * grad_vectors * grad_vectors
    first_hat = new_adam_first / (1.0 - beta_one ** STEP)
    second_hat = new_adam_second / (1.0 - beta_two ** STEP)
    new_vectors = vectors * (1.0 - adam_rate * decay) - adam_rate * first_hat / (jnp.sqrt(second_hat) + 1e-08)
    return (block_hi, block_lo, grad_hi, grad_lo, new_spectral, new_weight_in, new_weight_out, new_moment_spec, new_moment_in, new_moment_out, new_vectors, new_adam_first, new_adam_second)
```

```python
import functools
import math

import jax
import jax.numpy as jnp
import numpy as np
from jax import lax
from jax.experimental import pallas as pl
from jax.experimental.pallas import tpu as pltpu
from jax.sharding import PartitionSpec as P

D = 768
FF = 3072
NB = 8
BS = 96
H = 90
W = 180
HL = 23
WL = 45
STEP = 10
NEWTON_STEPS = 5

F32 = jnp.float32
BF = jnp.bfloat16
highest = lax.Precision.HIGHEST
epsilon = 1e-06
shrink_level = 0.01
shrink_sharp = 10.0
momentum = 0.95
newton_a = 3.4445
newton_b = -4.775
newton_c = 2.0315
muon_rate = 0.5
adam_rate = 0.3
decay = 0.01
beta_one = 0.9
beta_two = 0.999

K0 = math.sqrt(2.0 / math.pi)
K1 = K0 * 0.044715

SPLIT = 4
GD = D // SPLIT
PAIR = 2 * GD
HALF = H // 2
OWN = W // SPLIT
PW = 48
PM = 96
KF = W // 2 + 1
KP = 96
KG = 7
GROUPS = KF // KG
ROWS = KG * PM
LM = 24
LK = 24
LROWS = LK * LM
HB = 5
LB = 8
FC = 512
NC = FF // FC
VMEM_LIMIT = 60 * 2**20


def wave(length, rows, cols):
    phase = np.outer(rows, cols) % length
    angle = phase * (2.0 * math.pi / length)
    factor = 1.0 / math.sqrt(length)
    return np.cos(angle) * factor, np.sin(angle) * factor


def tables():
    wide = np.zeros((SPLIT, 2 * KP, SPLIT * PW))
    for s in range(SPLIT):
        for j in range(SPLIT):
            cols = (s ^ j) * OWN + np.arange(OWN)
            c, d = wave(W, np.arange(KF), cols)
            wide[s, :KF, j * PW : j * PW + OWN] = c
            wide[s, KP : KP + KF, j * PW : j * PW + OWN] = -d
    tall = np.zeros((2 * PM, 2 * PM))
    for part in range(2):
        c, d = wave(H, np.arange(H), part * HALF + np.arange(HALF))
        re, im = part * PW, PM + part * PW
        tall[:H, re : re + HALF] = c
        tall[:H, im : im + HALF] = d
        tall[PM : PM + H, re : re + HALF] = -d
        tall[PM : PM + H, im : im + HALF] = c
    wide_lo = np.zeros((2 * LK, PW))
    c, d = wave(WL, np.arange(WL // 2 + 1), np.arange(WL))
    wide_lo[: WL // 2 + 1, :WL] = c
    wide_lo[LK : LK + WL // 2 + 1, :WL] = -d
    tall_lo = np.zeros((2 * LM, 2 * LM))
    c, d = wave(HL, np.arange(HL), np.arange(HL))
    tall_lo[:HL, :HL] = c
    tall_lo[:HL, LM : LM + HL] = d
    tall_lo[LM : LM + HL, :HL] = -d
    tall_lo[LM : LM + HL, LM : LM + HL] = c
    return wide, tall, wide_lo, tall_lo


def dot(left, right):
    return jnp.dot(left, right, preferred_element_type=F32)


def dot_nt(left, right):
    return lax.dot_general(left, right, (((1,), (1,)), ((), ())), preferred_element_type=F32)


def dot_tn(left, right):
    return lax.dot_general(left, right, (((0,), (0,)), ((), ())), preferred_element_type=F32)


def normed(values):
    center = values - jnp.mean(values, axis=-1, keepdims=True)
    scale = lax.rsqrt(jnp.mean(center * center, axis=-1, keepdims=True) + epsilon)
    return center * scale, scale


def norm_back(grad, norm, scale, gain):
    pushed = grad * gain
    return scale * (
        pushed
        - jnp.mean(pushed, axis=-1, keepdims=True)
        - norm * jnp.mean(pushed * norm, axis=-1, keepdims=True)
    )


def pad_rows(values):
    return jnp.concatenate(
        [values, jnp.zeros((PW - values.shape[0], values.shape[1]), values.dtype)], axis=0
    )


def lanes(*pieces):
    return jnp.concatenate(pieces, axis=1)


def unpack_pair(fs):
    pieces = [fs[g].astype(F32) for g in range(SPLIT)]
    return (
        lanes(*[p[:, :GD] for p in pieces]),
        lanes(*[p[:, GD:] for p in pieces]),
    )


def pack_pair(row_a, row_b, fs):
    for g in range(SPLIT):
        cut = slice(g * GD, (g + 1) * GD)
        fs[g] = lanes(row_a[:, cut], row_b[:, cut]).astype(BF)


VM = pl.BlockSpec(memory_space=pltpu.VMEM)
SM = pl.BlockSpec(memory_space=pltpu.SMEM)
ANY = pl.BlockSpec(memory_space=pl.ANY)


def params():
    return pltpu.CompilerParams(vmem_limit_bytes=VMEM_LIMIT)


def shape(dims, kind):
    return jax.ShapeDtypeStruct(dims, kind)


PACKED = (HALF, PW, PAIR)
PACKED_BLOCK = pl.BlockSpec((HB, PW, PAIR), lambda i: (i, 0, 0))
WIDE_BLOCK = pl.BlockSpec((2, HB, OWN, D), lambda i: (0, i, 0, 0))


def pack_kernel(own_ref, x_ref, vec_ref, o0, o1, o2, o3, fs):
    own = own_ref[0]
    gain, shift = vec_ref[0:1, :], vec_ref[1:2, :]

    def one(i, _):
        rows = []
        for part in range(2):
            norm, _unused = normed(x_ref[part, i].astype(F32))
            rows.append(pad_rows(norm * gain + shift))
        pack_pair(rows[0], rows[1], fs)
        for j, out in enumerate((o0, o1, o2, o3)):
            out[i] = fs[own ^ j]
        return 0

    lax.fori_loop(0, HB, one, 0)


def norm_packed(own, samples, vectors):
    return pl.pallas_call(
        pack_kernel,
        grid=(HALF // HB,),
        in_specs=[SM, WIDE_BLOCK, VM],
        out_specs=[PACKED_BLOCK] * SPLIT,
        out_shape=[shape(PACKED, BF)] * SPLIT,
        scratch_shapes=[pltpu.VMEM((SPLIT, PW, PAIR), BF)],
        compiler_params=params(),
        name="norm_pack",
    )(own, samples, vectors)


def exchange(slabs):
    moved = [slabs[0]]
    for j in range(1, SPLIT):
        moved.append(lax.ppermute(slabs[j], "sp", [(i, i ^ j) for i in range(SPLIT)]))
    return moved


def to_freq_wide(slabs, table, space):
    def one(i, _):
        rows = jnp.concatenate([slab[i] for slab in slabs], axis=0)
        area = dot(table[...], rows)
        for c in range(3):
            space[c, pl.ds(i, 2 * KP, stride=PW), :] = area[:, c * 128 : (c + 1) * 128]
        return 0

    lax.fori_loop(0, HALF, one, 0)


def to_freq_tall(k, table, space):
    re = lanes(*[space[c, pl.ds(pl.multiple_of(k * PW, PW), PW), :] for c in range(3)])
    im = lanes(*[space[c, pl.ds(pl.multiple_of((KP + k) * PW, PW), PW), :] for c in range(3)])
    rows = jnp.concatenate([re[:, :GD], re[:, GD:], im[:, :GD], im[:, GD:]], axis=0)
    return dot(table[...], rows.astype(BF))


def to_space_tall(k, table, four, space):
    back = dot(table[...], four)
    for part in range(2):
        base = part * PM
        packed = lanes(back[base : base + PW], back[base + PW : base + PM])
        at = pl.ds(pl.multiple_of((part * KP + k) * PW, PW), PW)
        for c in range(3):
            space[c, at, :] = packed[:, c * 128 : (c + 1) * 128]


def to_space_wide(table, space, outs):
    def one(i, _):
        rows = lanes(*[space[c, pl.ds(i, 2 * KP, stride=PW), :] for c in range(3)])
        field = dot(table[...], rows.astype(BF)).astype(BF)
        for j, out in enumerate(outs):
            out[i] = field[j * PW : (j + 1) * PW]
        return 0

    lax.fori_loop(0, HALF, one, 0)


def clear(ref):
    def one(i, _):
        for c in range(ref.shape[0]):
            ref[c, pl.ds(pl.multiple_of(i * 192, 192), 192), :] = jnp.zeros((192, 128), F32)
        return 0

    lax.fori_loop(0, ref.shape[1] // 192, one, 0)


def keep_minus(row, width, first, last):
    at = row + lax.broadcasted_iota(jnp.int32, (width, 1), 0)
    return jnp.where((at >= first) & (at < last), 1.0, 0.0).astype(F32)


def mlp_forward(fre, fim, wu, wv, w1, bias, us, vs, actp, actm, put, base, first, last, chunk):
    rows = us.shape[0]
    us[...] = dot(fre, wu)
    vs[...] = dot(fim, wv)
    b0, b1 = bias[0:1, :], bias[1:2, :]

    def act(i, _):
        at = pl.ds(pl.multiple_of(i * chunk, chunk), chunk)
        u = us[at, :] + b0
        v = vs[at, :]
        for ref, value in ((actp, u + v), (actm, u - v)):
            t = jnp.tanh(value * (K0 + K1 * (value * value)))
            ref[at, :] = (value * (0.5 + 0.5 * t)).astype(BF)
        return 0

    lax.fori_loop(0, rows // chunk, act, 0)
    us[...] = dot(actp[...], w1)
    vs[...] = dot(actm[...], w1)

    def shrunk(i, _):
        at = pl.ds(pl.multiple_of(i * chunk, chunk), chunk)
        p = us[at, :] + b1
        m = vs[at, :] + b1
        p = p - shrink_level * jnp.tanh(shrink_sharp * p)
        m = (m - shrink_level * jnp.tanh(shrink_sharp * m)) * keep_minus(
            base + i * chunk, chunk, first, last
        )
        put(at, (p[:, :GD] + m[:, :GD]).astype(BF), (p[:, GD:] - m[:, GD:]).astype(BF))
        return 0

    lax.fori_loop(0, rows // chunk, shrunk, 0)


def mlp_backward(
    fre, fim, gs, wu, wv, w1, bias, us, vs, actp, actm, dp, dm, gsp, gsm, sums, put,
    gwu, gwv, gw1, ge, base, first, last, chunk,
):
    rows = us.shape[0]
    us[...] = dot(fre, wu)
    vs[...] = dot(fim, wv)
    b0, b1 = bias[0:1, :], bias[1:2, :]
    sign = jnp.where(lax.broadcasted_iota(jnp.int32, (1, PAIR), 1) < GD, 1.0, -1.0).astype(F32)

    def act(i, _):
        at = pl.ds(pl.multiple_of(i * chunk, chunk), chunk)
        u = us[at, :] + b0
        v = vs[at, :]
        for ref, slope, value in ((actp, dp, u + v), (actm, dm, u - v)):
            square = value * value
            hp = 0.5 + 0.5 * jnp.tanh(value * (K0 + K1 * square))
            on = value * hp
            ref[at, :] = on.astype(BF)
            slope[at, :] = hp + on * (1.0 - hp) * (2.0 * K0 + 6.0 * K1 * square)
        return 0

    lax.fori_loop(0, rows // chunk, act, 0)
    us[...] = dot(actp[...], w1)
    vs[...] = dot(actm[...], w1)

    def second(i, total):
        at = pl.ds(pl.multiple_of(i * chunk, chunk), chunk)
        grad = gs[at, :]
        tp = jnp.tanh(shrink_sharp * (us[at, :] + b1))
        tm = jnp.tanh(shrink_sharp * (vs[at, :] + b1))
        flat = 1.0 - shrink_level * shrink_sharp
        bend = shrink_level * shrink_sharp
        p = grad * (flat + bend * (tp * tp))
        m = (grad * (sign * keep_minus(base + i * chunk, chunk, first, last))) * (
            flat + bend * (tm * tm)
        )
        gsp[at, :] = p.astype(BF)
        gsm[at, :] = m.astype(BF)
        return total + jnp.sum(p + m, axis=0, keepdims=True)

    ge[1:2, :] += lax.fori_loop(0, rows // chunk, second, jnp.zeros((1, PAIR), F32))
    us[...] = dot_nt(gsp[...], w1)
    vs[...] = dot_nt(gsm[...], w1)
    gw1[...] += dot_tn(actp[...], gsp[...]) + dot_tn(actm[...], gsm[...])

    def first_grad(i, total):
        at = pl.ds(pl.multiple_of(i * chunk, chunk), chunk)
        p = us[at, :] * dp[at, :]
        m = vs[at, :] * dm[at, :]
        both = p + m
        gsp[at, :] = both.astype(BF)
        gsm[at, :] = (p - m).astype(BF)
        return total + jnp.sum(both, axis=0, keepdims=True)

    ge[0:1, :] += lax.fori_loop(0, rows // chunk, first_grad, jnp.zeros((1, PAIR), F32))
    gwu[...] += dot_tn(fre, gsp[...])
    gwv[...] += dot_tn(fim, gsm[...])
    put(dot_nt(gsp[...], wu).astype(BF), dot_nt(gsm[...], wv).astype(BF))


def block_grads(gwu, gwv, gw1):
    cells = {}
    for b in range(2):
        r = slice(b * BS, (b + 1) * BS)
        i = slice(GD + b * BS, GD + (b + 1) * BS)
        cells[0, 0, b] = gwu[r, r] + gwv[r, i]
        cells[0, 1, b] = gwu[r, i] - gwv[r, r]
        cells[1, 0, b] = gw1[r, r] + gw1[i, i]
        cells[1, 1, b] = gw1[r, i] - gw1[i, r]
    return cells


def filter_kernel(
    x0, x1, x2, x3, tw, twt, th, tht, wu, wv, w1, bias,
    y0, y1, y2, y3, four, space, us, vs, actp, actm, zr, zi,
):
    clear(space)
    to_freq_wide((x0, x1, x2, x3), tw, space)

    def group(g, _):
        for n in range(KG):
            rows = to_freq_tall(g * KG + n, th, space).astype(BF)
            four[g, 0, n * PM : (n + 1) * PM, :] = rows[:PM]
            four[g, 1, n * PM : (n + 1) * PM, :] = rows[PM:]

        def put(at, re, im):
            zr[at, :] = re
            zi[at, :] = im

        mlp_forward(
            four[g, 0], four[g, 1], wu[...], wv[...], w1[...], bias, us, vs, actp, actm, put,
            g * ROWS, PM, (KF - 1) * PM, PM // 2,
        )
        for n in range(KG):
            at = slice(n * PM, (n + 1) * PM)
            to_space_tall(
                g * KG + n, tht, jnp.concatenate([zr[at, :], zi[at, :]], axis=0), space
            )
        return 0

    lax.fori_loop(0, GROUPS, group, 0)
    to_space_wide(twt, space, (y0, y1, y2, y3))


def filter_scratch(rows, wide):
    big = pltpu.VMEM((rows, PAIR), F32)
    low = pltpu.VMEM((rows, PAIR), BF)
    part = pltpu.VMEM((rows, GD), BF)
    return big, low, part


def filter_forward(slabs, tabs, weights, bias):
    big, low, part = filter_scratch(ROWS, None)
    outs = pl.pallas_call(
        filter_kernel,
        in_specs=[VM] * 12,
        out_specs=[VM] * 5,
        out_shape=[shape(PACKED, BF)] * SPLIT + [shape((GROUPS, 2, ROWS, GD), BF)],
        scratch_shapes=[pltpu.VMEM((3, 2 * KP * PW, 128), F32), big, big, low, low, part, part],
        compiler_params=params(),
        name="filter_forward",
    )(*slabs, *tabs, *weights, bias)
    return outs[:SPLIT], outs[SPLIT]


def filter_back_kernel(
    own_ref, x0, x1, x2, x3, four, tw, twt, th, tht, wu, wv, w1, bias, grads_in,
    y0, y1, y2, y3, grads, ge,
    space, us, vs, actp, actm, zr, zi, gs, dp, dm, gsp, gsm, gwu, gwv, gw1,
):
    clear(space)
    gwu[...] = jnp.zeros_like(gwu)
    gwv[...] = jnp.zeros_like(gwv)
    gw1[...] = jnp.zeros_like(gw1)
    ge[...] = jnp.zeros_like(ge)
    to_freq_wide((x0, x1, x2, x3), tw, space)

    def group(g, _):
        for n in range(KG):
            rows = to_freq_tall(g * KG + n, th, space)
            gs[n * PM : (n + 1) * PM, :] = lanes(rows[:PM], rows[PM:])

        def put(re, im):
            zr[...] = re
            zi[...] = im

        mlp_backward(
            four[g, 0], four[g, 1], gs, wu[...], wv[...], w1[...], bias, us, vs, actp, actm, dp, dm,
            gsp, gsm, None, put, gwu, gwv, gw1, ge, g * ROWS, PM, (KF - 1) * PM, PM // 2,
        )
        for n in range(KG):
            at = slice(n * PM, (n + 1) * PM)
            to_space_tall(
                g * KG + n, tht, jnp.concatenate([zr[at, :], zi[at, :]], axis=0), space
            )
        return 0

    lax.fori_loop(0, GROUPS, group, 0)
    grads[...] = grads_in[...]
    own = own_ref[0]
    for (layer, part, b), value in block_grads(gwu, gwv, gw1).items():
        grads[(2 * layer + part) * NB + 2 * own + b] += value
    to_space_wide(twt, space, (y0, y1, y2, y3))


def filter_backward(own, slabs, four, tabs, weights, bias, grads_in):
    big, low, part = filter_scratch(ROWS, None)
    outs = pl.pallas_call(
        filter_back_kernel,
        in_specs=[SM] + [VM] * 14,
        out_specs=[VM] * 6,
        out_shape=[shape(PACKED, BF)] * SPLIT
        + [shape((4 * NB, BS, BS), F32), shape((2, PAIR), F32)],
        scratch_shapes=[pltpu.VMEM((3, 2 * KP * PW, 128), F32), big, big, low, low, part, part]
        + [big, big, big, low, low]
        + [pltpu.VMEM((GD, PAIR), F32)] * 2
        + [pltpu.VMEM((PAIR, PAIR), F32)],
        compiler_params=params(),
        name="filter_backward",
    )(own, *slabs, four, *tabs, *weights, bias, grads_in)
    return outs[:SPLIT], outs[SPLIT], outs[SPLIT + 1]


def lo_freq_wide(i, rows, table, space):
    area = dot(table[...], rows)
    for c in range(6):
        space[c, pl.ds(i, 2 * LK, stride=LM), :] = area[:, c * 128 : (c + 1) * 128]


def lo_freq_tall(k, table, space):
    pair = []
    for n in range(2):
        parts = []
        for base in (0, LK):
            at = pl.ds(pl.multiple_of((base + 2 * k + n) * LM, LM), LM)
            parts.append(lanes(*[space[c, at, :] for c in range(6)]))
        pair.append(dot(table[...], jnp.concatenate(parts, axis=0).astype(BF)))
    re = jnp.concatenate([p[:LM] for p in pair], axis=0)
    im = jnp.concatenate([p[LM:] for p in pair], axis=0)
    return re, im


def lo_space_tall(k, table, re, im, space):
    for n in range(2):
        cut = slice(n * LM, (n + 1) * LM)
        rows = jnp.concatenate([re[cut], im[cut]], axis=0).astype(BF)
        back = dot(table[...], rows)
        for part, base in enumerate((0, LK)):
            at = pl.ds(pl.multiple_of((base + 2 * k + n) * LM, LM), LM)
            for c in range(6):
                space[c, at, :] = back[part * LM : (part + 1) * LM, c * 128 : (c + 1) * 128]


def lo_space_wide(i, table, space):
    rows = lanes(*[space[c, pl.ds(i, 2 * LK, stride=LM), :] for c in range(6)])
    return dot(table[...], rows.astype(BF))


def filter_lo_kernel(
    x_ref, vec_ref, tw, twt, th, tht, wu, wv, w1, bias, y_ref, four,
    space, us, vs, actp, actm, zr, zi,
):
    clear(space)
    gain, shift = vec_ref[0:1, :], vec_ref[1:2, :]

    def wide(i, _):
        norm, _unused = normed(x_ref[i].astype(F32))
        lo_freq_wide(i, pad_rows(norm * gain + shift).astype(BF), tw, space)
        return 0

    lax.fori_loop(0, HL, wide, 0)

    def tall(k, _):
        re, im = lo_freq_tall(k, th, space)
        at = pl.ds(pl.multiple_of(k * PW, PW), PW)
        for g in range(SPLIT):
            cut = slice(g * GD, (g + 1) * GD)
            four[g, 0, at, :] = re[:, cut].astype(BF)
            four[g, 1, at, :] = im[:, cut].astype(BF)
        return 0

    lax.fori_loop(0, LK // 2, tall, 0)

    def group(g, _):
        def put(at, re, im):
            zr[g, at, :] = re
            zi[g, at, :] = im

        mlp_forward(
            four[g, 0], four[g, 1], wu[g], wv[g], w1[g], bias.at[g], us, vs, actp, actm, put,
            0, LM, LROWS, PW,
        )
        return 0

    lax.fori_loop(0, SPLIT, group, 0)

    def back(k, _):
        at = pl.ds(pl.multiple_of(k * PW, PW), PW)
        re = lanes(*[zr[g, at, :].astype(F32) for g in range(SPLIT)])
        im = lanes(*[zi[g, at, :].astype(F32) for g in range(SPLIT)])
        lo_space_tall(k, tht, re, im, space)
        return 0

    lax.fori_loop(0, LK // 2, back, 0)

    def last(i, _):
        y_ref[i] = lo_space_wide(i, twt, space).astype(BF)
        return 0

    lax.fori_loop(0, HL, last, 0)
    y_ref[HL] = jnp.zeros((PW, D), BF)


def lo_scratch():
    big, low, _ = filter_scratch(LROWS, None)
    part = pltpu.VMEM((SPLIT, LROWS, GD), BF)
    return [pltpu.VMEM((6, 2 * LK * LM, 128), F32), big, big, low, low, part, part]


def filter_forward_lo(samples, vectors, tabs, weights, bias):
    return pl.pallas_call(
        filter_lo_kernel,
        in_specs=[VM] * 10,
        out_specs=[VM] * 2,
        out_shape=[shape((LM, PW, D), BF), shape((SPLIT, 2, LROWS, GD), BF)],
        scratch_shapes=lo_scratch(),
        compiler_params=params(),
        name="filter_forward_lo",
    )(samples, vectors, *tabs, *weights, bias)


def filter_back_lo_kernel(
    x_ref, gm_ref, four, vec_ref, tw, twt, th, tht, wu, wv, w1, bias,
    grad_ref, grads, ge, gvec,
    space, us, vs, actp, actm, zr, zi, gs, dp, dm, gsp, gsm, gwu, gwv, gw1,
):
    clear(space)
    ge[...] = jnp.zeros_like(ge)
    gvec[...] = jnp.zeros_like(gvec)

    def wide(i, _):
        lo_freq_wide(i, gm_ref[i], tw, space)
        return 0

    lax.fori_loop(0, HL, wide, 0)

    def tall(k, _):
        re, im = lo_freq_tall(k, th, space)
        at = pl.ds(pl.multiple_of(k * PW, PW), PW)
        for g in range(SPLIT):
            cut = slice(g * GD, (g + 1) * GD)
            gs[g, at, :] = lanes(re[:, cut], im[:, cut])
        return 0

    lax.fori_loop(0, LK // 2, tall, 0)

    def group(g, _):
        gwu[...] = jnp.zeros_like(gwu)
        gwv[...] = jnp.zeros_like(gwv)
        gw1[...] = jnp.zeros_like(gw1)

        def put(re, im):
            zr[g] = re
            zi[g] = im

        mlp_backward(
            four[g, 0], four[g, 1], gs.at[g], wu[g], wv[g], w1[g], bias.at[g], us, vs, actp, actm,
            dp, dm, gsp, gsm, None, put, gwu, gwv, gw1, ge.at[g], 0, LM, LROWS, PW,
        )
        for (layer, part, b), value in block_grads(gwu, gwv, gw1).items():
            grads[(2 * layer + part) * NB + 2 * g + b] = value
        return 0

    lax.fori_loop(0, SPLIT, group, 0)

    def back(k, _):
        at = pl.ds(pl.multiple_of(k * PW, PW), PW)
        re = lanes(*[zr[g, at, :].astype(F32) for g in range(SPLIT)])
        im = lanes(*[zi[g, at, :].astype(F32) for g in range(SPLIT)])
        lo_space_tall(k, tht, re, im, space)
        return 0

    lax.fori_loop(0, LK // 2, back, 0)
    gain = vec_ref[0:1, :]

    def last(i, _):
        field = lo_space_wide(i, twt, space)[:WL]
        direct = gm_ref[i].astype(F32)[:WL]
        norm, scale = normed(x_ref[i].astype(F32))
        grad = field + direct
        gvec[0:1, :] += jnp.sum(grad * norm, axis=0, keepdims=True)
        gvec[1:2, :] += jnp.sum(grad, axis=0, keepdims=True)
        grad_ref[i] = direct + norm_back(grad, norm, scale, gain)
        return 0

    lax.fori_loop(0, HL, last, 0)


def filter_backward_lo(samples, grad_mixed, four, vectors, tabs, weights, bias):
    big, low, _ = filter_scratch(LROWS, None)
    return pl.pallas_call(
        filter_back_lo_kernel,
        in_specs=[VM] * 12,
        out_specs=[VM] * 4,
        out_shape=[
            shape((HL, WL, D), F32),
            shape((4 * NB, BS, BS), F32),
            shape((SPLIT, 2, PAIR), F32),
            shape((2, D), F32),
        ],
        scratch_shapes=lo_scratch()
        + [pltpu.VMEM((SPLIT, LROWS, PAIR), F32), big, big, low, low]
        + [pltpu.VMEM((GD, PAIR), F32)] * 2
        + [pltpu.VMEM((PAIR, PAIR), F32)],
        compiler_params=params(),
        name="filter_backward_lo",
    )(samples, grad_mixed, four, vectors, *tabs, *weights, bias)


def feed_chunks(n2, cots, c1_ref, win, wout, out_acc, gn_acc, gwi, gwo, gc1):
    out_acc[...] = jnp.zeros_like(out_acc)
    gn_acc[...] = jnp.zeros_like(gn_acc)

    def chunk(c, _):
        rows = pl.ds(pl.multiple_of(c * FC, FC), FC)
        low, cot = n2[...], cots[...]
        wi, wo = win[rows, :], wout[rows, :]
        hidden = dot_nt(low, wi) + c1_ref[pl.ds(c, 1), :]
        grad = dot_nt(cot, wo)
        square = hidden * hidden
        hp = 0.5 + 0.5 * jnp.tanh(hidden * (K0 + K1 * square))
        act = hidden * hp
        grad = grad * (hp + act * (1.0 - hp) * (2.0 * K0 + 6.0 * K1 * square))
        gc1[pl.ds(c, 1), :] += jnp.sum(grad, axis=0, keepdims=True)
        act = act.astype(BF)
        grad = grad.astype(BF)
        out_acc[...] += dot(act, wo)
        gn_acc[...] += dot(grad, wi)
        gwo[rows, :] += dot_tn(act, cot)
        gwi[rows, :] += dot_tn(grad, low)
        return 0

    lax.fori_loop(0, NC, chunk, 0)


def feed_kernel(high, own_ref, live_ref, *refs):
    count = SPLIT if high else 1
    x_ref, cot_ref = refs[:2]
    fields = refs[2 : 2 + count]
    rest = refs[2 + count :]
    vec_ref, c1_ref, win, wout = rest[:4]
    rest = rest[4:]
    if high:
        gwi0, gwo0, gc1_in, gv_in = rest[:4]
        rest = rest[4:]
    block_ref = rest[0]
    packs = rest[1 : 1 + count]
    gwi_out, gwo_out, gc1, gv, gwi, gwo, sem, mixed, n2, cots, out_acc, gn_acc, fs = rest[1 + count :]
    step = pl.program_id(0)

    @pl.when(step == 0)
    def _():
        if high:
            loads = [
                pltpu.make_async_copy(gwi0, gwi, sem.at[0]),
                pltpu.make_async_copy(gwo0, gwo, sem.at[1]),
            ]
            for load in loads:
                load.start()
            for load in loads:
                load.wait()
            gc1[...] = gc1_in[...]
            gv[...] = gv_in[...]
        else:
            gwi[...] = jnp.zeros_like(gwi)
            gwo[...] = jnp.zeros_like(gwo)
            gc1[...] = jnp.zeros_like(gc1)
            gv[...] = jnp.zeros_like(gv)

    own = own_ref[0]
    gain_one, shift_one = vec_ref[0:1, :], vec_ref[1:2, :]
    gain_two, shift_two = vec_ref[2:3, :], vec_ref[3:4, :]
    bias_out = vec_ref[4:5, :]

    def enter(plane, x, cot, field):
        at = pl.ds(pl.multiple_of(plane * PW, PW), PW)
        norm, _unused = normed(x)
        total = field + (norm * gain_one + shift_one) + x
        mixed[at, :] = total
        norm, _unused = normed(total)
        n2[at, :] = (norm * gain_two + shift_two).astype(BF)
        cots[at, :] = cot.astype(BF)

    def leave(plane):
        at = pl.ds(pl.multiple_of(plane * PW, PW), PW)
        total = mixed[at, :]
        out = total + (out_acc[at, :] + bias_out)
        norm, scale = normed(total)
        grad = gn_acc[at, :]
        cot = cots[at, :].astype(F32)
        gv[0:1, :] += jnp.sum(grad * norm, axis=0, keepdims=True)
        gv[1:2, :] += jnp.sum(grad, axis=0, keepdims=True)
        gv[2:3, :] += jnp.sum(cot, axis=0, keepdims=True)
        return out.astype(BF), cot + norm_back(grad, norm, scale, gain_two)

    if high:

        def before(i, _):
            for j in range(SPLIT):
                fs[own ^ j] = fields[j][i]
            for part, field in enumerate(unpack_pair(fs)):
                x = pad_rows(x_ref[part, i].astype(F32))
                cot = pad_rows(cot_ref[part, i].astype(F32))
                enter(part * HB + i, x, cot, field)
            return 0

        def after(i, _):
            grads = []
            for part in range(2):
                out, grad = leave(part * HB + i)
                block_ref[part, i] = out[:OWN]
                grads.append(grad)
            pack_pair(grads[0], grads[1], fs)
            for j in range(SPLIT):
                packs[j][i] = fs[own ^ j]
            return 0

        trips = HB
    else:
        live = live_ref[0].astype(F32)

        def before(i, _):
            here = (step * LB + i) < HL
            x = jnp.where(here, pad_rows(x_ref[i].astype(F32)), 0.0)
            cot = jnp.where(here, pad_rows(cot_ref[i].astype(F32)), 0.0) * live
            enter(i, x, cot, fields[0][i].astype(F32))
            return 0

        def after(i, _):
            out, grad = leave(i)
            block_ref[i] = out[:WL]
            packs[0][i] = grad.astype(BF)
            return 0

        trips = LB

    lax.fori_loop(0, trips, before, 0)
    feed_chunks(n2, cots, c1_ref, win, wout, out_acc, gn_acc, gwi, gwo, gc1)
    lax.fori_loop(0, trips, after, 0)

    @pl.when(step == pl.num_programs(0) - 1)
    def _():
        stores = [
            pltpu.make_async_copy(gwi, gwi_out, sem.at[0]),
            pltpu.make_async_copy(gwo, gwo_out, sem.at[1]),
        ]
        for store in stores:
            store.start()
        for store in stores:
            store.wait()


def feed(high, own, live, samples, cotan, fields, vectors, bias_hidden, win, wout, earlier):
    tokens = (2 * HB if high else LB) * PW
    if high:
        steps = HALF // HB
        wide, packed, packed_shape = WIDE_BLOCK, PACKED_BLOCK, PACKED
    else:
        steps = LM // LB
        wide = pl.BlockSpec((LB, WL, D), lambda i: (i, 0, 0))
        packed = pl.BlockSpec((LB, PW, D), lambda i: (i, 0, 0))
        packed_shape = (LM, PW, D)
    count = len(fields)
    return pl.pallas_call(
        functools.partial(feed_kernel, high),
        grid=(steps,),
        in_specs=[SM, SM, wide, wide]
        + [packed] * count
        + [VM] * 4
        + ([ANY, ANY, VM, VM] if high else []),
        out_specs=[wide] + [packed] * count + [ANY, ANY, VM, VM],
        out_shape=[shape(samples.shape, BF)]
        + [shape(packed_shape, BF)] * count
        + [shape((FF, D), F32)] * 2
        + [shape((NC, FC), F32), shape((8, D), F32)],
        scratch_shapes=[pltpu.VMEM((FF, D), F32)] * 2
        + [
            pltpu.SemaphoreType.DMA((2,)),
            pltpu.VMEM((tokens, D), F32),
            pltpu.VMEM((tokens, D), BF),
            pltpu.VMEM((tokens, D), BF),
            pltpu.VMEM((tokens, D), F32),
            pltpu.VMEM((tokens, D), F32),
            pltpu.VMEM((SPLIT, PW, PAIR), BF),
        ],
        compiler_params=params(),
        name="feed_hi" if high else "feed_lo",
    )(own, live, samples, cotan, *fields, vectors, bias_hidden, win, wout, *earlier)


def norm_back_kernel(own_ref, x_ref, m0, m1, m2, m3, f0, f1, f2, f3, vec_ref, grad_ref, gvec, fs, ms):
    @pl.when(pl.program_id(0) == 0)
    def _():
        gvec[...] = jnp.zeros_like(gvec)

    own = own_ref[0]
    gain = vec_ref[0:1, :]

    def one(i, _):
        for j, (m, f) in enumerate(((m0, f0), (m1, f1), (m2, f2), (m3, f3))):
            ms[own ^ j] = m[i]
            fs[own ^ j] = f[i]
        for part, (direct, field) in enumerate(zip(unpack_pair(ms), unpack_pair(fs))):
            direct, field = direct[:OWN], field[:OWN]
            norm, scale = normed(x_ref[part, i].astype(F32))
            grad = field + direct
            gvec[0:1, :] += jnp.sum(grad * norm, axis=0, keepdims=True)
            gvec[1:2, :] += jnp.sum(grad, axis=0, keepdims=True)
            grad_ref[part, i] = direct + norm_back(grad, norm, scale, gain)
        return 0

    lax.fori_loop(0, HB, one, 0)


def norm_backward(own, samples, direct, fields, vectors):
    return pl.pallas_call(
        norm_back_kernel,
        grid=(HALF // HB,),
        in_specs=[SM, WIDE_BLOCK] + [PACKED_BLOCK] * (2 * SPLIT) + [VM],
        out_specs=[WIDE_BLOCK, VM],
        out_shape=[shape(samples.shape, F32), shape((2, D), F32)],
        scratch_shapes=[pltpu.VMEM((SPLIT, PW, PAIR), BF)] * 2,
        compiler_params=params(),
        name="norm_backward",
    )(own, samples, *direct, *fields, vectors)


def newton_poly(gram, square):
    size = gram.shape[0]
    eye = lax.broadcasted_iota(jnp.int32, (size, size), 0) == lax.broadcasted_iota(
        jnp.int32, (size, size), 1
    )
    return jnp.where(eye, newton_a, 0.0) + newton_b * gram + newton_c * square


def mul(left, right):
    return jnp.dot(left, right, precision=highest, preferred_element_type=F32)


def newton_kernel(g_in, g_out, x_in, x_out, y_in, y_out, gram, poly):
    for g_ref, x_ref, y_ref in ((g_in, x_in, y_in), (g_out, x_out, y_out)):
        size = g_ref.shape[0]
        eye = lax.broadcasted_iota(jnp.int32, (size, size), 0) == lax.broadcasted_iota(
            jnp.int32, (size, size), 1
        )
        trace = jnp.sum(jnp.where(eye, g_ref[...], 0.0), keepdims=True)
        scale = 1.0 / (jnp.sqrt(trace) + 1e-07)
        gram[...] = g_ref[...] * (scale * scale)
        y_ref[...] = x_ref[...] * scale
        for turn in range(NEWTON_STEPS):
            now = y_ref[...]
            if turn < NEWTON_STEPS - 1:
                poly[...] = newton_poly(gram[...], mul(gram[...], gram[...]))
                y_ref[...] = mul(now, poly[...])
                gram[...] = mul(poly[...], gram[...])
                gram[...] = mul(gram[...], poly[...])
            else:
                once = mul(now, gram[...])
                y_ref[...] = (
                    newton_a * now + newton_b * once + newton_c * mul(once, gram[...])
                )


def newton_pair(gram_in, gram_out, x_in, x_out):
    return pl.pallas_call(
        newton_kernel,
        in_specs=[VM] * 4,
        out_specs=[VM] * 2,
        out_shape=[shape(x_in.shape, F32), shape(x_out.shape, F32)],
        scratch_shapes=[pltpu.VMEM((D, D), F32)] * 2,
        compiler_params=params(),
        name="newton",
    )(gram_in, gram_out, x_in, x_out)


def newton_small_kernel(x_ref, y_ref):
    values = x_ref[...]
    size = 1.0 / (jnp.sqrt(jnp.sum(values * values, keepdims=True)) + 1e-07)
    values = values * size
    for _ in range(NEWTON_STEPS):
        gram = lax.dot_general(
            values, values, (((0,), (0,)), ((), ())), precision=highest, preferred_element_type=F32
        )
        once = mul(values, gram)
        values = newton_a * values + newton_b * once + newton_c * mul(once, gram)
    y_ref[...] = values


def newton_small(values):
    return pl.pallas_call(
        newton_small_kernel,
        in_specs=[VM],
        out_specs=VM,
        out_shape=shape(values.shape, F32),
        name="newton_small",
    )(values)


def spread(blocks):
    pairs = blocks.reshape(SPLIT, 2, BS, 1, BS)
    eye = jnp.eye(2, dtype=blocks.dtype).reshape(1, 2, 1, 2, 1)
    return (pairs * eye).reshape(SPLIT, GD, GD)


def spectral_matrices(spectral):
    low = spectral.astype(BF).reshape(2, 2, NB, BS, BS)
    re0, im0, re1, im1 = (spread(low[layer, part]) for layer in range(2) for part in range(2))
    wu = jnp.concatenate([re0, im0], axis=2)
    wv = jnp.concatenate([-im0, re0], axis=2)
    w1 = jnp.concatenate(
        [jnp.concatenate([re1, im1], axis=2), jnp.concatenate([-im1, re1], axis=2)], axis=1
    )
    return wu, wv, w1


def body(
    samples_hi, samples_lo, cotan_hi, cotan_lo, live_slots, spectral_w, vectors, weight_in,
    weight_out, moment_spec, moment_in, moment_out, adam_first, adam_second,
):
    axes = ("dp", "sp")
    sp = lax.axis_index("sp")
    own = sp.astype(jnp.int32).reshape(1)
    wide, tall, wide_lo, tall_lo = (jnp.asarray(t, BF) for t in tables())
    wide = lax.dynamic_index_in_dim(wide, sp, 0, keepdims=False)
    tabs = (wide, wide.T, tall, tall.T)
    tabs_lo = (wide_lo, wide_lo.T, tall_lo, tall_lo.T)

    vectors_full = lax.all_gather(vectors, axes, axis=1, tiled=True)
    spectral_full = lax.all_gather(spectral_w.astype(BF), axes, axis=0, tiled=True)
    win = lax.all_gather(weight_in.T.astype(BF), axes, axis=0, tiled=True)
    wout = lax.all_gather(weight_out.astype(BF), axes, axis=0, tiled=True)

    split_hi = samples_hi.reshape(2, HALF, OWN, D)
    split_cot = cotan_hi.reshape(2, HALF, OWN, D)
    one_lo = samples_lo.reshape(HL, WL, D)
    one_cot = cotan_lo.reshape(HL, WL, D)

    slabs = exchange(norm_packed(own, split_hi, vectors_full))
    weights_lo = spectral_matrices(spectral_full)
    weights = tuple(lax.dynamic_index_in_dim(w, sp, 0, keepdims=False) for w in weights_lo)
    e = vectors_full[9:13].reshape(2, 2, SPLIT, GD)
    bias_lo = jnp.transpose(e, (2, 0, 1, 3)).reshape(SPLIT, 2, PAIR)
    bias = lax.dynamic_index_in_dim(bias_lo, sp, 0, keepdims=False)
    bias_hidden = vectors_full[5:9].reshape(NC, FC)

    field_lo, four_lo = filter_forward_lo(one_lo, vectors_full, tabs_lo, weights_lo, bias_lo)
    fields, four = filter_forward(slabs, tabs, weights, bias)
    fields = exchange(fields)

    block_lo, gm_lo, gwi, gwo, gc1, gv = feed(
        False, own, live_slots, one_lo, one_cot, [field_lo], vectors_full, bias_hidden, win, wout, ()
    )
    block_hi, p0, p1, p2, p3, gwi, gwo, gc1, gv = feed(
        True, own, live_slots, split_hi, split_cot, fields, vectors_full, bias_hidden, win, wout,
        (gwi, gwo, gc1, gv),
    )
    packs = [p0, p1, p2, p3]
    red_in = lax.psum_scatter(gwi, axes, scatter_dimension=0, tiled=True)
    red_out = lax.psum_scatter(gwo, axes, scatter_dimension=0, tiled=True)

    grad_slabs = exchange(packs)
    grad_lo, gspec, ge_lo, gv_lo = filter_backward_lo(
        one_lo, gm_lo, four_lo, vectors_full, tabs_lo, weights_lo, bias_lo
    )
    back, gspec, ge = filter_backward(own, grad_slabs, four, tabs, weights, bias, gspec)
    back = exchange(back)
    grad_hi, gv_hi = norm_backward(own, split_hi, packs, back, vectors_full)

    ge_all = lax.dynamic_update_index_in_dim(
        ge_lo, lax.dynamic_index_in_dim(ge_lo, sp, 0, keepdims=False) + ge, sp, 0
    )
    ge_rows = jnp.transpose(ge_all.reshape(SPLIT, 2, 2, GD), (1, 2, 0, 3)).reshape(4, D)
    grad_vectors = jnp.concatenate([gv_lo + gv_hi, gv[:3], gc1.reshape(4, D), ge_rows], axis=0)

    red_spec = lax.psum_scatter(
        gspec.reshape(4 * NB * BS, BS), axes, scatter_dimension=0, tiled=True
    )
    red_vectors = lax.psum_scatter(grad_vectors, axes, scatter_dimension=1, tiled=True)

    new_moment_spec = momentum * moment_spec + red_spec
    new_moment_in = momentum * moment_in.T + red_in
    new_moment_out = momentum * moment_out + red_out
    dir_in = red_in + momentum * new_moment_in
    dir_out = red_out + momentum * new_moment_out
    dir_spec = red_spec + momentum * new_moment_spec

    gram_in, gram_out = lax.psum(
        (
            jnp.dot(dir_in.T, dir_in, precision=highest),
            jnp.dot(dir_out.T, dir_out, precision=highest),
        ),
        axes,
    )
    orth_in, orth_out = newton_pair(gram_in, gram_out, dir_in, dir_out)
    rows = moment_spec.shape[0]
    if rows == BS:
        orth_spec = newton_small(dir_spec)
    else:
        whole = lax.all_gather(dir_spec, "sp", axis=0, tiled=True)
        orth_spec = lax.dynamic_slice_in_dim(newton_small(whole), sp * rows, rows, 0)

    keep_share = 1.0 - muon_rate * decay
    new_weight_in = weight_in * keep_share - muon_rate * orth_in.T
    new_weight_out = weight_out * keep_share - muon_rate * math.sqrt(max(1.0, FF / D)) * orth_out
    new_spectral = spectral_w * keep_share - muon_rate * orth_spec
    new_adam_first = beta_one * adam_first + (1.0 - beta_one) * red_vectors
    new_adam_second = beta_two * adam_second + (1.0 - beta_two) * red_vectors * red_vectors
    first_hat = new_adam_first / (1.0 - beta_one**STEP)
    second_hat = new_adam_second / (1.0 - beta_two**STEP)
    new_vectors = vectors * (1.0 - adam_rate * decay) - adam_rate * first_hat / (
        jnp.sqrt(second_hat) + 1e-08
    )
    return (
        block_hi.reshape(samples_hi.shape),
        block_lo.reshape(samples_lo.shape),
        grad_hi.reshape(samples_hi.shape),
        grad_lo.reshape(samples_lo.shape),
        new_spectral,
        new_weight_in,
        new_weight_out,
        new_moment_spec,
        new_moment_in.T,
        new_moment_out,
        new_vectors,
        new_adam_first,
        new_adam_second,
    )


def solution(mesh):
    both = ("dp", "sp")
    hi = P("dp", None, "sp", None)
    lo = P(both, None, None, None)
    rows = P(both, None)
    cols = P(None, both)
    return jax.shard_map(
        body,
        mesh=mesh,
        in_specs=(hi, lo, hi, lo, P(both), rows, cols, cols, rows, rows, cols, rows, cols, cols),
        out_specs=(hi, lo, hi, lo, rows, cols, rows, rows, cols, rows, cols, cols, cols),
        check_vma=False,
    )
```

```python
import functools
import math

import jax
import jax.numpy as jnp
import numpy as np
from jax import lax
from jax.experimental import pallas as pl
from jax.experimental.pallas import tpu as pltpu
from jax.sharding import PartitionSpec as P

D = 768
FF = 3072
NB = 8
BS = 96
H = 90
W = 180
HL = 23
WL = 45
STEP = 10
NEWTON_STEPS = 5

F32 = jnp.float32
BF = jnp.bfloat16
highest = lax.Precision.HIGHEST
epsilon = 1e-06
shrink_level = 0.01
shrink_sharp = 10.0
momentum = 0.95
newton_a = 3.4445
newton_b = -4.775
newton_c = 2.0315
muon_rate = 0.5
adam_rate = 0.3
decay = 0.01
beta_one = 0.9
beta_two = 0.999

K0 = math.sqrt(2.0 / math.pi)
K1 = K0 * 0.044715

SPLIT = 4
GD = D // SPLIT
PAIR = 2 * GD
HALF = H // 2
OWN = W // SPLIT
PW = 48
PM = 96
KF = W // 2 + 1
KP = 96
KG = 7
GROUPS = KF // KG
ROWS = KG * PM
LH = 24
LK = HL // 2 + 1
LROWS = LK * PW
HB = 5
LB = 15
FC = 512
NC = FF // FC
VMEM_LIMIT = 60 * 2**20
UNROLL = 5
CHUNK = 48


def wave(length, rows, cols):
    phase = np.outer(rows, cols) % length
    angle = phase * (2.0 * math.pi / length)
    factor = 1.0 / math.sqrt(length)
    return np.cos(angle) * factor, np.sin(angle) * factor


def tables():
    wide = np.zeros((SPLIT, 2 * KP, SPLIT * PW))
    for s in range(SPLIT):
        for j in range(SPLIT):
            cols = (s ^ j) * OWN + np.arange(OWN)
            c, d = wave(W, np.arange(KF), cols)
            wide[s, :KF, j * PW : j * PW + OWN] = c
            wide[s, KP : KP + KF, j * PW : j * PW + OWN] = -d
    tall = np.zeros((2 * PM, 2 * PM))
    for part in range(2):
        c, d = wave(H, np.arange(H), part * HALF + np.arange(HALF))
        re, im = part * PW, PM + part * PW
        tall[:H, re : re + HALF] = c
        tall[:H, im : im + HALF] = d
        tall[PM : PM + H, re : re + HALF] = -d
        tall[PM : PM + H, im : im + HALF] = c
    wide_lo = np.zeros((2 * LK, LH))
    c, d = wave(HL, np.arange(LK), np.arange(HL))
    wide_lo[:LK, :HL] = c
    wide_lo[LK:, :HL] = -d
    tall_lo = np.zeros((2 * PW, 2 * PW))
    c, d = wave(WL, np.arange(WL), np.arange(WL))
    tall_lo[:WL, :WL] = c
    tall_lo[:WL, PW : PW + WL] = d
    tall_lo[PW : PW + WL, :WL] = -d
    tall_lo[PW : PW + WL, PW : PW + WL] = c
    return wide, tall, wide_lo, tall_lo


def loop(count, unroll, one):
    def some(i, carry):
        for n in range(unroll):
            one(i * unroll + n)
        return carry

    lax.fori_loop(0, count // unroll, some, 0)


def dot(left, right):
    return jnp.dot(left, right, preferred_element_type=F32)


def dot_nt(left, right):
    return lax.dot_general(left, right, (((1,), (1,)), ((), ())), preferred_element_type=F32)


def dot_tn(left, right):
    return lax.dot_general(left, right, (((0,), (0,)), ((), ())), preferred_element_type=F32)


def normed(values):
    center = values - jnp.mean(values, axis=-1, keepdims=True)
    scale = lax.rsqrt(jnp.mean(center * center, axis=-1, keepdims=True) + epsilon)
    return center * scale, scale


def norm_back(grad, norm, scale, gain):
    pushed = grad * gain
    return scale * (
        pushed
        - jnp.mean(pushed, axis=-1, keepdims=True)
        - norm * jnp.mean(pushed * norm, axis=-1, keepdims=True)
    )


def pad_rows(values, rows=PW):
    return jnp.concatenate(
        [values, jnp.zeros((rows - values.shape[0], values.shape[1]), values.dtype)], axis=0
    )


def lanes(*pieces):
    return jnp.concatenate(pieces, axis=1)


def unpack_pair(fs):
    pieces = [fs[g].astype(F32) for g in range(SPLIT)]
    return (
        lanes(*[p[:, :GD] for p in pieces]),
        lanes(*[p[:, GD:] for p in pieces]),
    )


def pack_pair(row_a, row_b, fs):
    for g in range(SPLIT):
        cut = slice(g * GD, (g + 1) * GD)
        fs[g] = lanes(row_a[:, cut], row_b[:, cut]).astype(BF)


SP = ("sy", "sc")
VM = pl.BlockSpec(memory_space=pltpu.VMEM)
SM = pl.BlockSpec(memory_space=pltpu.SMEM)
ANY = pl.BlockSpec(memory_space=pl.ANY)


def params():
    return pltpu.CompilerParams(vmem_limit_bytes=VMEM_LIMIT)


def cost(us):
    return pl.CostEstimate(flops=us * 10**9, bytes_accessed=us * 10**6, transcendentals=0)


def shape(dims, kind):
    return jax.ShapeDtypeStruct(dims, kind)


PACKED = (HALF, PW, PAIR)
PACKED_BLOCK = pl.BlockSpec((HB, PW, PAIR), lambda i: (i, 0, 0))
WIDE_BLOCK = pl.BlockSpec((2, HB, OWN, D), lambda i: (0, i, 0, 0))


def pack_kernel(own_ref, x_ref, vec_ref, o0, o1, o2, o3, fs):
    own = own_ref[0]
    gain, shift = vec_ref[0:1, :], vec_ref[1:2, :]

    for i in range(HB):
        rows = []
        for part in range(2):
            norm, _unused = normed(x_ref[part, i].astype(F32))
            rows.append(pad_rows(norm * gain + shift))
        pack_pair(rows[0], rows[1], fs.at[i])
    for i in range(HB):
        for j, out in enumerate((o0, o1, o2, o3)):
            out[i] = fs[i, own ^ j]


def norm_packed(own, samples, vectors):
    return pl.pallas_call(
        pack_kernel,
        grid=(HALF // HB,),
        in_specs=[SM, WIDE_BLOCK, VM],
        out_specs=[PACKED_BLOCK] * SPLIT,
        out_shape=[shape(PACKED, BF)] * SPLIT,
        scratch_shapes=[pltpu.VMEM((HB, SPLIT, PW, PAIR), BF)],
        compiler_params=params(),
        name="norm_pack",
        cost_estimate=cost(16),
    )(own, samples, vectors)


def exchange(slabs):
    moved = [slabs[0]]
    for j in range(1, SPLIT):
        moved.append(lax.ppermute(slabs[j], SP, [(i, i ^ j) for i in range(SPLIT)]))
    return moved


def to_freq_wide(slabs, table, space):
    def one(i):
        rows = jnp.concatenate([slab[i] for slab in slabs], axis=0)
        area = dot(table[...], rows)
        for c in range(3):
            space[c, pl.ds(i, 2 * KP, stride=PW), :] = area[:, c * 128 : (c + 1) * 128]

    loop(HALF, UNROLL, one)


def to_freq_tall(k, table, space):
    re = lanes(*[space[c, pl.ds(pl.multiple_of(k * PW, PW), PW), :] for c in range(3)])
    im = lanes(*[space[c, pl.ds(pl.multiple_of((KP + k) * PW, PW), PW), :] for c in range(3)])
    rows = jnp.concatenate([re[:, :GD], re[:, GD:], im[:, :GD], im[:, GD:]], axis=0)
    return dot(table[...], rows.astype(BF))


def to_space_tall(k, table, four, space):
    back = dot(table[...], four)
    for part in range(2):
        base = part * PM
        packed = lanes(back[base : base + PW], back[base + PW : base + PM])
        at = pl.ds(pl.multiple_of((part * KP + k) * PW, PW), PW)
        for c in range(3):
            space[c, at, :] = packed[:, c * 128 : (c + 1) * 128]


def to_space_wide(table, space, outs):
    def one(i):
        rows = lanes(*[space[c, pl.ds(i, 2 * KP, stride=PW), :] for c in range(3)])
        field = dot(table[...], rows.astype(BF)).astype(BF)
        for j, out in enumerate(outs):
            out[i] = field[j * PW : (j + 1) * PW]

    loop(HALF, UNROLL, one)


def clear(ref):
    def one(i, _):
        for c in range(ref.shape[0]):
            ref[c, pl.ds(pl.multiple_of(i * 96, 96), 96), :] = jnp.zeros((96, 128), F32)
        return 0

    lax.fori_loop(0, ref.shape[1] // 96, one, 0)


def keep_minus(row, width, first, last):
    at = row + lax.broadcasted_iota(jnp.int32, (width, 1), 0)
    return jnp.where((at >= first) & (at < last), 1.0, 0.0).astype(F32)


def mlp_forward(fre, fim, wu, wv, w1, bias, us, vs, actp, actm, put, base, first, last, chunk):
    rows = us.shape[0]
    us[...] = dot(fre, wu)
    vs[...] = dot(fim, wv)
    b0, b1 = bias[0:1, :], bias[1:2, :]

    def act(i, _):
        at = pl.ds(pl.multiple_of(i * chunk, chunk), chunk)
        u = us[at, :] + b0
        v = vs[at, :]
        for ref, value in ((actp, u + v), (actm, u - v)):
            t = jnp.tanh(value * (K0 + K1 * (value * value)))
            ref[at, :] = (value * (0.5 + 0.5 * t)).astype(BF)
        return 0

    lax.fori_loop(0, rows // chunk, act, 0)
    us[...] = dot(actp[...], w1)
    vs[...] = dot(actm[...], w1)

    def shrunk(i, _):
        at = pl.ds(pl.multiple_of(i * chunk, chunk), chunk)
        p = us[at, :] + b1
        m = vs[at, :] + b1
        p = p - shrink_level * jnp.tanh(shrink_sharp * p)
        m = (m - shrink_level * jnp.tanh(shrink_sharp * m)) * keep_minus(
            base + i * chunk, chunk, first, last
        )
        put(at, (p[:, :GD] + m[:, :GD]).astype(BF), (p[:, GD:] - m[:, GD:]).astype(BF))
        return 0

    lax.fori_loop(0, rows // chunk, shrunk, 0)


def mlp_backward(
    fre, fim, gs, wu, wv, w1, bias, us, vs, actp, actm, dp, dm, gsp, gsm, sums, put,
    gwu, gwv, gw1, ge, base, first, last, chunk,
):
    rows = us.shape[0]
    us[...] = dot(fre, wu)
    vs[...] = dot(fim, wv)
    b0, b1 = bias[0:1, :], bias[1:2, :]
    sign = jnp.where(lax.broadcasted_iota(jnp.int32, (1, PAIR), 1) < GD, 1.0, -1.0).astype(F32)

    def act(i, _):
        at = pl.ds(pl.multiple_of(i * chunk, chunk), chunk)
        u = us[at, :] + b0
        v = vs[at, :]
        for ref, slope, value in ((actp, dp, u + v), (actm, dm, u - v)):
            square = value * value
            hp = 0.5 + 0.5 * jnp.tanh(value * (K0 + K1 * square))
            on = value * hp
            ref[at, :] = on.astype(BF)
            slope[at, :] = hp + on * (1.0 - hp) * (2.0 * K0 + 6.0 * K1 * square)
        return 0

    lax.fori_loop(0, rows // chunk, act, 0)
    us[...] = dot(actp[...], w1)
    vs[...] = dot(actm[...], w1)

    def second(i, total):
        at = pl.ds(pl.multiple_of(i * chunk, chunk), chunk)
        grad = gs[at, :]
        tp = jnp.tanh(shrink_sharp * (us[at, :] + b1))
        tm = jnp.tanh(shrink_sharp * (vs[at, :] + b1))
        flat = 1.0 - shrink_level * shrink_sharp
        bend = shrink_level * shrink_sharp
        p = grad * (flat + bend * (tp * tp))
        m = (grad * (sign * keep_minus(base + i * chunk, chunk, first, last))) * (
            flat + bend * (tm * tm)
        )
        gsp[at, :] = p.astype(BF)
        gsm[at, :] = m.astype(BF)
        return total + jnp.sum(p + m, axis=0, keepdims=True)

    ge[1:2, :] += lax.fori_loop(0, rows // chunk, second, jnp.zeros((1, PAIR), F32))
    us[...] = dot_nt(gsp[...], w1)
    vs[...] = dot_nt(gsm[...], w1)
    gw1[...] += dot_tn(actp[...], gsp[...]) + dot_tn(actm[...], gsm[...])

    def first_grad(i, total):
        at = pl.ds(pl.multiple_of(i * chunk, chunk), chunk)
        p = us[at, :] * dp[at, :]
        m = vs[at, :] * dm[at, :]
        both = p + m
        gsp[at, :] = both.astype(BF)
        gsm[at, :] = (p - m).astype(BF)
        return total + jnp.sum(both, axis=0, keepdims=True)

    ge[0:1, :] += lax.fori_loop(0, rows // chunk, first_grad, jnp.zeros((1, PAIR), F32))
    gwu[...] += dot_tn(fre, gsp[...])
    gwv[...] += dot_tn(fim, gsm[...])
    put(dot_nt(gsp[...], wu).astype(BF), dot_nt(gsm[...], wv).astype(BF))


def block_grads(gwu, gwv, gw1):
    cells = {}
    for b in range(2):
        r = slice(b * BS, (b + 1) * BS)
        i = slice(GD + b * BS, GD + (b + 1) * BS)
        cells[0, 0, b] = gwu[r, r] + gwv[r, i]
        cells[0, 1, b] = gwu[r, i] - gwv[r, r]
        cells[1, 0, b] = gw1[r, r] + gw1[i, i]
        cells[1, 1, b] = gw1[r, i] - gw1[i, r]
    return cells


def filter_kernel(
    own_ref, x0, x1, x2, x3, tw, twt, th, tht, wu, wv, w1, bias,
    y0, y1, y2, y3, four, space, us, vs, actp, actm, zr, zi,
):
    own = own_ref[0]
    clear(space)
    to_freq_wide((x0, x1, x2, x3), tw.at[own], space)

    def group(g, _):
        for n in range(KG):
            rows = to_freq_tall(g * KG + n, th, space).astype(BF)
            four[g, 0, n * PM : (n + 1) * PM, :] = rows[:PM]
            four[g, 1, n * PM : (n + 1) * PM, :] = rows[PM:]

        def put(at, re, im):
            zr[at, :] = re
            zi[at, :] = im

        mlp_forward(
            four[g, 0], four[g, 1], wu[own], wv[own], w1[own], bias.at[own], us, vs, actp, actm, put,
            g * ROWS, PM, (KF - 1) * PM, CHUNK,
        )
        for n in range(KG):
            at = slice(n * PM, (n + 1) * PM)
            to_space_tall(
                g * KG + n, tht, jnp.concatenate([zr[at, :], zi[at, :]], axis=0), space
            )
        return 0

    lax.fori_loop(0, GROUPS, group, 0)
    to_space_wide(twt.at[own], space, (y0, y1, y2, y3))


def filter_scratch(rows, wide):
    big = pltpu.VMEM((rows, PAIR), F32)
    low = pltpu.VMEM((rows, PAIR), BF)
    part = pltpu.VMEM((rows, GD), BF)
    return big, low, part


def filter_forward(own, slabs, tabs, weights, bias):
    big, low, part = filter_scratch(ROWS, None)
    outs = pl.pallas_call(
        filter_kernel,
        in_specs=[SM] + [VM] * 12,
        out_specs=[VM] * 5,
        out_shape=[shape(PACKED, BF)] * SPLIT + [shape((GROUPS, 2, ROWS, GD), BF)],
        scratch_shapes=[pltpu.VMEM((3, 2 * KP * PW, 128), F32), big, big, low, low, part, part],
        compiler_params=params(),
        name="filter_forward",
        cost_estimate=cost(95),
    )(own, *slabs, *tabs, *weights, bias)
    return outs[:SPLIT], outs[SPLIT]


def filter_back_kernel(
    own_ref, x0, x1, x2, x3, four, tw, twt, th, tht, wu, wv, w1, bias,
    y0, y1, y2, y3, grads, ge,
    space, us, vs, actp, actm, zr, zi, gs, dp, dm, gsp, gsm, gwu, gwv, gw1,
):
    own = own_ref[0]
    clear(space)
    gwu[...] = jnp.zeros_like(gwu)
    gwv[...] = jnp.zeros_like(gwv)
    gw1[...] = jnp.zeros_like(gw1)
    ge[...] = jnp.zeros_like(ge)
    to_freq_wide((x0, x1, x2, x3), tw.at[own], space)

    def group(g, _):
        for n in range(KG):
            rows = to_freq_tall(g * KG + n, th, space)
            gs[n * PM : (n + 1) * PM, :] = lanes(rows[:PM], rows[PM:])

        def put(re, im):
            zr[...] = re
            zi[...] = im

        mlp_backward(
            four[g, 0], four[g, 1], gs, wu[own], wv[own], w1[own], bias.at[own], us, vs, actp, actm, dp, dm,
            gsp, gsm, None, put, gwu, gwv, gw1, ge, g * ROWS, PM, (KF - 1) * PM, CHUNK,
        )
        for n in range(KG):
            at = slice(n * PM, (n + 1) * PM)
            to_space_tall(
                g * KG + n, tht, jnp.concatenate([zr[at, :], zi[at, :]], axis=0), space
            )
        return 0

    lax.fori_loop(0, GROUPS, group, 0)
    grads[...] = jnp.zeros_like(grads)
    for (layer, part, b), value in block_grads(gwu, gwv, gw1).items():
        grads[(2 * layer + part) * NB + 2 * own + b] = value
    to_space_wide(twt.at[own], space, (y0, y1, y2, y3))


def filter_backward(own, slabs, four, tabs, weights, bias):
    big, low, part = filter_scratch(ROWS, None)
    outs = pl.pallas_call(
        filter_back_kernel,
        in_specs=[SM] + [VM] * 13,
        out_specs=[VM] * 6,
        out_shape=[shape(PACKED, BF)] * SPLIT
        + [shape((4 * NB, BS, BS), F32), shape((2, PAIR), F32)],
        scratch_shapes=[pltpu.VMEM((3, 2 * KP * PW, 128), F32), big, big, low, low, part, part]
        + [big, big, big, low, low]
        + [pltpu.VMEM((GD, PAIR), F32)] * 2
        + [pltpu.VMEM((PAIR, PAIR), F32)],
        compiler_params=params(),
        name="filter_backward",
        cost_estimate=cost(125),
    )(own, *slabs, four, *tabs, *weights, bias)
    return outs[:SPLIT], outs[SPLIT], outs[SPLIT + 1]


def lo_freq_wide(i, rows, table, space):
    area = dot(table[...], rows)
    for c in range(6):
        space[c, pl.ds(i, 2 * LK, stride=PW), :] = area[:, c * 128 : (c + 1) * 128]


def lo_freq_tall(k, table, space):
    parts = []
    for base in (0, LK):
        at = pl.ds(pl.multiple_of((base + k) * PW, PW), PW)
        parts.append(lanes(*[space[c, at, :] for c in range(6)]))
    rows = dot(table[...], jnp.concatenate(parts, axis=0).astype(BF))
    return rows[:PW], rows[PW:]


def lo_space_tall(k, table, re, im, space):
    back = dot(table[...], jnp.concatenate([re, im], axis=0).astype(BF))
    for part, base in enumerate((0, LK)):
        at = pl.ds(pl.multiple_of((base + k) * PW, PW), PW)
        for c in range(6):
            space[c, at, :] = back[part * PW : (part + 1) * PW, c * 128 : (c + 1) * 128]


def lo_space_wide(i, table, space):
    rows = lanes(*[space[c, pl.ds(i, 2 * LK, stride=PW), :] for c in range(6)])
    return dot(table[...], rows.astype(BF))


def filter_lo_kernel(
    x_ref, vec_ref, tw, twt, th, tht, wu, wv, w1, bias, y_ref, four,
    space, us, vs, actp, actm, zr, zi,
):
    clear(space)
    gain, shift = vec_ref[0:1, :], vec_ref[1:2, :]

    def wide(i):
        norm, _unused = normed(x_ref[i].astype(F32))
        lo_freq_wide(i, pad_rows(norm * gain + shift, LH).astype(BF), tw, space)

    loop(WL, UNROLL, wide)

    def tall(k):
        re, im = lo_freq_tall(k, th, space)
        at = pl.ds(pl.multiple_of(k * PW, PW), PW)
        for g in range(SPLIT):
            cut = slice(g * GD, (g + 1) * GD)
            four[g, 0, at, :] = re[:, cut].astype(BF)
            four[g, 1, at, :] = im[:, cut].astype(BF)

    loop(LK, 3, tall)

    def group(g, _):
        def put(at, re, im):
            zr[g, at, :] = re
            zi[g, at, :] = im

        mlp_forward(
            four[g, 0], four[g, 1], wu[g], wv[g], w1[g], bias.at[g], us, vs, actp, actm, put,
            0, PW, LROWS, CHUNK,
        )
        return 0

    lax.fori_loop(0, SPLIT, group, 0)

    def back(k):
        at = pl.ds(pl.multiple_of(k * PW, PW), PW)
        re = lanes(*[zr[g, at, :].astype(F32) for g in range(SPLIT)])
        im = lanes(*[zi[g, at, :].astype(F32) for g in range(SPLIT)])
        lo_space_tall(k, tht, re, im, space)

    loop(LK, 3, back)

    def last(i):
        y_ref[i] = lo_space_wide(i, twt, space).astype(BF)

    loop(WL, UNROLL, last)


def lo_scratch():
    big, low, _ = filter_scratch(LROWS, None)
    part = pltpu.VMEM((SPLIT, LROWS, GD), BF)
    return [pltpu.VMEM((6, 2 * LK * PW, 128), F32), big, big, low, low, part, part]


def filter_forward_lo(samples, vectors, tabs, weights, bias):
    return pl.pallas_call(
        filter_lo_kernel,
        in_specs=[VM] * 10,
        out_specs=[VM] * 2,
        out_shape=[shape((WL, LH, D), BF), shape((SPLIT, 2, LROWS, GD), BF)],
        scratch_shapes=lo_scratch(),
        compiler_params=params(),
        name="filter_forward_lo",
        cost_estimate=cost(35),
    )(samples, vectors, *tabs, *weights, bias)


def filter_back_lo_kernel(
    x_ref, gm_ref, four, vec_ref, tw, twt, th, tht, wu, wv, w1, bias, grads_in,
    grad_ref, grads, ge, gvec,
    space, us, vs, actp, actm, zr, zi, gs, dp, dm, gsp, gsm, gwu, gwv, gw1,
):
    clear(space)
    ge[...] = jnp.zeros_like(ge)
    gvec[...] = jnp.zeros_like(gvec)

    def wide(i):
        lo_freq_wide(i, gm_ref[i], tw, space)

    loop(WL, UNROLL, wide)

    def tall(k):
        re, im = lo_freq_tall(k, th, space)
        at = pl.ds(pl.multiple_of(k * PW, PW), PW)
        for g in range(SPLIT):
            cut = slice(g * GD, (g + 1) * GD)
            gs[g, at, :] = lanes(re[:, cut], im[:, cut])

    loop(LK, 3, tall)

    def group(g, _):
        gwu[...] = jnp.zeros_like(gwu)
        gwv[...] = jnp.zeros_like(gwv)
        gw1[...] = jnp.zeros_like(gw1)

        def put(re, im):
            zr[g] = re
            zi[g] = im

        mlp_backward(
            four[g, 0], four[g, 1], gs.at[g], wu[g], wv[g], w1[g], bias.at[g], us, vs, actp, actm,
            dp, dm, gsp, gsm, None, put, gwu, gwv, gw1, ge.at[g], 0, PW, LROWS, CHUNK,
        )
        for (layer, part, b), value in block_grads(gwu, gwv, gw1).items():
            at = (2 * layer + part) * NB + 2 * g + b
            grads[at] = grads_in[at] + value
        return 0

    lax.fori_loop(0, SPLIT, group, 0)

    def back(k):
        at = pl.ds(pl.multiple_of(k * PW, PW), PW)
        re = lanes(*[zr[g, at, :].astype(F32) for g in range(SPLIT)])
        im = lanes(*[zi[g, at, :].astype(F32) for g in range(SPLIT)])
        lo_space_tall(k, tht, re, im, space)

    loop(LK, 3, back)
    gain = vec_ref[0:1, :]

    def last(t, _):
        sums = []
        for n in range(UNROLL):
            i = t * UNROLL + n
            field = lo_space_wide(i, twt, space)[:HL]
            direct = gm_ref[i].astype(F32)[:HL]
            norm, scale = normed(x_ref[i].astype(F32))
            grad = field + direct
            sums.append((jnp.sum(grad * norm, axis=0, keepdims=True), jnp.sum(grad, axis=0, keepdims=True)))
            value = direct + norm_back(grad, norm, scale, gain)
            for c in range(6):
                at = pl.ds(6 * i + c, HL, stride=6 * WL)
                grad_ref[at, 0, :] = value[:, c * 128 : (c + 1) * 128]
        gvec[0:1, :] += sum(a for a, b in sums)
        gvec[1:2, :] += sum(b for a, b in sums)
        return 0

    lax.fori_loop(0, WL // UNROLL, last, 0)


def filter_backward_lo(samples, grad_mixed, four, vectors, tabs, weights, bias, grads_in):
    big, low, _ = filter_scratch(LROWS, None)
    return pl.pallas_call(
        filter_back_lo_kernel,
        in_specs=[VM] * 13,
        out_specs=[VM] * 4,
        out_shape=[
            shape((HL * WL * 6, 1, 128), F32),
            shape((4 * NB, BS, BS), F32),
            shape((SPLIT, 2, PAIR), F32),
            shape((2, D), F32),
        ],
        scratch_shapes=lo_scratch()
        + [pltpu.VMEM((SPLIT, LROWS, PAIR), F32), big, big, low, low]
        + [pltpu.VMEM((GD, PAIR), F32)] * 2
        + [pltpu.VMEM((PAIR, PAIR), F32)],
        compiler_params=params(),
        name="filter_backward_lo",
        cost_estimate=cost(45),
    )(samples, grad_mixed, four, vectors, *tabs, *weights, bias, grads_in)


def feed_chunks(n2, cots, c1_ref, win, wout, out_acc, gn_acc, gw, gc1):
    out_acc[...] = jnp.zeros_like(out_acc)
    gn_acc[...] = jnp.zeros_like(gn_acc)

    def chunk(c, _):
        rows = pl.ds(c * FC, FC)
        low, cot = n2[...].reshape(-1, D), cots[...].reshape(-1, D)
        wi, wo = win[rows, :], wout[rows, :]
        hidden = dot_nt(low, wi) + c1_ref[pl.ds(c, 1), :]
        grad = dot_nt(cot, wo)
        square = hidden * hidden
        hp = 0.5 + 0.5 * jnp.tanh(hidden * (K0 + K1 * square))
        act = hidden * hp
        grad = grad * (hp + act * (1.0 - hp) * (2.0 * K0 + 6.0 * K1 * square))
        gc1[pl.ds(c, 1), :] += jnp.sum(grad, axis=0, keepdims=True)
        act = act.astype(BF)
        grad = grad.astype(BF)
        out_acc[...] += dot(act, wo)
        gn_acc[...] += dot(grad, wi)
        gw[1, rows, :] += dot_tn(act, cot)
        gw[0, rows, :] += dot_tn(grad, low)
        return 0

    for c in range(NC):
        chunk(c, 0)


def feed_kernel(high, own_ref, live_ref, *refs):
    count = SPLIT if high else 1
    x_ref, cot_ref = refs[:2]
    fields = refs[2 : 2 + count]
    rest = refs[2 + count :]
    vec_ref, c1_ref, win, wout = rest[:4]
    rest = rest[4:]
    if high:
        gw_in, gc1_in, gv_in = rest[:3]
        rest = rest[3:]
    block_ref = rest[0]
    packs = rest[1 : 1 + count]
    rest = rest[1 + count :]
    keep_out = rest[0]
    if high:
        give_out = rest[1]
        rest = rest[1:]
    gc1, gv, gw, sem, mixed, n2, cots, out_acc, gn_acc, fs = rest[1:]
    step = pl.program_id(0)

    @pl.when(step == 0)
    def _():
        if high:
            load = pltpu.make_async_copy(gw_in, gw, sem)
            load.start()
            load.wait()
            gc1[...] = gc1_in[...]
            gv[...] = gv_in[...]
        else:
            gw[...] = jnp.zeros_like(gw)
            gc1[...] = jnp.zeros_like(gc1)
            gv[...] = jnp.zeros_like(gv)

    own = own_ref[0]
    tall = PW if high else LH
    gain_one, shift_one = vec_ref[0:1, :], vec_ref[1:2, :]
    gain_two, shift_two = vec_ref[2:3, :], vec_ref[3:4, :]
    bias_out = vec_ref[4:5, :]

    def enter(plane, x, cot, field):
        at = pl.ds(plane * tall, tall)
        norm, _unused = normed(x)
        total = field + (norm * gain_one + shift_one) + x
        mixed[at, :] = total
        norm, _unused = normed(total)
        n2[plane] = (norm * gain_two + shift_two).astype(BF)
        cots[plane] = cot.astype(BF)

    def leave(plane):
        at = pl.ds(plane * tall, tall)
        total = mixed[at, :]
        out = total + (out_acc[at, :] + bias_out)
        norm, scale = normed(total)
        grad = gn_acc[at, :]
        cot = cots[plane].astype(F32)
        sums.append(
            tuple(jnp.sum(v, axis=0, keepdims=True) for v in (grad * norm, grad, cot))
        )
        return out.astype(BF), cot + norm_back(grad, norm, scale, gain_two)

    sums = []

    def add_sums():
        for row in range(3):
            gv[row : row + 1, :] += sum(entry[row] for entry in sums)
        sums.clear()

    if high:

        def before():
            for i in range(HB):
                for j in range(SPLIT):
                    fs[i, own ^ j] = fields[j][i]
            for i in range(HB):
                for part, field in enumerate(unpack_pair(fs.at[i])):
                    x = pad_rows(x_ref[part, i].astype(F32))
                    cot = pad_rows(cot_ref[part, i].astype(F32))
                    enter(part * HB + i, x, cot, field)

        def after():
            for i in range(HB):
                grads = []
                for part in range(2):
                    out, grad = leave(part * HB + i)
                    block_ref[part, i] = out[:OWN]
                    grads.append(grad)
                pack_pair(grads[0], grads[1], fs.at[i])
            add_sums()
            for i in range(HB):
                for j in range(SPLIT):
                    packs[j][i] = fs[i, own ^ j]

    else:
        live = live_ref[0].astype(F32)

        def before():
            for i in range(LB):
                x = pad_rows(x_ref[i].astype(F32), LH)
                cot = pad_rows(cot_ref[i].astype(F32), LH) * live
                enter(i, x, cot, fields[0][i].astype(F32))

        def after():
            for i in range(LB):
                out, grad = leave(i)
                block_ref[i] = out[:HL]
                packs[0][i] = grad.astype(BF)
            add_sums()

    before()
    feed_chunks(n2, cots, c1_ref, win, wout, out_acc, gn_acc, gw, gc1)
    after()

    @pl.when(step == pl.num_programs(0) - 1)
    def _():
        if not high:
            store = pltpu.make_async_copy(gw, keep_out, sem)
            store.start()
            store.wait()
        else:
            mine = lax.rem(own, 2)
            store = pltpu.make_async_copy(gw.at[mine], keep_out, sem)
            store.start()

            def low(c, _):
                rows = pl.ds(pl.multiple_of(c * FC, FC), FC)
                give_out[rows, :] = gw[1 - mine, rows, :].astype(BF)
                return 0

            lax.fori_loop(0, NC, low, 0)
            store.wait()


def feed(high, own, live, samples, cotan, fields, vectors, bias_hidden, win, wout, earlier):
    planes, tall = (2 * HB, PW) if high else (LB, LH)
    tokens = planes * tall
    if high:
        steps = HALF // HB
        wide, packed, packed_shape = WIDE_BLOCK, PACKED_BLOCK, PACKED
    else:
        steps = WL // LB
        wide = pl.BlockSpec((LB, HL, D), lambda i: (i, 0, 0))
        packed = pl.BlockSpec((LB, LH, D), lambda i: (i, 0, 0))
        packed_shape = (WL, LH, D)
    count = len(fields)
    return pl.pallas_call(
        functools.partial(feed_kernel, high),
        grid=(steps,),
        in_specs=[SM, SM, wide, wide]
        + [packed] * count
        + [VM] * 4
        + ([ANY, VM, VM] if high else []),
        out_specs=[wide] + [packed] * count + ([ANY, VM] if high else [ANY]) + [VM, VM],
        out_shape=[shape(samples.shape, BF)]
        + [shape(packed_shape, BF)] * count
        + ([shape((FF, D), F32), shape((FF, D), BF)] if high else [shape((2, FF, D), F32)])
        + [shape((NC, FC), F32), shape((8, D), F32)],
        scratch_shapes=[
            pltpu.VMEM((2, FF, D), F32),
            pltpu.SemaphoreType.DMA,
            pltpu.VMEM((tokens, D), F32),
            pltpu.VMEM((planes, tall, D), BF),
            pltpu.VMEM((planes, tall, D), BF),
            pltpu.VMEM((tokens, D), F32),
            pltpu.VMEM((tokens, D), F32),
            pltpu.VMEM((HB, SPLIT, PW, PAIR), BF),
        ],
        compiler_params=params(),
        name="feed_hi" if high else "feed_lo",
        cost_estimate=cost(210 if high else 70),
    )(own, live, samples, cotan, *fields, vectors, bias_hidden, win, wout, *earlier)


def norm_back_kernel(own_ref, x_ref, m0, m1, m2, m3, f0, f1, f2, f3, vec_ref, grad_ref, gvec, fs, ms):
    @pl.when(pl.program_id(0) == 0)
    def _():
        gvec[...] = jnp.zeros_like(gvec)

    own = own_ref[0]
    gain = vec_ref[0:1, :]

    for i in range(HB):
        for j, (m, f) in enumerate(((m0, f0), (m1, f1), (m2, f2), (m3, f3))):
            ms[i, own ^ j] = m[i]
            fs[i, own ^ j] = f[i]
    sums = []
    for i in range(HB):
        for part, (direct, field) in enumerate(zip(unpack_pair(ms.at[i]), unpack_pair(fs.at[i]))):
            direct, field = direct[:OWN], field[:OWN]
            norm, scale = normed(x_ref[part, i].astype(F32))
            grad = field + direct
            sums.append((jnp.sum(grad * norm, axis=0, keepdims=True), jnp.sum(grad, axis=0, keepdims=True)))
            value = direct + norm_back(grad, norm, scale, gain)
            for c in range(6):
                at = pl.ds(i * (6 * OWN) + c, OWN, stride=6)
                grad_ref[part, at, 0, :] = value[:, c * 128 : (c + 1) * 128]
    gvec[0:1, :] += sum(a for a, b in sums)
    gvec[1:2, :] += sum(b for a, b in sums)


def norm_backward(own, samples, direct, fields, vectors):
    return pl.pallas_call(
        norm_back_kernel,
        grid=(HALF // HB,),
        in_specs=[SM, WIDE_BLOCK] + [PACKED_BLOCK] * (2 * SPLIT) + [VM],
        out_specs=[pl.BlockSpec((2, HB * OWN * 6, 1, 128), lambda i: (0, i, 0, 0)), VM],
        out_shape=[shape((2, HALF * OWN * 6, 1, 128), F32), shape((2, D), F32)],
        scratch_shapes=[pltpu.VMEM((HB, SPLIT, PW, PAIR), BF)] * 2,
        compiler_params=params(),
        name="norm_backward",
        cost_estimate=cost(22),
    )(own, samples, *direct, *fields, vectors)


def eye_of(size):
    return lax.broadcasted_iota(jnp.int32, (size, size), 0) == lax.broadcasted_iota(
        jnp.int32, (size, size), 1
    )


def mul(left, right):
    return jnp.dot(left, right, precision=highest, preferred_element_type=F32)


def split_three(values):
    top = values.astype(BF)
    rest = values - top.astype(F32)
    middle = rest.astype(BF)
    return top, middle, (rest - middle.astype(F32)).astype(BF)


TILE = 256


def mul_parts(left, right_ref, parts, full, out, finish=None):
    size = right_ref.shape[0]
    rows = left.shape[0]
    tile = TILE if rows % TILE == 0 else rows

    def cut(i, _):
        at = pl.ds(pl.multiple_of(i * TILE, TILE), TILE)
        for n, part in enumerate(split_three(right_ref[at, :])):
            parts[n, at, :] = part
        return 0

    lax.fori_loop(0, size // TILE, cut, 0)

    def one(i, _):
        at = pl.ds(pl.multiple_of(i * tile, tile), tile)
        top, middle, low = split_three(left[at, :])
        total = dot(middle, parts[0]) + dot(top, parts[1])
        if full:
            total = total + (dot(middle, parts[1]) + dot(top, parts[2]) + dot(low, parts[0]))
        total = total + dot(top, parts[0])
        out[at, :] = total if finish is None else finish(at, total)
        return 0

    lax.fori_loop(0, rows // tile, one, 0)


def newton_kernel(g_ref, x_ref, y_ref, gram, poly, hold, parts, once, twice):
    size = g_ref.shape[0]
    trace = jnp.sum(jnp.where(eye_of(size), g_ref[...], 0.0), keepdims=True)
    scale = 1.0 / (jnp.sqrt(trace) + 1e-07)
    gram[...] = g_ref[...] * (scale * scale)
    y_ref[...] = x_ref[...] * scale

    def turn(full):
        def polynomial(at, square):
            rows = at.start + lax.broadcasted_iota(jnp.int32, (TILE, size), 0)
            diagonal = rows == lax.broadcasted_iota(jnp.int32, (TILE, size), 1)
            return jnp.where(diagonal, newton_a, 0.0) + newton_b * gram[at, :] + newton_c * square

        mul_parts(gram, gram, parts, full, poly, polynomial)
        mul_parts(gram, poly, parts, full, hold)
        mul_parts(y_ref, poly, parts, full, once)
        y_ref[...] = once[...]
        mul_parts(poly, hold, parts, full, gram)

    turn(True)

    def later(_, carry):
        turn(False)
        return carry

    lax.fori_loop(1, NEWTON_STEPS - 1, later, 0)
    mul_parts(y_ref, gram, parts, False, once)
    mul_parts(once, gram, parts, False, twice)
    y_ref[...] = newton_a * y_ref[...] + newton_b * once[...] + newton_c * twice[...]


def newton_one(gram, rows):
    return pl.pallas_call(
        newton_kernel,
        in_specs=[VM] * 2,
        out_specs=VM,
        out_shape=shape(rows.shape, F32),
        scratch_shapes=[pltpu.VMEM((D, D), F32)] * 3
        + [pltpu.VMEM((3, D, D), BF)]
        + [pltpu.VMEM(rows.shape, F32)] * 2,
        compiler_params=params(),
        name="newton",
        cost_estimate=cost(60),
    )(gram, rows)


SWAP = [(0, 1), (1, 0)]


def choose(first, when_first, when_second):
    return jnp.where(first, when_first, when_second)


def both_rows(first, of_first, of_second):
    keep = choose(first, of_first, of_second)
    other = lax.ppermute(choose(first, of_second, of_first), "sc", SWAP)
    return jnp.concatenate(
        [choose(first, keep, other), choose(first, other, keep)], axis=0
    )


def own_rows(first, rows):
    upper, lower = jnp.split(rows, 2, axis=0)
    keep = choose(first, upper, lower)
    other = lax.ppermute(choose(first, lower, upper), "sc", SWAP)
    return choose(first, keep, other), choose(first, other, keep)


def newton_small_kernel(x_ref, y_ref):
    values = x_ref[...]
    size = 1.0 / (jnp.sqrt(jnp.sum(values * values, keepdims=True)) + 1e-07)
    values = values * size
    for _ in range(NEWTON_STEPS):
        gram = lax.dot_general(
            values, values, (((0,), (0,)), ((), ())), precision=highest, preferred_element_type=F32
        )
        once = mul(values, gram)
        values = newton_a * values + newton_b * once + newton_c * mul(once, gram)
    y_ref[...] = values


def newton_small(values):
    return pl.pallas_call(
        newton_small_kernel,
        in_specs=[VM],
        out_specs=VM,
        out_shape=shape(values.shape, F32),
        name="newton_small",
    )(values)


def place(dp, sp):
    return (dp, sp // 2, lax.rem(sp, 2))


def greet(count):
    dp, sp = lax.axis_index("dp"), lax.axis_index("sy") * 2 + lax.axis_index("sc")
    barrier = pltpu.get_barrier_semaphore()
    for o in range(1, count):
        pl.semaphore_signal(
            barrier, inc=1, device_id=place(lax.rem(dp + o, count), sp),
            device_id_type=pl.DeviceIdType.MESH,
        )
    for j in range(1, SPLIT):
        pl.semaphore_signal(
            barrier, inc=1, device_id=place(dp, sp ^ j), device_id_type=pl.DeviceIdType.MESH
        )
    pl.semaphore_wait(barrier, count - 1 + SPLIT - 1)
    return dp, sp


def send(source, target, out_sem, in_sem, device):
    copy = pltpu.make_async_remote_copy(
        src_ref=source, dst_ref=target, send_sem=out_sem, recv_sem=in_sem, device_id=device,
        device_id_type=pl.DeviceIdType.MESH,
    )
    copy.start()
    return copy


def gather_kernel(
    count, vec_ref, spec_ref, vec_out, wu, wv, w1, bias, c1,
    vbuf, sbuf, send_v, recv_v, send_s, recv_s, send_w, recv_w, send_t, recv_t,
):
    rows, cols = spec_ref.shape[0], vec_ref.shape[1]
    dp, sp = greet(count)
    vbuf[sp, dp] = jnp.zeros(vbuf.shape[2:], F32)
    vbuf[sp, dp, : vec_ref.shape[0], :cols] = vec_ref[...]
    sbuf[sp, dp] = jnp.zeros(sbuf.shape[2:], BF)
    sbuf[sp, dp, :, :BS] = spec_ref[...].astype(BF)
    copies = []
    for o in range(1, count):
        device = place(lax.rem(dp + o, count), sp)
        here = vbuf.at[sp, dp]
        copies.append(send(here, here, send_v.at[o], recv_v.at[o], device))
        here = sbuf.at[sp, dp]
        copies.append(send(here, here, send_s.at[o], recv_s.at[o], device))
    for ref in (wu, wv, w1):
        ref[...] = jnp.zeros_like(ref)
    for copy in copies:
        copy.wait()
    copies = []
    for j in range(1, SPLIT):
        device = place(dp, sp ^ j)
        copies.append(send(vbuf.at[sp], vbuf.at[sp], send_w.at[j], recv_w.at[j], device))
        copies.append(send(sbuf.at[sp], sbuf.at[sp], send_t.at[j], recv_t.at[j], device))
    for copy in copies:
        copy.wait()
    for i in range(count * SPLIT):
        vec_out[: vec_ref.shape[0], i * cols : (i + 1) * cols] = vbuf[
            i % SPLIT, i // SPLIT, : vec_ref.shape[0], :cols
        ]
        value = sbuf[i % SPLIT, i // SPLIT][:, :BS]
        cell, off = divmod(i * rows, BS)
        layer, part, g, b = cell // 16, (cell // 8) % 2, (cell % 8) // 2, cell % 2
        re = slice(b * BS + off, b * BS + off + rows)
        im = slice(GD + b * BS + off, GD + b * BS + off + rows)
        to_re, to_im = slice(b * BS, (b + 1) * BS), slice(GD + b * BS, GD + (b + 1) * BS)
        if layer == 0 and part == 0:
            wu[g, re, to_re] = value
            wv[g, re, to_im] = value
        elif layer == 0:
            wu[g, re, to_im] = value
            wv[g, re, to_re] = -value
        elif part == 0:
            w1[g, re, to_re] = value
            w1[g, im, to_im] = value
        else:
            w1[g, re, to_im] = value
            w1[g, im, to_re] = -value
    for g in range(SPLIT):
        cut = slice(g * GD, (g + 1) * GD)
        for layer in range(2):
            row = 9 + 2 * layer
            bias[g, layer : layer + 1, :GD] = vec_out[row : row + 1, cut]
            bias[g, layer : layer + 1, GD:] = vec_out[row + 1 : row + 2, cut]
    for piece in range(12):
        r, k = divmod(piece, 3)
        c, m = divmod(piece, 2)
        c1[c : c + 1, m * 256 : (m + 1) * 256] = vec_out[5 + r : 6 + r, k * 256 : (k + 1) * 256]


def dma_sems(*counts):
    return [pltpu.SemaphoreType.DMA((n,)) for n in counts]


def gather_small(count, vectors, spectral):
    rows = spectral.shape[0]
    return pl.pallas_call(
        functools.partial(gather_kernel, count),
        in_specs=[VM] * 2,
        out_specs=[VM] * 6,
        out_shape=[
            shape((16, D), F32),
            shape((SPLIT, GD, PAIR), BF),
            shape((SPLIT, GD, PAIR), BF),
            shape((SPLIT, PAIR, PAIR), BF),
            shape((SPLIT, 2, PAIR), F32),
            shape((NC, FC), F32),
        ],
        scratch_shapes=[
            pltpu.VMEM((SPLIT, count, 16, 128), F32),
            pltpu.VMEM((SPLIT, count, rows, 128), BF),
        ]
        + dma_sems(count, count, count, count, SPLIT, SPLIT, SPLIT, SPLIT),
        compiler_params=pltpu.CompilerParams(
            vmem_limit_bytes=VMEM_LIMIT, collective_id=0, has_side_effects=True
        ),
        name="gather_small",
        cost_estimate=cost(20),
    )(vectors, spectral)


def scatter_sums(count, dp, sp, jobs):
    copies = []
    for x_ref, land, total, land_two, (send_a, recv_a, send_b, recv_b) in jobs:
        for j in range(1, SPLIT):
            source = x_ref.at[:, sp ^ j]
            copies.append(
                send(source, land.at[j - 1], send_a.at[j], recv_a.at[j], place(dp, sp ^ j))
            )
    for copy in copies:
        copy.wait()
    copies = []
    for x_ref, land, total, land_two, (send_a, recv_a, send_b, recv_b) in jobs:
        total[...] = (x_ref[:, sp] + land[0]) + (land[1] + land[2])
        for o in range(1, count):
            to = lax.rem(dp + o, count)
            copies.append(
                send(total.at[to], land_two.at[o - 1], send_b.at[o], recv_b.at[o], place(to, sp))
            )
    for copy in copies:
        copy.wait()
    results = []
    for x_ref, land, total, land_two, sems in jobs:
        result = total[dp]
        for o in range(1, count):
            result = result + land_two[o - 1]
        results.append(result)
    return results


def scatter_scratch(count, rows, width):
    return [
        pltpu.VMEM((SPLIT - 1, count, rows, width), F32),
        pltpu.VMEM((count, rows, width), F32),
        pltpu.VMEM((count, rows, width), F32),
    ] + dma_sems(SPLIT, SPLIT, count, count)


def vectors_kernel(
    count, gspec, gv_lo, gv_hi, gv, gc1, ge_lo, ge, vec_ref, first_ref, second_ref,
    red_spec, new_vec, new_first, new_second, full, esum, x_ref, *scratch,
):
    height, cols = vec_ref.shape
    dp, sp = greet(count)
    full[...] = jnp.zeros_like(full)
    full[0:2, :] = gv_lo[...] + gv_hi[...]
    full[2:5, :] = gv[0:3, :]
    esum[...] = ge_lo[...]
    esum[sp] += ge[...]
    for piece in range(12):
        r, k = divmod(piece, 3)
        c, m = divmod(piece, 2)
        full[5 + r : 6 + r, k * 256 : (k + 1) * 256] = gc1[c : c + 1, m * 256 : (m + 1) * 256]
    for g in range(SPLIT):
        cut = slice(g * GD, (g + 1) * GD)
        for layer in range(2):
            row = 9 + 2 * layer
            full[row : row + 1, cut] = esum[g, layer : layer + 1, :GD]
            full[row + 1 : row + 2, cut] = esum[g, layer : layer + 1, GD:]
    x_ref[...] = jnp.zeros_like(x_ref)
    for i in range(count * SPLIT):
        x_ref[i // SPLIT, i % SPLIT, :, :cols] = full[:, i * cols : (i + 1) * cols]
    jobs = [
        (ref, *mine[:3], mine[3:]) for ref, mine in ((gspec, scratch[:7]), (x_ref, scratch[7:]))
    ]
    red_spec[...], grad = scatter_sums(count, dp, sp, jobs)
    grad = grad[:height, :cols]
    first = beta_one * first_ref[...] + (1.0 - beta_one) * grad
    second = beta_two * second_ref[...] + (1.0 - beta_two) * grad * grad
    new_first[...] = first
    new_second[...] = second
    first_hat = first / (1.0 - beta_one**STEP)
    second_hat = second / (1.0 - beta_two**STEP)
    new_vec[...] = vec_ref[...] * (1.0 - adam_rate * decay) - adam_rate * first_hat / (
        jnp.sqrt(second_hat) + 1e-08
    )


def update_small(count, grads, pieces, vectors, first, second):
    rows = 4 * NB * BS // (count * SPLIT)
    return pl.pallas_call(
        functools.partial(vectors_kernel, count),
        in_specs=[VM] * 10,
        out_specs=[VM] * 4,
        out_shape=[shape((rows, BS), F32)] + [shape(vectors.shape, F32)] * 3,
        scratch_shapes=[
            pltpu.VMEM((16, D), F32),
            pltpu.VMEM((SPLIT, 2, PAIR), F32),
            pltpu.VMEM((count, SPLIT, 16, 128), F32),
        ]
        + scatter_scratch(count, rows, BS)
        + scatter_scratch(count, 16, 128),
        compiler_params=pltpu.CompilerParams(
            vmem_limit_bytes=VMEM_LIMIT, collective_id=2, has_side_effects=True
        ),
        name="update_small",
        cost_estimate=cost(25),
    )(grads.reshape(count, SPLIT, rows, BS), *pieces, vectors, first, second)


def reduce_kernel(
    bits, keep, give, moment, new_moment, direction, gram,
    acc, land, red, load_sem, give_sems, *scratch,
):
    half = moment.shape[0] // 2
    dp, sy, sc = (lax.axis_index(name) for name in ("dp", "sy", "sc"))
    swap = (dp, sy, 1 - sc)
    partners = [(dp, 1 - sy, sc)] + [(dp ^ (1 << b), sy, sc) for b in range(bits - 1)]
    mine = [sy] + [lax.rem(dp // (1 << b), 2) for b in range(bits - 1)]
    barrier = pltpu.get_barrier_semaphore()
    for device in [swap] + partners:
        pl.semaphore_signal(barrier, inc=1, device_id=device, device_id_type=pl.DeviceIdType.MESH)
    load = pltpu.make_async_copy(keep, acc, load_sem)
    load.start()
    pl.semaphore_wait(barrier, bits + 1)
    copy = send(give, land, give_sems.at[0], give_sems.at[1], swap)
    load.wait()
    copy.wait()

    def join(o, _):
        for t in range(2):
            acc[o, t] = acc[o, t] + land[o, t].astype(F32)
        return 0

    lax.fori_loop(0, 2**bits, join, 0)
    streams = []
    for t in range(2):
        order = list(range(1, bits)) + [0]
        if t == 1:
            order[0], order[1] = order[1], order[0]
        streams.append(order)
    left = [list(range(bits)), list(range(bits))]
    current = [lambda block, t=t: acc.at[block, t] for t in range(2)]
    for stage in range(bits):
        count = 2 ** (bits - 1 - stage)
        copies = []
        for t in range(2):
            outgoing, incoming, _sum, sems = scratch[(stage * 2 + t) * 4 : (stage * 2 + t) * 4 + 4]
            bit = streams[t][stage]
            step = 1 << left[t].index(bit)
            side = mine[bit]

            def cast(o, _, t=t, outgoing=outgoing, step=step, side=side):
                block = (o // step) * (2 * step) + (1 - side) * step + lax.rem(o, step)
                outgoing[o] = current[t](block)[...].astype(BF)
                return 0

            lax.fori_loop(0, count, cast, 0)
            copies.append(send(outgoing, incoming, sems.at[0], sems.at[1], partners[bit]))
        following = []
        for t in range(2):
            outgoing, incoming, total, sems = scratch[(stage * 2 + t) * 4 : (stage * 2 + t) * 4 + 4]
            bit = streams[t][stage]
            step = 1 << left[t].index(bit)
            side = mine[bit]
            left[t].remove(bit)
            copies[t].wait()

            def add(o, _, t=t, incoming=incoming, total=total, step=step, side=side):
                block = (o // step) * (2 * step) + side * step + lax.rem(o, step)
                total[o] = current[t](block)[...] + incoming[o].astype(F32)
                return 0

            lax.fori_loop(0, count, add, 0)
            following.append(lambda block, total=total: total.at[block])
        current = following
    for t in range(2):
        red[t * half : (t + 1) * half, :] = current[t](0)[...]
    new = momentum * moment[...] + red[...]
    new_moment[...] = new
    pushed = red[...] + momentum * new
    direction[...] = pushed
    top, middle, low = split_three(pushed)
    gram[...] = (
        (dot_tn(middle, middle) + dot_tn(top, low) + dot_tn(low, top))
        + (dot_tn(top, middle) + dot_tn(middle, top))
    ) + dot_tn(top, top)


def reduce_feed(count, keep, give, moment):
    rows = moment.shape[0]
    blocks = FF // rows
    bits = blocks.bit_length() - 1
    whole = (blocks, 2, rows // 2, D)
    scratch = []
    for stage in range(bits):
        for _ in range(2):
            part = (2 ** (bits - 1 - stage), rows // 2, D)
            scratch += [pltpu.VMEM(part, BF), pltpu.VMEM(part, BF), pltpu.VMEM(part, F32)] + dma_sems(2)
    return pl.pallas_call(
        functools.partial(reduce_kernel, bits),
        in_specs=[ANY, ANY, VM],
        out_specs=[VM] * 3,
        out_shape=[shape((rows, D), F32)] * 2 + [shape((D, D), F32)],
        scratch_shapes=[
            pltpu.VMEM(whole, F32),
            pltpu.VMEM(whole, BF),
            pltpu.VMEM((rows, D), F32),
            pltpu.SemaphoreType.DMA,
        ]
        + dma_sems(2)
        + scratch,
        compiler_params=pltpu.CompilerParams(
            vmem_limit_bytes=VMEM_LIMIT, collective_id=1, has_side_effects=True
        ),
        name="reduce_feed",
        cost_estimate=cost(80),
    )(keep.reshape(whole), give.reshape(whole), moment)


def after(values, earlier):
    return lax.optimization_barrier((values, earlier))[0]


def body(
    count, samples_hi, samples_lo, cotan_hi, cotan_lo, live_slots, spectral_w, vectors, weight_in,
    weight_out, moment_spec, moment_in, moment_out, adam_first, adam_second,
):
    axes = ("dp", *SP)
    chips = ("dp", "sy")
    sp = lax.axis_index(SP)
    first = lax.axis_index("sc") == 0
    own = sp.astype(jnp.int32).reshape(1)
    wide, tall, wide_lo, tall_lo = (t.astype(BF) for t in tables())
    tabs = (wide, np.swapaxes(wide, 1, 2), tall, tall.T)
    tabs_lo = (wide_lo, wide_lo.T, tall_lo, tall_lo.T)
    tabs = tuple(jnp.asarray(np.ascontiguousarray(t)) for t in tabs)
    tabs_lo = tuple(jnp.asarray(np.ascontiguousarray(t)) for t in tabs_lo)

    vec, wu, wv, w1, bias, bias_hidden = gather_small(count, vectors, spectral_w)
    weights = (wu, wv, w1)
    slice_in, slice_out = after((weight_in, weight_out), vec)
    win = lax.all_gather(slice_in.T.astype(BF), axes, axis=0, tiled=True)
    wout = lax.all_gather(slice_out.astype(BF), axes, axis=0, tiled=True)

    split_hi = samples_hi.reshape(2, HALF, OWN, D)
    split_cot = cotan_hi.reshape(2, HALF, OWN, D)
    one_lo = samples_lo.reshape(HL, WL, D).transpose(1, 0, 2)
    one_cot = cotan_lo.reshape(HL, WL, D).transpose(1, 0, 2)

    moment = both_rows(first, moment_in.T, moment_out)
    slabs = exchange(norm_packed(own, split_hi, vec))
    field_lo, four_lo = filter_forward_lo(one_lo, vec, tabs_lo, weights, bias)
    slabs = after(slabs, field_lo)
    fields, four = filter_forward(own, slabs, tabs, weights, bias)
    field_lo = after(field_lo, fields)
    fields = exchange(fields)
    block_lo, gm_lo, gw, gc1, gv = feed(
        False, own, live_slots, one_lo, one_cot, [field_lo], vec, bias_hidden, win, wout, ()
    )
    block_hi, p0, p1, p2, p3, keep, give, gc1, gv = feed(
        True, own, live_slots, split_hi, split_cot, fields, vec, bias_hidden, win, wout,
        (gw, gc1, gv),
    )
    packs = [p0, p1, p2, p3]
    grad_slabs = exchange(packs)
    new_moment, direction, gram = reduce_feed(count, keep, give, moment)
    gram = lax.psum(gram, chips)
    grad_slabs = after(grad_slabs, direction)
    back, gspec, ge = filter_backward(own, grad_slabs, four, tabs, weights, bias)
    back = exchange(back)
    gm_lo = after(gm_lo, gspec)
    grad_lo, gspec, ge_lo, gv_lo = filter_backward_lo(
        one_lo, gm_lo, four_lo, vec, tabs_lo, weights, bias, gspec
    )
    gram = after(gram, gspec)
    orth = newton_one(gram, direction)
    back = after(back, orth)
    grad_hi, gv_hi = norm_backward(own, split_hi, packs, back, vec)
    red_spec, new_vectors, new_adam_first, new_adam_second = update_small(
        count, gspec, (gv_lo, gv_hi, gv, gc1, ge_lo, ge), vectors, adam_first, adam_second
    )
    new_moment_in, new_moment_out = own_rows(first, new_moment)
    orth_in, orth_out = own_rows(first, orth)
    new_moment_spec = momentum * moment_spec + red_spec
    dir_spec = red_spec + momentum * new_moment_spec
    rows = moment_spec.shape[0]
    if rows == BS:
        orth_spec = newton_small(dir_spec)
    else:
        gathered = lax.all_gather(dir_spec, SP, axis=0, tiled=True)
        orth_spec = lax.dynamic_slice_in_dim(newton_small(gathered), sp * rows, rows, 0)

    keep_share = 1.0 - muon_rate * decay
    new_weight_in = weight_in * keep_share - muon_rate * orth_in.T
    new_weight_out = weight_out * keep_share - muon_rate * math.sqrt(max(1.0, FF / D)) * orth_out
    new_spectral = spectral_w * keep_share - muon_rate * orth_spec
    return (
        block_hi.reshape(samples_hi.shape),
        block_lo.transpose(1, 0, 2).reshape(samples_lo.shape),
        grad_hi.reshape(samples_hi.shape),
        grad_lo.reshape(samples_lo.shape),
        new_spectral,
        new_weight_in,
        new_weight_out,
        new_moment_spec,
        new_moment_in.T,
        new_moment_out,
        new_vectors,
        new_adam_first,
        new_adam_second,
    )


def solution(mesh):
    count = mesh.shape["dp"]
    fine = jax.sharding.Mesh(mesh.devices.reshape(count, 2, 2), ("dp", *SP))
    both = ("dp", *SP)
    hi = P("dp", None, SP, None)
    lo = P(both, None, None, None)
    rows = P(both, None)
    cols = P(None, both)
    return jax.shard_map(
        functools.partial(body, count),
        mesh=fine,
        in_specs=(hi, lo, hi, lo, P(both), rows, cols, cols, rows, rows, cols, rows, cols, cols),
        out_specs=(hi, lo, hi, lo, rows, cols, rows, rows, cols, rows, cols, cols, cols),
        check_vma=False,
    )
```

```python
import functools
import math

import jax
import jax.numpy as jnp
import numpy as np
from jax import lax
from jax.experimental import pallas as pl
from jax.experimental.pallas import tpu as pltpu
from jax.sharding import PartitionSpec as P

D = 768
FF = 3072
NB = 8
BS = 96
H = 90
W = 180
HL = 23
WL = 45
STEP = 10
NEWTON_STEPS = 5

F32 = jnp.float32
BF = jnp.bfloat16
highest = lax.Precision.HIGHEST
epsilon = 1e-06
shrink_level = 0.01
shrink_sharp = 10.0
momentum = 0.95
newton_a = 3.4445
newton_b = -4.775
newton_c = 2.0315
muon_rate = 0.5
adam_rate = 0.3
decay = 0.01
beta_one = 0.9
beta_two = 0.999

K0 = math.sqrt(2.0 / math.pi)
K1 = K0 * 0.044715

SPLIT = 4
GD = D // SPLIT
PAIR = 2 * GD
HALF = H // 2
OWN = W // SPLIT
PW = 48
PM = 96
KF = W // 2 + 1
KP = 96
KG = 7
GROUPS = KF // KG
ROWS = KG * PM
LH = 24
LK = HL // 2 + 1
LROWS = LK * PW
HB = 5
LB = 15
FC = 768
NC = FF // FC
VMEM_LIMIT = 60 * 2**20
UNROLL = 9
PITCH = 56


def wave(length, rows, cols):
    phase = np.outer(rows, cols) % length
    angle = phase * (2.0 * math.pi / length)
    factor = 1.0 / math.sqrt(length)
    return np.cos(angle) * factor, np.sin(angle) * factor


def tables():
    wide = np.zeros((SPLIT, 2 * KP, SPLIT * PW))
    for s in range(SPLIT):
        for j in range(SPLIT):
            cols = (s ^ j) * OWN + np.arange(OWN)
            c, d = wave(W, np.arange(KF), cols)
            wide[s, :KF, j * PW : j * PW + OWN] = c
            wide[s, KP : KP + KF, j * PW : j * PW + OWN] = -d
    tall = np.zeros((2 * PM, 2 * PM))
    for part in range(2):
        c, d = wave(H, np.arange(H), part * HALF + np.arange(HALF))
        re, im = part * PW, PM + part * PW
        tall[:H, re : re + HALF] = c
        tall[:H, im : im + HALF] = d
        tall[PM : PM + H, re : re + HALF] = -d
        tall[PM : PM + H, im : im + HALF] = c
    wide_lo = np.zeros((2 * LK, LH))
    c, d = wave(HL, np.arange(LK), np.arange(HL))
    wide_lo[:LK, :HL] = c
    wide_lo[LK:, :HL] = -d
    tall_lo = np.zeros((2 * PW, 2 * PW))
    c, d = wave(WL, np.arange(WL), np.arange(WL))
    tall_lo[:WL, :WL] = c
    tall_lo[:WL, PW : PW + WL] = d
    tall_lo[PW : PW + WL, :WL] = -d
    tall_lo[PW : PW + WL, PW : PW + WL] = c
    return wide, tall, wide_lo, tall_lo


def loop(count, unroll, one):
    def some(i, carry):
        for n in range(unroll):
            one(i * unroll + n)
        return carry

    lax.fori_loop(0, count // unroll, some, 0)


def dot(left, right):
    return jnp.dot(left, right, preferred_element_type=F32)


def dot_nt(left, right):
    return lax.dot_general(left, right, (((1,), (1,)), ((), ())), preferred_element_type=F32)


def dot_tn(left, right):
    return lax.dot_general(left, right, (((0,), (0,)), ((), ())), preferred_element_type=F32)


def normed(values):
    center = values - jnp.mean(values, axis=-1, keepdims=True)
    scale = lax.rsqrt(jnp.mean(center * center, axis=-1, keepdims=True) + epsilon)
    return center * scale, scale


def norm_back(grad, norm, scale, gain):
    pushed = grad * gain
    return scale * (
        pushed
        - jnp.mean(pushed, axis=-1, keepdims=True)
        - norm * jnp.mean(pushed * norm, axis=-1, keepdims=True)
    )


def pad_rows(values, rows=PW):
    return jnp.concatenate(
        [values, jnp.zeros((rows - values.shape[0], values.shape[1]), values.dtype)], axis=0
    )


def lanes(*pieces):
    return jnp.concatenate(pieces, axis=1)


def unpack_pair(fs):
    pieces = [fs[g].astype(F32) for g in range(SPLIT)]
    return (
        lanes(*[p[:, :GD] for p in pieces]),
        lanes(*[p[:, GD:] for p in pieces]),
    )


def pack_pair(row_a, row_b, fs):
    for g in range(SPLIT):
        cut = slice(g * GD, (g + 1) * GD)
        fs[g] = lanes(row_a[:, cut], row_b[:, cut]).astype(BF)


SP = ("sy", "sc")
VM = pl.BlockSpec(memory_space=pltpu.VMEM)
SM = pl.BlockSpec(memory_space=pltpu.SMEM)
ANY = pl.BlockSpec(memory_space=pl.ANY)


def params():
    return pltpu.CompilerParams(vmem_limit_bytes=VMEM_LIMIT)


def cost(us):
    return pl.CostEstimate(flops=us * 10**9, bytes_accessed=us * 10**6, transcendentals=0)


def shape(dims, kind):
    return jax.ShapeDtypeStruct(dims, kind)


PACKED = (HALF, PW, PAIR)
PACKED_BLOCK = pl.BlockSpec((HB, PW, PAIR), lambda i: (i, 0, 0))
WIDE_BLOCK = pl.BlockSpec((2, HB, OWN, D), lambda i: (0, i, 0, 0))


def pack_kernel(own_ref, x_ref, o0, o1, o2, o3, fs):
    own = own_ref[0]

    for i in range(HB):
        rows = []
        for part in range(2):
            norm, _unused = normed(x_ref[part, i].astype(F32))
            rows.append(pad_rows(norm))
        pack_pair(rows[0], rows[1], fs.at[i])
    for i in range(HB):
        for j, out in enumerate((o0, o1, o2, o3)):
            out[i] = fs[i, own ^ j]


def norm_packed(own, samples):
    return pl.pallas_call(
        pack_kernel,
        grid=(HALF // HB,),
        in_specs=[SM, WIDE_BLOCK],
        out_specs=[PACKED_BLOCK] * SPLIT,
        out_shape=[shape(PACKED, BF)] * SPLIT,
        scratch_shapes=[pltpu.VMEM((HB, SPLIT, PW, PAIR), BF)],
        compiler_params=params(),
        name="norm_pack",
        cost_estimate=cost(16),
    )(own, samples)


def exchange(slabs):
    moved = [slabs[0]]
    for j in range(1, SPLIT):
        moved.append(lax.ppermute(slabs[j], SP, [(i, i ^ j) for i in range(SPLIT)]))
    return moved


def to_freq_wide(slabs, table, space, lead=None):
    def one(i):
        rows = jnp.concatenate([slab[i] for slab in slabs], axis=0)
        if lead is not None:
            rows = (rows.astype(F32) * lead[0:1, :] + lead[1:2, :]).astype(BF)
        area = dot(table[...], rows)
        for c in range(3):
            space[c, pl.ds(i, 2 * KP, stride=PITCH), :] = area[:, c * 128 : (c + 1) * 128]

    loop(HALF, UNROLL, one)


def to_freq_tall(k, table, space):
    re = lanes(*[space[c, pl.ds(pl.multiple_of(k * PITCH, 8), PW), :] for c in range(3)])
    im = lanes(*[space[c, pl.ds(pl.multiple_of((KP + k) * PITCH, 8), PW), :] for c in range(3)])
    rows = jnp.concatenate([re[:, :GD], re[:, GD:], im[:, :GD], im[:, GD:]], axis=0)
    return dot(table[...], rows.astype(BF))


def to_space_tall(k, table, four, space):
    back = dot(table[...], four)
    for part in range(2):
        base = part * PM
        packed = lanes(back[base : base + PW], back[base + PW : base + PM])
        at = pl.ds(pl.multiple_of((part * KP + k) * PITCH, 8), PW)
        for c in range(3):
            space[c, at, :] = packed[:, c * 128 : (c + 1) * 128]


def to_space_wide(table, space, outs):
    def one(i):
        rows = lanes(*[space[c, pl.ds(i, 2 * KP, stride=PITCH), :] for c in range(3)])
        field = dot(table[...], rows.astype(BF)).astype(BF)
        for j, out in enumerate(outs):
            out[i] = field[j * PW : (j + 1) * PW]

    loop(HALF, UNROLL, one)


def clear_pads(space, used, count):
    for c in range(space.shape[0]):
        for row in range(used, PW):
            space[c, pl.ds(row, count, stride=PITCH), :] = jnp.zeros((count, 128), F32)


def keep_minus(row, width, first, last):
    at = row + lax.broadcasted_iota(jnp.int32, (width, 1), 0)
    return jnp.where((at >= first) & (at < last), 1.0, 0.0).astype(F32)


def mlp_forward(fre, fim, wu, wv, w1, bias, us, vs, actp, actm, put, base, first, last, chunk):
    rows = us.shape[0]
    cuts = [slice(i * chunk, (i + 1) * chunk) for i in range(rows // chunk)]
    for at in cuts:
        us[at, :] = dot(fre[at, :], wu)
        vs[at, :] = dot(fim[at, :], wv)
    b0, b1 = bias[0:1, :], bias[1:2, :]

    def act(i, _):
        at = slice(i * chunk, (i + 1) * chunk)
        u = us[at, :] + b0
        v = vs[at, :]
        for ref, value in ((actp, u + v), (actm, u - v)):
            t = jnp.tanh(value * (K0 + K1 * (value * value)))
            ref[at, :] = (value * (0.5 + 0.5 * t)).astype(BF)
        return 0

    for i in range(rows // chunk):
        act(i, 0)
    for at in cuts:
        us[at, :] = dot(actp[at, :], w1)
        vs[at, :] = dot(actm[at, :], w1)

    def shrunk(i, _):
        at = slice(i * chunk, (i + 1) * chunk)
        p = us[at, :] + b1
        m = vs[at, :] + b1
        p = p - shrink_level * jnp.tanh(shrink_sharp * p)
        m = (m - shrink_level * jnp.tanh(shrink_sharp * m)) * keep_minus(
            base + i * chunk, chunk, first, last
        )
        put(at, (p[:, :GD] + m[:, :GD]).astype(BF), (p[:, GD:] - m[:, GD:]).astype(BF))
        return 0

    for i in range(rows // chunk):
        shrunk(i, 0)


def mlp_backward(
    fre, fim, gs, wu, wv, w1, bias, us, vs, actp, actm, dp, dm, gsp, gsm, sums, put,
    gwu, gwv, gw1, ge, base, first, last, chunk,
):
    rows = us.shape[0]
    us[...] = dot(fre, wu)
    vs[...] = dot(fim, wv)
    b0, b1 = bias[0:1, :], bias[1:2, :]
    sign = jnp.where(lax.broadcasted_iota(jnp.int32, (1, PAIR), 1) < GD, 1.0, -1.0).astype(F32)

    def act(i, _):
        at = slice(i * chunk, (i + 1) * chunk)
        u = us[at, :] + b0
        v = vs[at, :]
        for ref, slope, value in ((actp, dp, u + v), (actm, dm, u - v)):
            square = value * value
            hp = 0.5 + 0.5 * jnp.tanh(value * (K0 + K1 * square))
            on = value * hp
            ref[at, :] = on.astype(BF)
            slope[at, :] = hp + on * (1.0 - hp) * (2.0 * K0 + 6.0 * K1 * square)
        return 0

    for i in range(rows // chunk):
        act(i, 0)
    us[...] = dot(actp[...], w1)
    vs[...] = dot(actm[...], w1)

    def second(i, total):
        at = slice(i * chunk, (i + 1) * chunk)
        grad = gs[at, :]
        tp = jnp.tanh(shrink_sharp * (us[at, :] + b1))
        tm = jnp.tanh(shrink_sharp * (vs[at, :] + b1))
        flat = 1.0 - shrink_level * shrink_sharp
        bend = shrink_level * shrink_sharp
        p = grad * (flat + bend * (tp * tp))
        m = (grad * (sign * keep_minus(base + i * chunk, chunk, first, last))) * (
            flat + bend * (tm * tm)
        )
        gsp[at, :] = p.astype(BF)
        gsm[at, :] = m.astype(BF)
        return total + jnp.sum(p + m, axis=0, keepdims=True)

    total = jnp.zeros((1, PAIR), F32)
    for i in range(rows // chunk):
        total = second(i, total)
    ge[1:2, :] += total
    us[...] = dot_nt(gsp[...], w1)
    vs[...] = dot_nt(gsm[...], w1)
    gw1[...] += dot_tn(actp[...], gsp[...]) + dot_tn(actm[...], gsm[...])

    def first_grad(i, total):
        at = slice(i * chunk, (i + 1) * chunk)
        p = us[at, :] * dp[at, :]
        m = vs[at, :] * dm[at, :]
        both = p + m
        gsp[at, :] = both.astype(BF)
        gsm[at, :] = (p - m).astype(BF)
        return total + jnp.sum(both, axis=0, keepdims=True)

    total = jnp.zeros((1, PAIR), F32)
    for i in range(rows // chunk):
        total = first_grad(i, total)
    ge[0:1, :] += total
    gwu[...] += dot_tn(fre, gsp[...])
    gwv[...] += dot_tn(fim, gsm[...])
    put(dot_nt(gsp[...], wu).astype(BF), dot_nt(gsm[...], wv).astype(BF))


def block_grads(gwu, gwv, gw1):
    cells = {}
    for b in range(2):
        r = slice(b * BS, (b + 1) * BS)
        i = slice(GD + b * BS, GD + (b + 1) * BS)
        cells[0, 0, b] = gwu[r, r] + gwv[r, i]
        cells[0, 1, b] = gwu[r, i] - gwv[r, r]
        cells[1, 0, b] = gw1[r, r] + gw1[i, i]
        cells[1, 1, b] = gw1[r, i] - gw1[i, r]
    return cells


def filter_kernel(
    own_ref, x0, x1, x2, x3, tw, twt, th, tht, wu, wv, w1, bias, lead,
    y0, y1, y2, y3, four, space, us, vs, actp, actm, zr, zi,
):
    own = own_ref[0]
    clear_pads(space, HALF, 2 * KP)
    to_freq_wide((x0, x1, x2, x3), tw.at[own], space, lead.at[own])

    def group(g, _):
        for n in range(KG):
            rows = to_freq_tall(g * KG + n, th, space).astype(BF)
            four[g, 0, n * PM : (n + 1) * PM, :] = rows[:PM]
            four[g, 1, n * PM : (n + 1) * PM, :] = rows[PM:]

        def put(at, re, im):
            zr[at, :] = re
            zi[at, :] = im

        mlp_forward(
            four[g, 0], four[g, 1], wu[own], wv[own], w1[own], bias.at[own], us, vs, actp, actm, put,
            g * ROWS, PM, (KF - 1) * PM, ROWS // 3,
        )
        for n in range(KG):
            at = slice(n * PM, (n + 1) * PM)
            to_space_tall(
                g * KG + n, tht, jnp.concatenate([zr[at, :], zi[at, :]], axis=0), space
            )
        return 0

    lax.fori_loop(0, GROUPS, group, 0)
    to_space_wide(twt.at[own], space, (y0, y1, y2, y3))


def filter_scratch(rows, wide):
    big = pltpu.VMEM((rows, PAIR), F32)
    low = pltpu.VMEM((rows, PAIR), BF)
    part = pltpu.VMEM((rows, GD), BF)
    return big, low, part


def filter_forward(own, slabs, tabs, weights, bias, lead):
    big, low, part = filter_scratch(ROWS, None)
    outs = pl.pallas_call(
        filter_kernel,
        in_specs=[SM] + [VM] * 13,
        out_specs=[VM] * 5,
        out_shape=[shape(PACKED, BF)] * SPLIT + [shape((GROUPS, 2, ROWS, GD), BF)],
        scratch_shapes=[pltpu.VMEM((3, 2 * KP * PITCH, 128), F32), big, big, low, low, part, part],
        compiler_params=params(),
        name="filter_forward",
        cost_estimate=cost(95),
    )(own, *slabs, *tabs, *weights, bias, lead)
    return outs[:SPLIT], outs[SPLIT]


def filter_back_kernel(
    own_ref, x0, x1, x2, x3, four, tw, twt, th, tht, wu, wv, w1, bias, grads_in,
    y0, y1, y2, y3, grads, ge,
    space, us, vs, actp, actm, zr, zi, gs, dp, dm, gsp, gsm, gwu, gwv, gw1,
):
    own = own_ref[0]
    clear_pads(space, HALF, 2 * KP)
    gwu[...] = jnp.zeros_like(gwu)
    gwv[...] = jnp.zeros_like(gwv)
    gw1[...] = jnp.zeros_like(gw1)
    ge[...] = jnp.zeros_like(ge)
    to_freq_wide((x0, x1, x2, x3), tw.at[own], space)

    def group(g, _):
        for n in range(KG):
            rows = to_freq_tall(g * KG + n, th, space)
            gs[n * PM : (n + 1) * PM, :] = lanes(rows[:PM], rows[PM:])

        def put(re, im):
            zr[...] = re
            zi[...] = im

        mlp_backward(
            four[g, 0], four[g, 1], gs, wu[own], wv[own], w1[own], bias.at[own], us, vs, actp, actm, dp, dm,
            gsp, gsm, None, put, gwu, gwv, gw1, ge, g * ROWS, PM, (KF - 1) * PM, ROWS // 2,
        )
        for n in range(KG):
            at = slice(n * PM, (n + 1) * PM)
            to_space_tall(
                g * KG + n, tht, jnp.concatenate([zr[at, :], zi[at, :]], axis=0), space
            )
        return 0

    lax.fori_loop(0, GROUPS, group, 0)
    grads[...] = grads_in[...]
    for (layer, part, b), value in block_grads(gwu, gwv, gw1).items():
        grads[(2 * layer + part) * NB + 2 * own + b] += value
    to_space_wide(twt.at[own], space, (y0, y1, y2, y3))


def filter_backward(own, slabs, four, tabs, weights, bias, grads_in):
    big, low, part = filter_scratch(ROWS, None)
    outs = pl.pallas_call(
        filter_back_kernel,
        in_specs=[SM] + [VM] * 14,
        out_specs=[VM] * 6,
        out_shape=[shape(PACKED, BF)] * SPLIT
        + [shape((4 * NB, BS, BS), F32), shape((2, PAIR), F32)],
        scratch_shapes=[pltpu.VMEM((3, 2 * KP * PITCH, 128), F32), big, big, low, low, part, part]
        + [big, big, big, low, low]
        + [pltpu.VMEM((GD, PAIR), F32)] * 2
        + [pltpu.VMEM((PAIR, PAIR), F32)],
        compiler_params=params(),
        name="filter_backward",
        cost_estimate=cost(125),
    )(own, *slabs, four, *tabs, *weights, bias, grads_in)
    return outs[:SPLIT], outs[SPLIT], outs[SPLIT + 1]


def lo_freq_wide(i, rows, table, space):
    area = dot(table[...], rows)
    for c in range(6):
        space[c, pl.ds(i, 2 * LK, stride=PITCH), :] = area[:, c * 128 : (c + 1) * 128]


def lo_freq_tall(k, table, space):
    parts = []
    for base in (0, LK):
        at = pl.ds(pl.multiple_of((base + k) * PITCH, 8), PW)
        parts.append(lanes(*[space[c, at, :] for c in range(6)]))
    rows = dot(table[...], jnp.concatenate(parts, axis=0).astype(BF))
    return rows[:PW], rows[PW:]


def lo_space_tall(k, table, re, im, space):
    back = dot(table[...], jnp.concatenate([re, im], axis=0).astype(BF))
    for part, base in enumerate((0, LK)):
        at = pl.ds(pl.multiple_of((base + k) * PITCH, 8), PW)
        for c in range(6):
            space[c, at, :] = back[part * PW : (part + 1) * PW, c * 128 : (c + 1) * 128]


def lo_space_wide(i, table, space):
    rows = lanes(*[space[c, pl.ds(i, 2 * LK, stride=PITCH), :] for c in range(6)])
    return dot(table[...], rows.astype(BF))


def filter_lo_kernel(
    x_ref, vec_ref, tw, twt, th, tht, wu, wv, w1, bias, y_ref, four,
    space, us, vs, actp, actm, zr, zi,
):
    clear_pads(space, WL, 2 * LK)
    gain, shift = vec_ref[0:1, :], vec_ref[1:2, :]

    def wide(i):
        norm, _unused = normed(x_ref[i].astype(F32))
        lo_freq_wide(i, pad_rows(norm * gain + shift, LH).astype(BF), tw, space)

    loop(WL, UNROLL, wide)

    def tall(k):
        re, im = lo_freq_tall(k, th, space)
        at = pl.ds(pl.multiple_of(k * PW, PW), PW)
        for g in range(SPLIT):
            cut = slice(g * GD, (g + 1) * GD)
            four[g, 0, at, :] = re[:, cut].astype(BF)
            four[g, 1, at, :] = im[:, cut].astype(BF)

    loop(LK, 3, tall)

    def group(g, _):
        def put(at, re, im):
            zr[g, at, :] = re
            zi[g, at, :] = im

        mlp_forward(
            four[g, 0], four[g, 1], wu[g], wv[g], w1[g], bias.at[g], us, vs, actp, actm, put,
            0, PW, LROWS, LROWS // 3,
        )
        return 0

    lax.fori_loop(0, SPLIT, group, 0)

    def back(k):
        at = pl.ds(pl.multiple_of(k * PW, PW), PW)
        re = lanes(*[zr[g, at, :].astype(F32) for g in range(SPLIT)])
        im = lanes(*[zi[g, at, :].astype(F32) for g in range(SPLIT)])
        lo_space_tall(k, tht, re, im, space)

    loop(LK, 3, back)

    def last(i):
        y_ref[i] = lo_space_wide(i, twt, space).astype(BF)

    loop(WL, UNROLL, last)


def lo_scratch():
    big, low, _ = filter_scratch(LROWS, None)
    part = pltpu.VMEM((SPLIT, LROWS, GD), BF)
    return [pltpu.VMEM((6, 2 * LK * PITCH, 128), F32), big, big, low, low, part, part]


def filter_forward_lo(samples, vectors, tabs, weights, bias):
    return pl.pallas_call(
        filter_lo_kernel,
        in_specs=[VM] * 10,
        out_specs=[VM] * 2,
        out_shape=[shape((WL, LH, D), BF), shape((SPLIT, 2, LROWS, GD), BF)],
        scratch_shapes=lo_scratch(),
        compiler_params=params(),
        name="filter_forward_lo",
        cost_estimate=cost(35),
    )(samples, vectors, *tabs, *weights, bias)


def filter_back_lo_kernel(
    x_ref, gm_ref, four, vec_ref, tw, twt, th, tht, wu, wv, w1, bias,
    grad_ref, grads, ge, gvec,
    space, us, vs, actp, actm, zr, zi, gs, dp, dm, gsp, gsm, gwu, gwv, gw1,
):
    clear_pads(space, WL, 2 * LK)
    ge[...] = jnp.zeros_like(ge)
    gvec[...] = jnp.zeros_like(gvec)

    def wide(i):
        lo_freq_wide(i, gm_ref[i], tw, space)

    loop(WL, UNROLL, wide)

    def tall(k):
        re, im = lo_freq_tall(k, th, space)
        at = pl.ds(pl.multiple_of(k * PW, PW), PW)
        for g in range(SPLIT):
            cut = slice(g * GD, (g + 1) * GD)
            gs[g, at, :] = lanes(re[:, cut], im[:, cut])

    loop(LK, 3, tall)

    def group(g, _):
        gwu[...] = jnp.zeros_like(gwu)
        gwv[...] = jnp.zeros_like(gwv)
        gw1[...] = jnp.zeros_like(gw1)

        def put(re, im):
            zr[g] = re
            zi[g] = im

        mlp_backward(
            four[g, 0], four[g, 1], gs.at[g], wu[g], wv[g], w1[g], bias.at[g], us, vs, actp, actm,
            dp, dm, gsp, gsm, None, put, gwu, gwv, gw1, ge.at[g], 0, PW, LROWS, LROWS // 2,
        )
        for (layer, part, b), value in block_grads(gwu, gwv, gw1).items():
            at = (2 * layer + part) * NB + 2 * g + b
            grads[at] = value
        return 0

    lax.fori_loop(0, SPLIT, group, 0)

    def back(k):
        at = pl.ds(pl.multiple_of(k * PW, PW), PW)
        re = lanes(*[zr[g, at, :].astype(F32) for g in range(SPLIT)])
        im = lanes(*[zi[g, at, :].astype(F32) for g in range(SPLIT)])
        lo_space_tall(k, tht, re, im, space)

    loop(LK, 3, back)
    gain = vec_ref[0:1, :]

    def last(t, _):
        sums = []
        for n in range(UNROLL):
            i = t * UNROLL + n
            field = lo_space_wide(i, twt, space)[:HL]
            direct = gm_ref[i].astype(F32)[:HL]
            norm, scale = normed(x_ref[i].astype(F32))
            grad = field + direct
            sums.append((jnp.sum(grad * norm, axis=0, keepdims=True), jnp.sum(grad, axis=0, keepdims=True)))
            value = direct + norm_back(grad, norm, scale, gain)
            for c in range(6):
                at = pl.ds(6 * i + c, HL, stride=6 * WL)
                grad_ref[at, 0, :] = value[:, c * 128 : (c + 1) * 128]
        gvec[0:1, :] += sum(a for a, b in sums)
        gvec[1:2, :] += sum(b for a, b in sums)
        return 0

    lax.fori_loop(0, WL // UNROLL, last, 0)


def filter_backward_lo(samples, grad_mixed, four, vectors, tabs, weights, bias):
    big, low, _ = filter_scratch(LROWS, None)
    return pl.pallas_call(
        filter_back_lo_kernel,
        in_specs=[VM] * 12,
        out_specs=[VM] * 4,
        out_shape=[
            shape((HL * WL * 6, 1, 128), F32),
            shape((4 * NB, BS, BS), F32),
            shape((SPLIT, 2, PAIR), F32),
            shape((2, D), F32),
        ],
        scratch_shapes=lo_scratch()
        + [pltpu.VMEM((SPLIT, LROWS, PAIR), F32), big, big, low, low]
        + [pltpu.VMEM((GD, PAIR), F32)] * 2
        + [pltpu.VMEM((PAIR, PAIR), F32)],
        compiler_params=params(),
        name="filter_backward_lo",
        cost_estimate=cost(45),
    )(samples, grad_mixed, four, vectors, *tabs, *weights, bias)


def feed_chunks(n2, cots, c1_ref, wts, out_acc, gn_acc, gw, gc1):
    out_acc[...] = jnp.zeros_like(out_acc)
    gn_acc[...] = jnp.zeros_like(gn_acc)

    def chunk(c, _):
        rows = pl.ds(c * FC, FC)
        low, cot = n2[...].reshape(-1, D), cots[...].reshape(-1, D)
        half, part = divmod(c * FC, FF // 2)
        blocks = slice(part // wts.shape[3], (part + FC) // wts.shape[3])
        wi, wo = (wts[half, blocks, m].reshape(FC, D) for m in range(2))
        hidden = dot_nt(low, wi) + c1_ref[pl.ds(c, 1), :]
        grad = dot_nt(cot, wo)
        square = hidden * hidden
        hp = 0.5 + 0.5 * jnp.tanh(hidden * (K0 + K1 * square))
        act = hidden * hp
        grad = grad * (hp + act * (1.0 - hp) * (2.0 * K0 + 6.0 * K1 * square))
        gc1[pl.ds(c, 1), :] += jnp.sum(grad, axis=0, keepdims=True)
        act = act.astype(BF)
        grad = grad.astype(BF)
        out_acc[...] += dot(act, wo)
        gn_acc[...] += dot(grad, wi)
        gw[1, rows, :] += dot_tn(act, cot)
        gw[0, rows, :] += dot_tn(grad, low)
        return 0

    for c in range(NC):
        chunk(c, 0)


def feed_kernel(high, own_ref, live_ref, *refs):
    count = SPLIT if high else 1
    x_ref, cot_ref = refs[:2]
    fields = refs[2 : 2 + count]
    rest = refs[2 + count :]
    vec_ref, c1_ref = rest[:2]
    weights_here, weights_there = rest[2:4]
    rest = rest[4:]
    if high:
        gw_in, gc1_in, gv_in = rest[:3]
        rest = rest[3:]
    block_ref = rest[0]
    packs = rest[1 : 1 + count]
    rest = rest[1 + count :]
    keep_out = rest[0]
    if high:
        give_out = rest[1]
        rest = rest[1:]
    gc1, gv, wts, wsem, gw, sem, mixed, n2, cots, out_acc, gn_acc, fs = rest[1:]
    step = pl.program_id(0)

    side = lax.rem(own_ref[0], 2)

    @pl.when(step == 0)
    def _():
        loads = [
            pltpu.make_async_copy(weights_here, wts.at[side], wsem.at[0]),
            pltpu.make_async_copy(weights_there, wts.at[1 - side], wsem.at[1]),
        ]
        for load in loads:
            load.start()
        if high:
            load = pltpu.make_async_copy(gw_in, gw, sem)
            load.start()
            load.wait()
            gc1[...] = gc1_in[...]
            gv[...] = gv_in[...]
        else:
            gw[...] = jnp.zeros_like(gw)
            gc1[...] = jnp.zeros_like(gc1)
            gv[...] = jnp.zeros_like(gv)
        for load in loads:
            load.wait()

    own = own_ref[0]
    tall = PW if high else LH
    gain_one, shift_one = vec_ref[0:1, :], vec_ref[1:2, :]
    gain_two, shift_two = vec_ref[2:3, :], vec_ref[3:4, :]
    bias_out = vec_ref[4:5, :]

    def enter(plane, x, cot, field):
        at = pl.ds(plane * tall, tall)
        norm, _unused = normed(x)
        total = field + (norm * gain_one + shift_one) + x
        mixed[at, :] = total
        norm, _unused = normed(total)
        n2[plane] = (norm * gain_two + shift_two).astype(BF)
        cots[plane] = cot.astype(BF)

    def leave(plane):
        at = pl.ds(plane * tall, tall)
        total = mixed[at, :]
        out = total + (out_acc[at, :] + bias_out)
        norm, scale = normed(total)
        grad = gn_acc[at, :]
        cot = cots[plane].astype(F32)
        sums.append(
            tuple(jnp.sum(v, axis=0, keepdims=True) for v in (grad * norm, grad, cot))
        )
        return out.astype(BF), cot + norm_back(grad, norm, scale, gain_two)

    sums = []

    def add_sums():
        for row in range(3):
            gv[row : row + 1, :] += sum(entry[row] for entry in sums)
        sums.clear()

    if high:

        def before():
            for i in range(HB):
                for j in range(SPLIT):
                    fs[i, own ^ j] = fields[j][i]
            for i in range(HB):
                for part, field in enumerate(unpack_pair(fs.at[i])):
                    x = pad_rows(x_ref[part, i].astype(F32))
                    cot = pad_rows(cot_ref[part, i].astype(F32))
                    enter(part * HB + i, x, cot, field)

        def after():
            for i in range(HB):
                grads = []
                for part in range(2):
                    out, grad = leave(part * HB + i)
                    block_ref[part, i] = out[:OWN]
                    grads.append(grad)
                pack_pair(grads[0], grads[1], fs.at[i])
            add_sums()
            for i in range(HB):
                for j in range(SPLIT):
                    packs[j][i] = fs[i, own ^ j]

    else:
        live = live_ref[0].astype(F32)

        def before():
            for i in range(LB):
                x = pad_rows(x_ref[i].astype(F32), LH)
                cot = pad_rows(cot_ref[i].astype(F32), LH) * live
                enter(i, x, cot, fields[0][i].astype(F32))

        def after():
            for i in range(LB):
                out, grad = leave(i)
                block_ref[i] = out[:HL]
                packs[0][i] = grad.astype(BF)
            add_sums()

    before()
    feed_chunks(n2, cots, c1_ref, wts, out_acc, gn_acc, gw, gc1)
    after()

    @pl.when(step == pl.num_programs(0) - 1)
    def _():
        if not high:
            store = pltpu.make_async_copy(gw, keep_out, sem)
            store.start()
            store.wait()
        else:
            mine = lax.rem(own, 2)
            store = pltpu.make_async_copy(gw.at[mine], keep_out, sem)
            store.start()

            def low(c, _):
                rows = pl.ds(pl.multiple_of(c * FC, FC), FC)
                give_out[rows, :] = gw[1 - mine, rows, :].astype(BF)
                return 0

            lax.fori_loop(0, NC, low, 0)
            store.wait()


def feed(high, own, live, samples, cotan, fields, vectors, bias_hidden, weights, earlier):
    planes, tall = (2 * HB, PW) if high else (LB, LH)
    tokens = planes * tall
    if high:
        steps = HALF // HB
        wide, packed, packed_shape = WIDE_BLOCK, PACKED_BLOCK, PACKED
    else:
        steps = WL // LB
        wide = pl.BlockSpec((LB, HL, D), lambda i: (i, 0, 0))
        packed = pl.BlockSpec((LB, LH, D), lambda i: (i, 0, 0))
        packed_shape = (WL, LH, D)
    count = len(fields)
    return pl.pallas_call(
        functools.partial(feed_kernel, high),
        grid=(steps,),
        in_specs=[SM, SM, wide, wide]
        + [packed] * count
        + [VM, VM, ANY, ANY]
        + ([ANY, VM, VM] if high else []),
        out_specs=[wide] + [packed] * count + ([ANY, VM] if high else [ANY]) + [VM, VM],
        out_shape=[shape(samples.shape, BF)]
        + [shape(packed_shape, BF)] * count
        + ([shape((FF, D), F32), shape((FF, D), BF)] if high else [shape((2, FF, D), F32)])
        + [shape((NC, FC), F32), shape((8, D), F32)],
        scratch_shapes=[
            pltpu.VMEM((2, *weights[0].shape), BF),
            pltpu.SemaphoreType.DMA((2,)),
            pltpu.VMEM((2, FF, D), F32),
            pltpu.SemaphoreType.DMA,
            pltpu.VMEM((tokens, D), F32),
            pltpu.VMEM((planes, tall, D), BF),
            pltpu.VMEM((planes, tall, D), BF),
            pltpu.VMEM((tokens, D), F32),
            pltpu.VMEM((tokens, D), F32),
            pltpu.VMEM((HB, SPLIT, PW, PAIR), BF),
        ],
        compiler_params=params(),
        name="feed_hi" if high else "feed_lo",
        cost_estimate=cost(210 if high else 70),
    )(own, live, samples, cotan, *fields, vectors, bias_hidden, *weights, *earlier)


def eye_of(size):
    return lax.broadcasted_iota(jnp.int32, (size, size), 0) == lax.broadcasted_iota(
        jnp.int32, (size, size), 1
    )


def mul(left, right):
    return jnp.dot(left, right, precision=highest, preferred_element_type=F32)


def split_three(values):
    top = values.astype(BF)
    rest = values - top.astype(F32)
    middle = rest.astype(BF)
    return top, middle, (rest - middle.astype(F32)).astype(BF)


TILE = 256


def mul_parts(left, right_ref, parts, full, out, finish=None):
    size = right_ref.shape[0]
    rows = left.shape[0]
    tile = TILE if rows % TILE == 0 else rows

    def cut(i, _):
        at = pl.ds(pl.multiple_of(i * TILE, TILE), TILE)
        for n, part in enumerate(split_three(right_ref[at, :])):
            parts[n, at, :] = part
        return 0

    lax.fori_loop(0, size // TILE, cut, 0)

    def one(i, _):
        at = pl.ds(pl.multiple_of(i * tile, tile), tile)
        top, middle, low = split_three(left[at, :])
        total = dot(lanes(middle, top), parts[0:2].reshape(2 * size, size))
        if full:
            total = total + dot(lanes(low, middle, top), parts[...].reshape(3 * size, size))
        total = total + dot(top, parts[0])
        out[at, :] = total if finish is None else finish(at, total)
        return 0

    lax.fori_loop(0, rows // tile, one, 0)


def newton_kernel(g_ref, x_ref, y_ref, gram, poly, hold, parts, once, twice):
    size = g_ref.shape[0]
    trace = jnp.sum(jnp.where(eye_of(size), g_ref[...], 0.0), keepdims=True)
    scale = 1.0 / (jnp.sqrt(trace) + 1e-07)
    gram[...] = g_ref[...] * (scale * scale)
    y_ref[...] = x_ref[...] * scale

    def turn(full):
        def polynomial(at, square):
            rows = at.start + lax.broadcasted_iota(jnp.int32, (TILE, size), 0)
            diagonal = rows == lax.broadcasted_iota(jnp.int32, (TILE, size), 1)
            return jnp.where(diagonal, newton_a, 0.0) + newton_b * gram[at, :] + newton_c * square

        mul_parts(gram, gram, parts, full, poly, polynomial)
        mul_parts(gram, poly, parts, full, hold)
        mul_parts(y_ref, poly, parts, full, once)
        y_ref[...] = once[...]
        mul_parts(poly, hold, parts, full, gram)

    turn(True)

    def later(_, carry):
        turn(False)
        return carry

    lax.fori_loop(1, NEWTON_STEPS - 1, later, 0)
    mul_parts(y_ref, gram, parts, False, once)
    mul_parts(once, gram, parts, False, twice)
    y_ref[...] = newton_a * y_ref[...] + newton_b * once[...] + newton_c * twice[...]


def newton_one(gram, rows):
    return pl.pallas_call(
        newton_kernel,
        in_specs=[VM] * 2,
        out_specs=VM,
        out_shape=shape(rows.shape, F32),
        scratch_shapes=[pltpu.VMEM((D, D), F32)] * 3
        + [pltpu.VMEM((3, D, D), BF)]
        + [pltpu.VMEM(rows.shape, F32)] * 2,
        compiler_params=params(),
        name="newton",
        cost_estimate=cost(60),
    )(gram, rows)


SWAP = [(0, 1), (1, 0)]


def choose(first, when_first, when_second):
    return jnp.where(first, when_first, when_second)


def both_rows(first, of_first, of_second):
    keep = choose(first, of_first, of_second)
    other = lax.ppermute(choose(first, of_second, of_first), "sc", SWAP)
    return jnp.concatenate(
        [choose(first, keep, other), choose(first, other, keep)], axis=0
    )


def own_rows(first, rows):
    upper, lower = jnp.split(rows, 2, axis=0)
    keep = choose(first, upper, lower)
    other = lax.ppermute(choose(first, lower, upper), "sc", SWAP)
    return choose(first, keep, other), choose(first, other, keep)


def newton_small_kernel(x_ref, y_ref):
    y_ref[...] = newton_rows(x_ref[...])


def newton_small(values):
    return pl.pallas_call(
        newton_small_kernel,
        in_specs=[VM],
        out_specs=VM,
        out_shape=shape(values.shape, F32),
        name="newton_small",
    )(values)


def place(dp, sp):
    return (dp, sp // 2, lax.rem(sp, 2))


def greet(count):
    dp, sp = lax.axis_index("dp"), lax.axis_index("sy") * 2 + lax.axis_index("sc")
    barrier = pltpu.get_barrier_semaphore()
    for o in range(1, count):
        pl.semaphore_signal(
            barrier, inc=1, device_id=place(lax.rem(dp + o, count), sp),
            device_id_type=pl.DeviceIdType.MESH,
        )
    for j in range(1, SPLIT):
        pl.semaphore_signal(
            barrier, inc=1, device_id=place(dp, sp ^ j), device_id_type=pl.DeviceIdType.MESH
        )
    pl.semaphore_wait(barrier, count - 1 + SPLIT - 1)
    return dp, sp


def remote_copy(source, target, out_sem, in_sem, device):
    return pltpu.make_async_remote_copy(
        src_ref=source, dst_ref=target, send_sem=out_sem, recv_sem=in_sem, device_id=device,
        device_id_type=pl.DeviceIdType.MESH,
    )


def send(source, target, out_sem, in_sem, device):
    copy = remote_copy(source, target, out_sem, in_sem, device)
    copy.start()
    return copy


def spread_out(count, dp, sp, jobs):
    copies = []
    for buf, sems in jobs:
        here = buf.at[sp, dp]
        for o in range(1, count):
            to = place(lax.rem(dp + o, count), sp)
            copies.append(send(here, here, sems[0].at[o], sems[1].at[o], to))
    for copy in copies:
        copy.wait()
    copies = []
    for buf, sems in jobs:
        for j in range(1, SPLIT):
            here = buf.at[sp]
            copies.append(send(here, here, sems[2].at[j], sems[3].at[j], place(dp, sp ^ j)))
    for copy in copies:
        copy.wait()


def gather_kernel(count, vec_ref, spec_ref, vec_out, bias, lead, wu, wv, w1, buf, sbuf, *sems):
    height, cols = vec_ref.shape
    rows = spec_ref.shape[0]
    dp, sp = greet(count)
    buf[sp, dp] = jnp.zeros(buf.shape[2:], F32)
    buf[sp, dp, :height, :cols] = vec_ref[...]
    sbuf[sp, dp] = jnp.zeros(sbuf.shape[2:], BF)
    sbuf[sp, dp, :, :BS] = spec_ref[...].astype(BF)
    spread_out(count, dp, sp, [(buf, sems[:4]), (sbuf, sems[4:])])
    for ref in (wu, wv, w1):
        ref[...] = jnp.zeros_like(ref)
    for i in range(count * SPLIT):
        vec_out[:height, i * cols : (i + 1) * cols] = buf[i % SPLIT, i // SPLIT, :height, :cols]
    for g in range(SPLIT):
        cut = slice(g * GD, (g + 1) * GD)
        for layer in range(2):
            row = 9 + 2 * layer
            bias[g, layer : layer + 1, :GD] = vec_out[row : row + 1, cut]
            bias[g, layer : layer + 1, GD:] = vec_out[row + 1 : row + 2, cut]
            for part in (slice(GD), slice(GD, PAIR)):
                lead[g, layer : layer + 1, part] = vec_out[layer : layer + 1, cut]
    for i in range(count * SPLIT):
        value = sbuf[i % SPLIT, i // SPLIT][:, :BS]
        cell, off = divmod(i * rows, BS)
        layer, part, g, b = cell // 16, (cell // 8) % 2, (cell % 8) // 2, cell % 2
        re = slice(b * BS + off, b * BS + off + rows)
        im = slice(GD + b * BS + off, GD + b * BS + off + rows)
        to_re, to_im = slice(b * BS, (b + 1) * BS), slice(GD + b * BS, GD + (b + 1) * BS)
        if layer == 0 and part == 0:
            wu[g, re, to_re] = value
            wv[g, re, to_im] = value
        elif layer == 0:
            wu[g, re, to_im] = value
            wv[g, re, to_re] = -value
        elif part == 0:
            w1[g, re, to_re] = value
            w1[g, im, to_im] = value
        else:
            w1[g, re, to_im] = value
            w1[g, im, to_re] = -value


def dma_sems(*counts):
    return [pltpu.SemaphoreType.DMA((n,)) for n in counts]


def remote(number):
    return pltpu.CompilerParams(
        vmem_limit_bytes=VMEM_LIMIT, collective_id=number, has_side_effects=True
    )


def gather_small(count, vectors, spectral):
    return pl.pallas_call(
        functools.partial(gather_kernel, count),
        in_specs=[VM] * 2,
        out_specs=[VM] * 6,
        out_shape=[
            shape((16, D), F32),
            shape((SPLIT, 2, PAIR), F32),
            shape((SPLIT, 2, PAIR), F32),
            shape((SPLIT, GD, PAIR), BF),
            shape((SPLIT, GD, PAIR), BF),
            shape((SPLIT, PAIR, PAIR), BF),
        ],
        scratch_shapes=[
            pltpu.VMEM((SPLIT, count, 16, 128), F32),
            pltpu.VMEM((SPLIT, count, spectral.shape[0], 128), BF),
        ]
        + dma_sems(count, count, SPLIT, SPLIT) * 2,
        compiler_params=remote(0),
        name="gather_small",
        cost_estimate=cost(70),
    )(vectors, spectral)


def scatter_near(dp, sp, x_ref, land, sems):
    return [
        remote_copy(
            x_ref.at[:, sp ^ j], land.at[j - 1], sems[0].at[j], sems[1].at[j], place(dp, sp ^ j)
        )
        for j in range(1, SPLIT)
    ]


def scatter_far(count, dp, sp, total, land_two, sems):
    copies = []
    for o in range(1, count):
        to = lax.rem(dp + o, count)
        copies.append(
            remote_copy(
                total.at[to], land_two.at[o - 1], sems[2].at[o], sems[3].at[o], place(to, sp)
            )
        )
    return copies


def scatter_total(count, dp, total, land_two):
    result = total[dp]
    for o in range(1, count):
        result = result + land_two[o - 1]
    return result


def scatter_scratch(count, rows, width):
    return [
        pltpu.VMEM((SPLIT - 1, count, rows, width), F32),
        pltpu.VMEM((count, rows, width), F32),
        pltpu.VMEM((count, rows, width), F32),
    ] + dma_sems(SPLIT, SPLIT, count, count)


def spec_kernel(count, x_ref, out_ref, land, total, land_two, *sems):
    dp, sp = greet(count)
    copies = []
    for o in range(1, count):
        to = lax.rem(dp + o, count)
        copies.append(
            send(x_ref.at[to], land.at[o - 1], sems[0].at[o], sems[1].at[o], place(to, sp))
        )
    for copy in copies:
        copy.wait()
    value = x_ref[dp]
    for o in range(1, count):
        value = value + land[o - 1]
    total[...] = value
    copies = []
    for j in range(1, SPLIT):
        source = total.at[sp ^ j]
        copies.append(
            send(source, land_two.at[j - 1], sems[2].at[j], sems[3].at[j], place(dp, sp ^ j))
        )
    for copy in copies:
        copy.wait()
    out_ref[...] = (total[sp] + land_two[0]) + (land_two[1] + land_two[2])


def scatter_spec(count, grads):
    rows = 4 * NB * BS // (count * SPLIT)
    return pl.pallas_call(
        functools.partial(spec_kernel, count),
        in_specs=[VM],
        out_specs=VM,
        out_shape=shape((rows, BS), F32),
        scratch_shapes=[
            pltpu.VMEM((count - 1, SPLIT, rows, BS), F32),
            pltpu.VMEM((SPLIT, rows, BS), F32),
            pltpu.VMEM((SPLIT - 1, rows, BS), F32),
        ]
        + dma_sems(count, count, SPLIT, SPLIT),
        compiler_params=remote(4),
        name="scatter_spec",
        cost_estimate=cost(25),
    )(grads.reshape(count, SPLIT, rows, BS))


def newton_rows(values):
    size = 1.0 / (jnp.sqrt(jnp.sum(values * values, keepdims=True)) + 1e-07)
    values = values * size
    for _ in range(NEWTON_STEPS):
        gram = lax.dot_general(
            values, values, (((0,), (0,)), ((), ())), precision=highest, preferred_element_type=F32
        )
        once = mul(values, gram)
        values = newton_a * values + newton_b * once + newton_c * mul(once, gram)
    return values


def vectors_kernel(
    count, gv_lo, gv_hi, gv, gc1, ge_lo, ge, vec_ref, first_ref, second_ref,
    red_spec, spec_ref, moment_ref,
    new_vec, new_first, new_second, new_spec, new_moment,
    full, esum, x_ref, land, total, land_two, *sems,
):
    height, cols = vec_ref.shape
    dp, sp = greet(count)
    full[...] = jnp.zeros_like(full)
    full[0:2, :] = gv_lo[...] + gv_hi[...]
    full[2:5, :] = gv[0:3, :]
    full[5:9, :] = gc1[...]
    esum[...] = ge_lo[...]
    esum[sp] += ge[...]
    for g in range(SPLIT):
        cut = slice(g * GD, (g + 1) * GD)
        for layer in range(2):
            row = 9 + 2 * layer
            full[row : row + 1, cut] = esum[g, layer : layer + 1, :GD]
            full[row + 1 : row + 2, cut] = esum[g, layer : layer + 1, GD:]
    x_ref[...] = jnp.zeros_like(x_ref)
    for i in range(count * SPLIT):
        x_ref[i // SPLIT, i % SPLIT, :, :cols] = full[:, i * cols : (i + 1) * cols]
    copies = scatter_near(dp, sp, x_ref, land, sems)
    for copy in copies:
        copy.start()
    moment = momentum * moment_ref[...] + red_spec[...]
    new_moment[...] = moment
    push = red_spec[...] + momentum * moment
    if red_spec.shape[0] == BS:
        new_spec[...] = spec_ref[...] * (1.0 - muon_rate * decay) - muon_rate * newton_rows(push)
    else:
        new_spec[...] = push
    for copy in copies:
        copy.wait()
    total[...] = (x_ref[:, sp] + land[0]) + (land[1] + land[2])
    copies = scatter_far(count, dp, sp, total, land_two, sems)
    for copy in copies:
        copy.start()
    for copy in copies:
        copy.wait()
    grad = scatter_total(count, dp, total, land_two)[:height, :cols]
    first = beta_one * first_ref[...] + (1.0 - beta_one) * grad
    second = beta_two * second_ref[...] + (1.0 - beta_two) * grad * grad
    new_first[...] = first
    new_second[...] = second
    first_hat = first / (1.0 - beta_one**STEP)
    second_hat = second / (1.0 - beta_two**STEP)
    new_vec[...] = vec_ref[...] * (1.0 - adam_rate * decay) - adam_rate * first_hat / (
        jnp.sqrt(second_hat) + 1e-08
    )


def update_small(count, pieces, vectors, first, second, red_spec, spectral, moment):
    return pl.pallas_call(
        functools.partial(vectors_kernel, count),
        in_specs=[VM] * 12,
        out_specs=[VM] * 5,
        out_shape=[shape(vectors.shape, F32)] * 3 + [shape(red_spec.shape, F32)] * 2,
        scratch_shapes=[
            pltpu.VMEM((16, D), F32),
            pltpu.VMEM((SPLIT, 2, PAIR), F32),
            pltpu.VMEM((count, SPLIT, 16, 128), F32),
        ]
        + scatter_scratch(count, 16, 128),
        compiler_params=remote(2),
        name="update_small",
        cost_estimate=cost(15),
    )(*pieces, vectors, first, second, red_spec, spectral, moment)


def norm_back_kernel(own_ref, x_ref, m0, m1, m2, m3, f0, f1, f2, f3, vec_ref, grad_ref, gvec, fs, ms):
    @pl.when(pl.program_id(0) == 0)
    def _():
        gvec[...] = jnp.zeros_like(gvec)

    own = own_ref[0]
    gain = vec_ref[0:1, :]

    for i in range(HB):
        for j, (m, f) in enumerate(((m0, f0), (m1, f1), (m2, f2), (m3, f3))):
            ms[i, own ^ j] = m[i]
            fs[i, own ^ j] = f[i]
    sums = []
    for i in range(HB):
        for part, (direct, field) in enumerate(zip(unpack_pair(ms.at[i]), unpack_pair(fs.at[i]))):
            direct, field = direct[:OWN], field[:OWN]
            norm, scale = normed(x_ref[part, i].astype(F32))
            grad = field + direct
            sums.append((jnp.sum(grad * norm, axis=0, keepdims=True), jnp.sum(grad, axis=0, keepdims=True)))
            value = direct + norm_back(grad, norm, scale, gain)
            for c in range(6):
                at = pl.ds(i * (6 * OWN) + c, OWN, stride=6)
                grad_ref[part, at, 0, :] = value[:, c * 128 : (c + 1) * 128]
    gvec[0:1, :] += sum(a for a, b in sums)
    gvec[1:2, :] += sum(b for a, b in sums)


def norm_backward(own, samples, direct, fields, vectors):
    return pl.pallas_call(
        norm_back_kernel,
        grid=(HALF // HB,),
        in_specs=[SM, WIDE_BLOCK] + [PACKED_BLOCK] * (2 * SPLIT) + [VM],
        out_specs=[pl.BlockSpec((2, HB * OWN * 6, 1, 128), lambda i: (0, i, 0, 0)), VM],
        out_shape=[shape((2, HALF * OWN * 6, 1, 128), F32), shape((2, D), F32)],
        scratch_shapes=[pltpu.VMEM((HB, SPLIT, PW, PAIR), BF)] * 2,
        compiler_params=params(),
        name="norm_backward",
        cost_estimate=cost(30),
    )(own, samples, *direct, *fields, vectors)


def reduce_kernel(
    bits, keep, give, moment, new_moment, direction, gram,
    acc, land, red, load_sem, give_sems, *scratch,
):
    half = moment.shape[0] // 2
    dp, sy, sc = (lax.axis_index(name) for name in ("dp", "sy", "sc"))
    swap = (dp, sy, 1 - sc)
    partners = [(dp, 1 - sy, sc)] + [(dp ^ (1 << b), sy, sc) for b in range(bits - 1)]
    mine = [sy] + [lax.rem(dp // (1 << b), 2) for b in range(bits - 1)]
    barrier = pltpu.get_barrier_semaphore()
    for device in [swap] + partners:
        pl.semaphore_signal(barrier, inc=1, device_id=device, device_id_type=pl.DeviceIdType.MESH)
    load = pltpu.make_async_copy(keep, acc, load_sem)
    load.start()
    pl.semaphore_wait(barrier, bits + 1)
    halves = [
        send(give.at[t], land.at[t], give_sems.at[2 * t], give_sems.at[2 * t + 1], swap)
        for t in range(2)
    ]
    load.wait()

    def join_half(t):
        halves[t].wait()

        def join(o, _):
            acc[t, o] = acc[t, o] + land[t, o].astype(F32)
            return 0

        lax.fori_loop(0, 2**bits, join, 0)

    streams = []
    for t in range(2):
        order = list(range(1, bits)) + [0]
        if t == 1:
            order[0], order[1] = order[1], order[0]
        streams.append(order)
    left = [list(range(bits)), list(range(bits))]
    current = [lambda block, t=t: acc.at[t, block] for t in range(2)]
    for stage in range(bits):
        count = 2 ** (bits - 1 - stage)
        copies = []
        for t in range(2):
            outgoing, incoming, _sum, sems = scratch[(stage * 2 + t) * 4 : (stage * 2 + t) * 4 + 4]
            bit = streams[t][stage]
            step = 1 << left[t].index(bit)
            side = mine[bit]
            if stage == 0:
                join_half(t)

            def cast(o, _, t=t, outgoing=outgoing, step=step, side=side):
                block = (o // step) * (2 * step) + (1 - side) * step + lax.rem(o, step)
                outgoing[o] = current[t](block)[...].astype(BF)
                return 0

            lax.fori_loop(0, count, cast, 0)
            copies.append(send(outgoing, incoming, sems.at[0], sems.at[1], partners[bit]))
        following = []
        for t in range(2):
            outgoing, incoming, total, sems = scratch[(stage * 2 + t) * 4 : (stage * 2 + t) * 4 + 4]
            bit = streams[t][stage]
            step = 1 << left[t].index(bit)
            side = mine[bit]
            left[t].remove(bit)
            copies[t].wait()

            def add(o, _, t=t, incoming=incoming, total=total, step=step, side=side):
                block = (o // step) * (2 * step) + side * step + lax.rem(o, step)
                total[o] = current[t](block)[...] + incoming[o].astype(F32)
                return 0

            lax.fori_loop(0, count, add, 0)
            following.append(lambda block, total=total: total.at[block])
        current = following
    for t in range(2):
        red[t * half : (t + 1) * half, :] = current[t](0)[...]
    new = momentum * moment[...] + red[...]
    new_moment[...] = new
    pushed = red[...] + momentum * new
    direction[...] = pushed
    top, middle, low = split_three(pushed)
    gram[...] = (
        (dot_tn(middle, middle) + dot_tn(top, low) + dot_tn(low, top))
        + (dot_tn(top, middle) + dot_tn(middle, top))
    ) + dot_tn(top, top)


def reduce_feed(count, keep, give, moment):
    rows = moment.shape[0]
    blocks = FF // rows
    bits = blocks.bit_length() - 1
    whole = (2, blocks, rows // 2, D)
    scratch = []
    for stage in range(bits):
        for _ in range(2):
            part = (2 ** (bits - 1 - stage), rows // 2, D)
            scratch += [pltpu.VMEM(part, BF), pltpu.VMEM(part, BF), pltpu.VMEM(part, F32)] + dma_sems(2)
    return pl.pallas_call(
        functools.partial(reduce_kernel, bits),
        in_specs=[ANY, ANY, VM],
        out_specs=[VM] * 3,
        out_shape=[shape((rows, D), F32)] * 2 + [shape((D, D), F32)],
        scratch_shapes=[
            pltpu.VMEM(whole, F32),
            pltpu.VMEM(whole, BF),
            pltpu.VMEM((rows, D), F32),
            pltpu.SemaphoreType.DMA,
        ]
        + dma_sems(4)
        + scratch,
        compiler_params=pltpu.CompilerParams(
            vmem_limit_bytes=VMEM_LIMIT, collective_id=1, has_side_effects=True
        ),
        name="reduce_feed",
        cost_estimate=cost(80),
    )(keep.reshape(whole), give.reshape(whole), moment)


def after(values, earlier):
    return lax.optimization_barrier((values, earlier))[0]


def body(
    count, samples_hi, samples_lo, cotan_hi, cotan_lo, live_slots, spectral_w, vectors, weight_in,
    weight_out, moment_spec, moment_in, moment_out, adam_first, adam_second,
):
    axes = ("dp", *SP)
    chips = ("dp", "sy")
    sp = lax.axis_index(SP)
    first = lax.axis_index("sc") == 0
    own = sp.astype(jnp.int32).reshape(1)
    wide, tall, wide_lo, tall_lo = (t.astype(BF) for t in tables())
    tabs = (wide, np.swapaxes(wide, 1, 2), tall, tall.T)
    tabs_lo = (wide_lo, wide_lo.T, tall_lo, tall_lo.T)
    tabs = tuple(jnp.asarray(np.ascontiguousarray(t)) for t in tabs)
    tabs_lo = tuple(jnp.asarray(np.ascontiguousarray(t)) for t in tabs_lo)

    own_width = weight_in.shape[1]
    split_hi = samples_hi.reshape(2, HALF, OWN, D)
    split_cot = cotan_hi.reshape(2, HALF, OWN, D)
    one_lo = samples_lo.reshape(HL, WL, D).transpose(1, 0, 2)
    one_cot = cotan_lo.reshape(HL, WL, D).transpose(1, 0, 2)

    moment = both_rows(first, moment_in.T, moment_out)
    piece = jnp.stack([weight_in.T.astype(BF), weight_out.astype(BF)])
    here = lax.all_gather(piece, chips, axis=0)
    packed = norm_packed(own, split_hi)
    vec, bias, lead, *weights = gather_small(count, *after((vectors, spectral_w), packed))
    bias_hidden = vec[5:9].reshape(2 * count, 2, own_width).transpose(1, 0, 2).reshape(NC, FC)
    slabs = after(exchange(packed), vec)
    slabs, here = after((slabs, here), (slabs[1], here))
    feed_weights = (here, lax.ppermute(here, "sc", SWAP))
    fields, four = filter_forward(own, slabs, tabs, weights, bias, lead)
    lo_after = after(one_lo, fields)
    fields = exchange(fields)
    field_lo, four_lo = filter_forward_lo(lo_after, vec, tabs_lo, weights, bias)
    block_lo, gm_lo, gw, gc1, gv = feed(
        False, own, live_slots, one_lo, one_cot, [field_lo], vec, bias_hidden, feed_weights, ()
    )
    block_hi, p0, p1, p2, p3, keep, give, gc1, gv = feed(
        True, own, live_slots, split_hi, split_cot, fields, vec, bias_hidden, feed_weights,
        (gw, gc1, gv),
    )
    packs = [p0, p1, p2, p3]
    grad_slabs = exchange(packs)
    new_moment, direction, gram = reduce_feed(count, keep, give, moment)
    gram = lax.psum(gram, chips)
    gm_lo, grad_slabs = after((gm_lo, grad_slabs), (direction, grad_slabs[1]))
    grad_lo, gspec, ge_lo, gv_lo = filter_backward_lo(
        one_lo, gm_lo, four_lo, vec, tabs_lo, weights, bias
    )
    back, gspec, ge = filter_backward(own, grad_slabs, four, tabs, weights, bias, gspec)
    red_spec = scatter_spec(count, gspec)
    back, gram = after((back, gram), red_spec)
    back = exchange(back)
    orth = newton_one(gram, direction)
    back = after(back, orth)
    grad_hi, gv_hi = norm_backward(own, split_hi, packs, back, vec)
    gc1 = gc1.reshape(2, 2 * count, own_width).transpose(1, 0, 2).reshape(4, D)
    new_vectors, new_adam_first, new_adam_second, new_spectral, new_moment_spec = update_small(
        count, (gv_lo, gv_hi, gv, gc1, ge_lo, ge), vectors, adam_first, adam_second,
        red_spec, spectral_w, moment_spec,
    )
    new_moment_in, new_moment_out = own_rows(first, new_moment)
    orth_in, orth_out = own_rows(first, orth)

    keep_share = 1.0 - muon_rate * decay
    new_weight_in = weight_in * keep_share - muon_rate * orth_in.T
    new_weight_out = weight_out * keep_share - muon_rate * math.sqrt(max(1.0, FF / D)) * orth_out
    rows = moment_spec.shape[0]
    if rows != BS:
        gathered = lax.all_gather(new_spectral, SP, axis=0, tiled=True)
        orth_spec = lax.dynamic_slice_in_dim(newton_small(gathered), sp * rows, rows, 0)
        new_spectral = spectral_w * keep_share - muon_rate * orth_spec
    return (
        block_hi.reshape(samples_hi.shape),
        block_lo.transpose(1, 0, 2).reshape(samples_lo.shape),
        grad_hi.reshape(samples_hi.shape),
        grad_lo.reshape(samples_lo.shape),
        new_spectral,
        new_weight_in,
        new_weight_out,
        new_moment_spec,
        new_moment_in.T,
        new_moment_out,
        new_vectors,
        new_adam_first,
        new_adam_second,
    )


def solution(mesh):
    count = mesh.shape["dp"]
    fine = jax.sharding.Mesh(mesh.devices.reshape(count, 2, 2), ("dp", *SP))
    both = ("dp", *SP)
    hi = P("dp", None, SP, None)
    lo = P(both, None, None, None)
    rows = P(both, None)
    cols = P(None, both)
    return jax.shard_map(
        functools.partial(body, count),
        mesh=fine,
        in_specs=(hi, lo, hi, lo, P(both), rows, cols, cols, rows, rows, cols, rows, cols, cols),
        out_specs=(hi, lo, hi, lo, rows, cols, rows, rows, cols, rows, cols, cols, cols),
        check_vma=False,
    )
```

```python
import functools
import math

import jax
import jax.numpy as jnp
import numpy as np
from jax import lax
from jax.experimental import pallas as pl
from jax.experimental.pallas import tpu as pltpu
from jax.sharding import PartitionSpec as P

D = 768
FF = 3072
NB = 8
BS = 96
H = 90
W = 180
HL = 23
WL = 45
STEP = 10
NEWTON_STEPS = 5

F32 = jnp.float32
BF = jnp.bfloat16
highest = lax.Precision.HIGHEST
epsilon = 1e-06
shrink_level = 0.01
shrink_sharp = 10.0
momentum = 0.95
newton_a = 3.4445
newton_b = -4.775
newton_c = 2.0315
muon_rate = 0.5
adam_rate = 0.3
decay = 0.01
beta_one = 0.9
beta_two = 0.999

K0 = math.sqrt(2.0 / math.pi)
K1 = K0 * 0.044715

SPLIT = 4
GD = D // SPLIT
PAIR = 2 * GD
HALF = H // 2
OWN = W // SPLIT
PW = 48
PM = 96
KF = W // 2 + 1
KP = 96
KG = 7
GROUPS = KF // KG
ROWS = KG * PM
LH = 24
LK = HL // 2 + 1
LROWS = LK * PW
HB = 5
LB = 15
FC = 768
NC = FF // FC
VMEM_LIMIT = 60 * 2**20
UNROLL = 9
PITCH = 56


def wave(length, rows, cols):
    phase = np.outer(rows, cols) % length
    angle = phase * (2.0 * math.pi / length)
    factor = 1.0 / math.sqrt(length)
    return np.cos(angle) * factor, np.sin(angle) * factor


def tables():
    wide = np.zeros((SPLIT, 2 * KP, SPLIT * PW))
    for s in range(SPLIT):
        for j in range(SPLIT):
            cols = (s ^ j) * OWN + np.arange(OWN)
            c, d = wave(W, np.arange(KF), cols)
            wide[s, :KF, j * PW : j * PW + OWN] = c
            wide[s, KP : KP + KF, j * PW : j * PW + OWN] = -d
    tall = np.zeros((2 * PM, 2 * PM))
    for part in range(2):
        c, d = wave(H, np.arange(H), part * HALF + np.arange(HALF))
        re, im = part * PW, PM + part * PW
        tall[:H, re : re + HALF] = c
        tall[:H, im : im + HALF] = d
        tall[PM : PM + H, re : re + HALF] = -d
        tall[PM : PM + H, im : im + HALF] = c
    wide_lo = np.zeros((2 * LK, LH))
    c, d = wave(HL, np.arange(LK), np.arange(HL))
    wide_lo[:LK, :HL] = c
    wide_lo[LK:, :HL] = -d
    tall_lo = np.zeros((2 * PW, 2 * PW))
    c, d = wave(WL, np.arange(WL), np.arange(WL))
    tall_lo[:WL, :WL] = c
    tall_lo[:WL, PW : PW + WL] = d
    tall_lo[PW : PW + WL, :WL] = -d
    tall_lo[PW : PW + WL, PW : PW + WL] = c
    return wide, tall, wide_lo, tall_lo


def loop(count, unroll, one):
    def some(i, carry):
        for n in range(unroll):
            one(i * unroll + n)
        return carry

    lax.fori_loop(0, count // unroll, some, 0)


def dot(left, right):
    return jnp.dot(left, right, preferred_element_type=F32)


def dot_nt(left, right):
    return lax.dot_general(left, right, (((1,), (1,)), ((), ())), preferred_element_type=F32)


def dot_tn(left, right):
    return lax.dot_general(left, right, (((0,), (0,)), ((), ())), preferred_element_type=F32)


def normed(values):
    center = values - jnp.mean(values, axis=-1, keepdims=True)
    scale = lax.rsqrt(jnp.mean(center * center, axis=-1, keepdims=True) + epsilon)
    return center * scale, scale


def norm_back(grad, norm, scale, gain):
    pushed = grad * gain
    return scale * (
        pushed
        - jnp.mean(pushed, axis=-1, keepdims=True)
        - norm * jnp.mean(pushed * norm, axis=-1, keepdims=True)
    )


def pad_rows(values, rows=PW):
    return jnp.concatenate(
        [values, jnp.zeros((rows - values.shape[0], values.shape[1]), values.dtype)], axis=0
    )


def lanes(*pieces):
    return jnp.concatenate(pieces, axis=1)


def unpack_pair(fs):
    pieces = [fs[g].astype(F32) for g in range(SPLIT)]
    return (
        lanes(*[p[:, :GD] for p in pieces]),
        lanes(*[p[:, GD:] for p in pieces]),
    )


def pack_pair(row_a, row_b, fs):
    for g in range(SPLIT):
        cut = slice(g * GD, (g + 1) * GD)
        fs[g] = lanes(row_a[:, cut], row_b[:, cut]).astype(BF)


SP = ("sy", "sc")
VM = pl.BlockSpec(memory_space=pltpu.VMEM)
SM = pl.BlockSpec(memory_space=pltpu.SMEM)
ANY = pl.BlockSpec(memory_space=pl.ANY)


def params():
    return pltpu.CompilerParams(vmem_limit_bytes=VMEM_LIMIT)


def cost(us):
    return pl.CostEstimate(flops=us * 10**9, bytes_accessed=us * 10**6, transcendentals=0)


def shape(dims, kind):
    return jax.ShapeDtypeStruct(dims, kind)


PACKED = (HALF, PW, PAIR)
PACKED_BLOCK = pl.BlockSpec((HB, PW, PAIR), lambda i: (i, 0, 0))
WIDE_BLOCK = pl.BlockSpec((2, HB, OWN, D), lambda i: (0, i, 0, 0))


def pack_kernel(own_ref, x_ref, o0, o1, o2, o3, fs):
    own = own_ref[0]

    for i in range(HB):
        rows = []
        for part in range(2):
            norm, _unused = normed(x_ref[part, i].astype(F32))
            rows.append(pad_rows(norm))
        pack_pair(rows[0], rows[1], fs.at[i])
    for i in range(HB):
        for j, out in enumerate((o0, o1, o2, o3)):
            out[i] = fs[i, own ^ j]


def norm_packed(own, samples):
    return pl.pallas_call(
        pack_kernel,
        grid=(HALF // HB,),
        in_specs=[SM, WIDE_BLOCK],
        out_specs=[PACKED_BLOCK] * SPLIT,
        out_shape=[shape(PACKED, BF)] * SPLIT,
        scratch_shapes=[pltpu.VMEM((HB, SPLIT, PW, PAIR), BF)],
        compiler_params=params(),
        name="norm_pack",
        cost_estimate=cost(16),
    )(own, samples)


def exchange(slabs):
    moved = [slabs[0]]
    for j in range(1, SPLIT):
        moved.append(lax.ppermute(slabs[j], SP, [(i, i ^ j) for i in range(SPLIT)]))
    return moved


def to_freq_wide(slabs, table, space, lead=None):
    def one(i):
        rows = jnp.concatenate([slab[i] for slab in slabs], axis=0)
        if lead is not None:
            rows = (rows.astype(F32) * lead[0:1, :] + lead[1:2, :]).astype(BF)
        area = dot(table[...], rows)
        for c in range(3):
            space[c, pl.ds(i, 2 * KP, stride=PITCH), :] = area[:, c * 128 : (c + 1) * 128]

    loop(HALF, UNROLL, one)


def to_freq_tall(k, table, space):
    re = lanes(*[space[c, pl.ds(pl.multiple_of(k * PITCH, 8), PW), :] for c in range(3)])
    im = lanes(*[space[c, pl.ds(pl.multiple_of((KP + k) * PITCH, 8), PW), :] for c in range(3)])
    rows = jnp.concatenate([re[:, :GD], re[:, GD:], im[:, :GD], im[:, GD:]], axis=0)
    return dot(table[...], rows.astype(BF))


def to_space_tall(k, table, four, space):
    back = dot(table[...], four)
    for part in range(2):
        base = part * PM
        packed = lanes(back[base : base + PW], back[base + PW : base + PM])
        at = pl.ds(pl.multiple_of((part * KP + k) * PITCH, 8), PW)
        for c in range(3):
            space[c, at, :] = packed[:, c * 128 : (c + 1) * 128]


def to_space_wide(table, space, outs):
    def one(i):
        rows = lanes(*[space[c, pl.ds(i, 2 * KP, stride=PITCH), :] for c in range(3)])
        field = dot(table[...], rows.astype(BF)).astype(BF)
        for j, out in enumerate(outs):
            out[i] = field[j * PW : (j + 1) * PW]

    loop(HALF, UNROLL, one)


def clear_pads(space, used, count):
    for c in range(space.shape[0]):
        for row in range(used, PW):
            space[c, pl.ds(row, count, stride=PITCH), :] = jnp.zeros((count, 128), F32)


def keep_minus(row, width, first, last):
    at = row + lax.broadcasted_iota(jnp.int32, (width, 1), 0)
    return jnp.where((at >= first) & (at < last), 1.0, 0.0).astype(F32)


def mlp_forward(fre, fim, wu, wv, w1, bias, us, vs, actp, actm, put, base, first, last, chunk):
    rows = us.shape[0]
    cuts = [slice(i * chunk, (i + 1) * chunk) for i in range(rows // chunk)]
    for at in cuts:
        us[at, :] = dot(fre[at, :], wu)
        vs[at, :] = dot(fim[at, :], wv)
    b0, b1 = bias[0:1, :], bias[1:2, :]

    def act(i, _):
        at = slice(i * chunk, (i + 1) * chunk)
        u = us[at, :] + b0
        v = vs[at, :]
        for ref, value in ((actp, u + v), (actm, u - v)):
            t = jnp.tanh(value * (K0 + K1 * (value * value)))
            ref[at, :] = (value * (0.5 + 0.5 * t)).astype(BF)
        return 0

    for i in range(rows // chunk):
        act(i, 0)
    for at in cuts:
        us[at, :] = dot(actp[at, :], w1)
        vs[at, :] = dot(actm[at, :], w1)

    def shrunk(i, _):
        at = slice(i * chunk, (i + 1) * chunk)
        p = us[at, :] + b1
        m = vs[at, :] + b1
        p = p - shrink_level * jnp.tanh(shrink_sharp * p)
        m = (m - shrink_level * jnp.tanh(shrink_sharp * m)) * keep_minus(
            base + i * chunk, chunk, first, last
        )
        put(at, (p[:, :GD] + m[:, :GD]).astype(BF), (p[:, GD:] - m[:, GD:]).astype(BF))
        return 0

    for i in range(rows // chunk):
        shrunk(i, 0)


def mlp_backward(
    fre, fim, gs, wu, wv, w1, bias, us, vs, actp, actm, dp, dm, gsp, gsm, sums, put,
    gwu, gwv, gw1, ge, base, first, last, chunk,
):
    rows = us.shape[0]
    us[...] = dot(fre, wu)
    vs[...] = dot(fim, wv)
    b0, b1 = bias[0:1, :], bias[1:2, :]
    sign = jnp.where(lax.broadcasted_iota(jnp.int32, (1, PAIR), 1) < GD, 1.0, -1.0).astype(F32)

    def act(i, _):
        at = slice(i * chunk, (i + 1) * chunk)
        u = us[at, :] + b0
        v = vs[at, :]
        for ref, slope, value in ((actp, dp, u + v), (actm, dm, u - v)):
            square = value * value
            hp = 0.5 + 0.5 * jnp.tanh(value * (K0 + K1 * square))
            on = value * hp
            ref[at, :] = on.astype(BF)
            slope[at, :] = hp + on * (1.0 - hp) * (2.0 * K0 + 6.0 * K1 * square)
        return 0

    for i in range(rows // chunk):
        act(i, 0)
    us[...] = dot(actp[...], w1)
    vs[...] = dot(actm[...], w1)

    def second(i, total):
        at = slice(i * chunk, (i + 1) * chunk)
        grad = gs[at, :]
        tp = jnp.tanh(shrink_sharp * (us[at, :] + b1))
        tm = jnp.tanh(shrink_sharp * (vs[at, :] + b1))
        flat = 1.0 - shrink_level * shrink_sharp
        bend = shrink_level * shrink_sharp
        p = grad * (flat + bend * (tp * tp))
        m = (grad * (sign * keep_minus(base + i * chunk, chunk, first, last))) * (
            flat + bend * (tm * tm)
        )
        gsp[at, :] = p.astype(BF)
        gsm[at, :] = m.astype(BF)
        return total + jnp.sum(p + m, axis=0, keepdims=True)

    total = jnp.zeros((1, PAIR), F32)
    for i in range(rows // chunk):
        total = second(i, total)
    ge[1:2, :] += total
    us[...] = dot_nt(gsp[...], w1)
    vs[...] = dot_nt(gsm[...], w1)
    gw1[...] += dot_tn(actp[...], gsp[...]) + dot_tn(actm[...], gsm[...])

    def first_grad(i, total):
        at = slice(i * chunk, (i + 1) * chunk)
        p = us[at, :] * dp[at, :]
        m = vs[at, :] * dm[at, :]
        both = p + m
        gsp[at, :] = both.astype(BF)
        gsm[at, :] = (p - m).astype(BF)
        return total + jnp.sum(both, axis=0, keepdims=True)

    total = jnp.zeros((1, PAIR), F32)
    for i in range(rows // chunk):
        total = first_grad(i, total)
    ge[0:1, :] += total
    gwu[...] += dot_tn(fre, gsp[...])
    gwv[...] += dot_tn(fim, gsm[...])
    put(dot_nt(gsp[...], wu).astype(BF), dot_nt(gsm[...], wv).astype(BF))


def block_grads(gwu, gwv, gw1):
    cells = {}
    for b in range(2):
        r = slice(b * BS, (b + 1) * BS)
        i = slice(GD + b * BS, GD + (b + 1) * BS)
        cells[0, 0, b] = gwu[r, r] + gwv[r, i]
        cells[0, 1, b] = gwu[r, i] - gwv[r, r]
        cells[1, 0, b] = gw1[r, r] + gw1[i, i]
        cells[1, 1, b] = gw1[r, i] - gw1[i, r]
    return cells


def filter_kernel(
    own_ref, x0, x1, x2, x3, tw, twt, th, tht, wu, wv, w1, bias, lead,
    y0, y1, y2, y3, four, space, us, vs, actp, actm, zr, zi,
):
    own = own_ref[0]
    clear_pads(space, HALF, 2 * KP)
    to_freq_wide((x0, x1, x2, x3), tw.at[own], space, lead.at[own])

    def group(g, _):
        for n in range(KG):
            rows = to_freq_tall(g * KG + n, th, space).astype(BF)
            four[g, 0, n * PM : (n + 1) * PM, :] = rows[:PM]
            four[g, 1, n * PM : (n + 1) * PM, :] = rows[PM:]

        def put(at, re, im):
            zr[at, :] = re
            zi[at, :] = im

        mlp_forward(
            four[g, 0], four[g, 1], wu[own], wv[own], w1[own], bias.at[own], us, vs, actp, actm, put,
            g * ROWS, PM, (KF - 1) * PM, ROWS // 3,
        )
        for n in range(KG):
            at = slice(n * PM, (n + 1) * PM)
            to_space_tall(
                g * KG + n, tht, jnp.concatenate([zr[at, :], zi[at, :]], axis=0), space
            )
        return 0

    lax.fori_loop(0, GROUPS, group, 0)
    to_space_wide(twt.at[own], space, (y0, y1, y2, y3))


def filter_scratch(rows, wide):
    big = pltpu.VMEM((rows, PAIR), F32)
    low = pltpu.VMEM((rows, PAIR), BF)
    part = pltpu.VMEM((rows, GD), BF)
    return big, low, part


def filter_forward(own, slabs, tabs, weights, bias, lead):
    big, low, part = filter_scratch(ROWS, None)
    outs = pl.pallas_call(
        filter_kernel,
        in_specs=[SM] + [VM] * 13,
        out_specs=[VM] * 5,
        out_shape=[shape(PACKED, BF)] * SPLIT + [shape((GROUPS, 2, ROWS, GD), BF)],
        scratch_shapes=[pltpu.VMEM((3, 2 * KP * PITCH, 128), F32), big, big, low, low, part, part],
        compiler_params=params(),
        name="filter_forward",
        cost_estimate=cost(95),
    )(own, *slabs, *tabs, *weights, bias, lead)
    return outs[:SPLIT], outs[SPLIT]


def filter_back_kernel(
    own_ref, x0, x1, x2, x3, four, tw, twt, th, tht, wu, wv, w1, bias, grads_in,
    y0, y1, y2, y3, grads, ge,
    space, us, vs, actp, actm, zr, zi, gs, dp, dm, gsp, gsm, gwu, gwv, gw1,
):
    own = own_ref[0]
    clear_pads(space, HALF, 2 * KP)
    gwu[...] = jnp.zeros_like(gwu)
    gwv[...] = jnp.zeros_like(gwv)
    gw1[...] = jnp.zeros_like(gw1)
    ge[...] = jnp.zeros_like(ge)
    to_freq_wide((x0, x1, x2, x3), tw.at[own], space)

    def group(g, _):
        for n in range(KG):
            rows = to_freq_tall(g * KG + n, th, space)
            gs[n * PM : (n + 1) * PM, :] = lanes(rows[:PM], rows[PM:])

        def put(re, im):
            zr[...] = re
            zi[...] = im

        mlp_backward(
            four[g, 0], four[g, 1], gs, wu[own], wv[own], w1[own], bias.at[own], us, vs, actp, actm, dp, dm,
            gsp, gsm, None, put, gwu, gwv, gw1, ge, g * ROWS, PM, (KF - 1) * PM, ROWS // 2,
        )
        for n in range(KG):
            at = slice(n * PM, (n + 1) * PM)
            to_space_tall(
                g * KG + n, tht, jnp.concatenate([zr[at, :], zi[at, :]], axis=0), space
            )
        return 0

    lax.fori_loop(0, GROUPS, group, 0)
    grads[...] = grads_in[...]
    for (layer, part, b), value in block_grads(gwu, gwv, gw1).items():
        grads[(2 * layer + part) * NB + 2 * own + b] += value
    to_space_wide(twt.at[own], space, (y0, y1, y2, y3))


def filter_backward(own, slabs, four, tabs, weights, bias, grads_in):
    big, low, part = filter_scratch(ROWS, None)
    outs = pl.pallas_call(
        filter_back_kernel,
        in_specs=[SM] + [VM] * 14,
        out_specs=[VM] * 6,
        out_shape=[shape(PACKED, BF)] * SPLIT
        + [shape((4 * NB, BS, BS), F32), shape((2, PAIR), F32)],
        scratch_shapes=[pltpu.VMEM((3, 2 * KP * PITCH, 128), F32), big, big, low, low, part, part]
        + [big, big, big, low, low]
        + [pltpu.VMEM((GD, PAIR), F32)] * 2
        + [pltpu.VMEM((PAIR, PAIR), F32)],
        compiler_params=params(),
        name="filter_backward",
        cost_estimate=cost(125),
    )(own, *slabs, four, *tabs, *weights, bias, grads_in)
    return outs[:SPLIT], outs[SPLIT], outs[SPLIT + 1]


def lo_freq_wide(i, rows, table, space):
    area = dot(table[...], rows)
    for c in range(6):
        space[c, pl.ds(i, 2 * LK, stride=PITCH), :] = area[:, c * 128 : (c + 1) * 128]


def lo_freq_tall(k, table, space):
    parts = []
    for base in (0, LK):
        at = pl.ds(pl.multiple_of((base + k) * PITCH, 8), PW)
        parts.append(lanes(*[space[c, at, :] for c in range(6)]))
    rows = dot(table[...], jnp.concatenate(parts, axis=0).astype(BF))
    return rows[:PW], rows[PW:]


def lo_space_tall(k, table, re, im, space):
    back = dot(table[...], jnp.concatenate([re, im], axis=0).astype(BF))
    for part, base in enumerate((0, LK)):
        at = pl.ds(pl.multiple_of((base + k) * PITCH, 8), PW)
        for c in range(6):
            space[c, at, :] = back[part * PW : (part + 1) * PW, c * 128 : (c + 1) * 128]


def lo_space_wide(i, table, space):
    rows = lanes(*[space[c, pl.ds(i, 2 * LK, stride=PITCH), :] for c in range(6)])
    return dot(table[...], rows.astype(BF))


def filter_lo_kernel(
    x_ref, vec_ref, tw, twt, th, tht, wu, wv, w1, bias, y_ref, four,
    space, us, vs, actp, actm, zr, zi,
):
    clear_pads(space, WL, 2 * LK)
    gain, shift = vec_ref[0:1, :], vec_ref[1:2, :]

    def wide(i):
        norm, _unused = normed(x_ref[i].astype(F32))
        lo_freq_wide(i, pad_rows(norm * gain + shift, LH).astype(BF), tw, space)

    loop(WL, UNROLL, wide)

    def tall(k):
        re, im = lo_freq_tall(k, th, space)
        at = pl.ds(pl.multiple_of(k * PW, PW), PW)
        for g in range(SPLIT):
            cut = slice(g * GD, (g + 1) * GD)
            four[g, 0, at, :] = re[:, cut].astype(BF)
            four[g, 1, at, :] = im[:, cut].astype(BF)

    loop(LK, 3, tall)

    def group(g, _):
        def put(at, re, im):
            zr[g, at, :] = re
            zi[g, at, :] = im

        mlp_forward(
            four[g, 0], four[g, 1], wu[g], wv[g], w1[g], bias.at[g], us, vs, actp, actm, put,
            0, PW, LROWS, LROWS // 3,
        )
        return 0

    lax.fori_loop(0, SPLIT, group, 0)

    def back(k):
        at = pl.ds(pl.multiple_of(k * PW, PW), PW)
        re = lanes(*[zr[g, at, :].astype(F32) for g in range(SPLIT)])
        im = lanes(*[zi[g, at, :].astype(F32) for g in range(SPLIT)])
        lo_space_tall(k, tht, re, im, space)

    loop(LK, 3, back)

    def last(i):
        y_ref[i] = lo_space_wide(i, twt, space).astype(BF)

    loop(WL, UNROLL, last)


def lo_scratch():
    big, low, _ = filter_scratch(LROWS, None)
    part = pltpu.VMEM((SPLIT, LROWS, GD), BF)
    return [pltpu.VMEM((6, 2 * LK * PITCH, 128), F32), big, big, low, low, part, part]


def filter_forward_lo(samples, vectors, tabs, weights, bias):
    return pl.pallas_call(
        filter_lo_kernel,
        in_specs=[VM] * 10,
        out_specs=[VM] * 2,
        out_shape=[shape((WL, LH, D), BF), shape((SPLIT, 2, LROWS, GD), BF)],
        scratch_shapes=lo_scratch(),
        compiler_params=params(),
        name="filter_forward_lo",
        cost_estimate=cost(35),
    )(samples, vectors, *tabs, *weights, bias)


def filter_back_lo_kernel(
    x_ref, gm_ref, four, vec_ref, tw, twt, th, tht, wu, wv, w1, bias,
    grad_ref, grads, ge, gvec,
    space, us, vs, actp, actm, zr, zi, gs, dp, dm, gsp, gsm, gwu, gwv, gw1,
):
    clear_pads(space, WL, 2 * LK)
    ge[...] = jnp.zeros_like(ge)
    gvec[...] = jnp.zeros_like(gvec)

    def wide(i):
        lo_freq_wide(i, gm_ref[i], tw, space)

    loop(WL, UNROLL, wide)

    def tall(k):
        re, im = lo_freq_tall(k, th, space)
        at = pl.ds(pl.multiple_of(k * PW, PW), PW)
        for g in range(SPLIT):
            cut = slice(g * GD, (g + 1) * GD)
            gs[g, at, :] = lanes(re[:, cut], im[:, cut])

    loop(LK, 3, tall)

    def group(g, _):
        gwu[...] = jnp.zeros_like(gwu)
        gwv[...] = jnp.zeros_like(gwv)
        gw1[...] = jnp.zeros_like(gw1)

        def put(re, im):
            zr[g] = re
            zi[g] = im

        mlp_backward(
            four[g, 0], four[g, 1], gs.at[g], wu[g], wv[g], w1[g], bias.at[g], us, vs, actp, actm,
            dp, dm, gsp, gsm, None, put, gwu, gwv, gw1, ge.at[g], 0, PW, LROWS, LROWS // 2,
        )
        for (layer, part, b), value in block_grads(gwu, gwv, gw1).items():
            at = (2 * layer + part) * NB + 2 * g + b
            grads[at] = value
        return 0

    lax.fori_loop(0, SPLIT, group, 0)

    def back(k):
        at = pl.ds(pl.multiple_of(k * PW, PW), PW)
        re = lanes(*[zr[g, at, :].astype(F32) for g in range(SPLIT)])
        im = lanes(*[zi[g, at, :].astype(F32) for g in range(SPLIT)])
        lo_space_tall(k, tht, re, im, space)

    loop(LK, 3, back)
    gain = vec_ref[0:1, :]

    def last(t, _):
        sums = []
        for n in range(UNROLL):
            i = t * UNROLL + n
            field = lo_space_wide(i, twt, space)[:HL]
            direct = gm_ref[i].astype(F32)[:HL]
            norm, scale = normed(x_ref[i].astype(F32))
            grad = field + direct
            sums.append((jnp.sum(grad * norm, axis=0, keepdims=True), jnp.sum(grad, axis=0, keepdims=True)))
            value = direct + norm_back(grad, norm, scale, gain)
            for c in range(6):
                at = pl.ds(6 * i + c, HL, stride=6 * WL)
                grad_ref[at, 0, :] = value[:, c * 128 : (c + 1) * 128]
        gvec[0:1, :] += sum(a for a, b in sums)
        gvec[1:2, :] += sum(b for a, b in sums)
        return 0

    lax.fori_loop(0, WL // UNROLL, last, 0)


def filter_backward_lo(samples, grad_mixed, four, vectors, tabs, weights, bias):
    big, low, _ = filter_scratch(LROWS, None)
    return pl.pallas_call(
        filter_back_lo_kernel,
        in_specs=[VM] * 12,
        out_specs=[VM] * 4,
        out_shape=[
            shape((HL * WL * 6, 1, 128), F32),
            shape((4 * NB, BS, BS), F32),
            shape((SPLIT, 2, PAIR), F32),
            shape((2, D), F32),
        ],
        scratch_shapes=lo_scratch()
        + [pltpu.VMEM((SPLIT, LROWS, PAIR), F32), big, big, low, low]
        + [pltpu.VMEM((GD, PAIR), F32)] * 2
        + [pltpu.VMEM((PAIR, PAIR), F32)],
        compiler_params=params(),
        name="filter_backward_lo",
        cost_estimate=cost(45),
    )(samples, grad_mixed, four, vectors, *tabs, *weights, bias)


def feed_chunks(n2, cots, c1_ref, wts, out_acc, gn_acc, gw, gc1):
    out_acc[...] = jnp.zeros_like(out_acc)
    gn_acc[...] = jnp.zeros_like(gn_acc)

    def chunk(c, _):
        rows = pl.ds(c * FC, FC)
        low, cot = n2[...].reshape(-1, D), cots[...].reshape(-1, D)
        half, part = divmod(c * FC, FF // 2)
        blocks = slice(part // wts.shape[3], (part + FC) // wts.shape[3])
        wi, wo = (wts[half, blocks, m].reshape(FC, D) for m in range(2))
        hidden = dot_nt(low, wi) + c1_ref[pl.ds(c, 1), :]
        grad = dot_nt(cot, wo)
        square = hidden * hidden
        hp = 0.5 + 0.5 * jnp.tanh(hidden * (K0 + K1 * square))
        act = hidden * hp
        grad = grad * (hp + act * (1.0 - hp) * (2.0 * K0 + 6.0 * K1 * square))
        gc1[pl.ds(c, 1), :] += jnp.sum(grad, axis=0, keepdims=True)
        act = act.astype(BF)
        grad = grad.astype(BF)
        out_acc[...] += dot(act, wo)
        gn_acc[...] += dot(grad, wi)
        gw[1, rows, :] += dot_tn(act, cot)
        gw[0, rows, :] += dot_tn(grad, low)
        return 0

    for c in range(NC):
        chunk(c, 0)


def feed_kernel(high, own_ref, live_ref, *refs):
    count = SPLIT if high else 1
    x_ref, cot_ref = refs[:2]
    fields = refs[2 : 2 + count]
    rest = refs[2 + count :]
    vec_ref, c1_ref = rest[:2]
    weights_here, weights_there = rest[2:4]
    rest = rest[4:]
    if high:
        gw_in, gc1_in, gv_in = rest[:3]
        rest = rest[3:]
    block_ref = rest[0]
    packs = rest[1 : 1 + count]
    rest = rest[1 + count :]
    keep_out = rest[0]
    if high:
        give_out = rest[1]
        rest = rest[1:]
    gc1, gv, wts, wsem, gw, sem, mixed, n2, cots, out_acc, gn_acc, fs = rest[1:]
    step = pl.program_id(0)

    side = lax.rem(own_ref[0], 2)

    @pl.when(step == 0)
    def _():
        loads = [
            pltpu.make_async_copy(weights_here, wts.at[side], wsem.at[0]),
            pltpu.make_async_copy(weights_there, wts.at[1 - side], wsem.at[1]),
        ]
        for load in loads:
            load.start()
        if high:
            load = pltpu.make_async_copy(gw_in, gw, sem)
            load.start()
            load.wait()
            gc1[...] = gc1_in[...]
            gv[...] = gv_in[...]
        else:
            gw[...] = jnp.zeros_like(gw)
            gc1[...] = jnp.zeros_like(gc1)
            gv[...] = jnp.zeros_like(gv)
        for load in loads:
            load.wait()

    own = own_ref[0]
    tall = PW if high else LH
    gain_one, shift_one = vec_ref[0:1, :], vec_ref[1:2, :]
    gain_two, shift_two = vec_ref[2:3, :], vec_ref[3:4, :]
    bias_out = vec_ref[4:5, :]

    def enter(plane, x, cot, field):
        at = pl.ds(plane * tall, tall)
        norm, _unused = normed(x)
        total = field + (norm * gain_one + shift_one) + x
        mixed[at, :] = total
        norm, _unused = normed(total)
        n2[plane] = (norm * gain_two + shift_two).astype(BF)
        cots[plane] = cot.astype(BF)

    def leave(plane):
        at = pl.ds(plane * tall, tall)
        total = mixed[at, :]
        out = total + (out_acc[at, :] + bias_out)
        norm, scale = normed(total)
        grad = gn_acc[at, :]
        cot = cots[plane].astype(F32)
        sums.append(
            tuple(jnp.sum(v, axis=0, keepdims=True) for v in (grad * norm, grad, cot))
        )
        return out.astype(BF), cot + norm_back(grad, norm, scale, gain_two)

    sums = []

    def add_sums():
        for row in range(3):
            gv[row : row + 1, :] += sum(entry[row] for entry in sums)
        sums.clear()

    if high:

        def before():
            for i in range(HB):
                for j in range(SPLIT):
                    fs[i, own ^ j] = fields[j][i]
            for i in range(HB):
                for part, field in enumerate(unpack_pair(fs.at[i])):
                    x = pad_rows(x_ref[part, i].astype(F32))
                    cot = pad_rows(cot_ref[part, i].astype(F32))
                    enter(part * HB + i, x, cot, field)

        def after():
            for i in range(HB):
                grads = []
                for part in range(2):
                    out, grad = leave(part * HB + i)
                    block_ref[part, i] = out[:OWN]
                    grads.append(grad)
                pack_pair(grads[0], grads[1], fs.at[i])
            add_sums()
            for i in range(HB):
                for j in range(SPLIT):
                    packs[j][i] = fs[i, own ^ j]

    else:
        live = live_ref[0].astype(F32)

        def before():
            for i in range(LB):
                x = pad_rows(x_ref[i].astype(F32), LH)
                cot = pad_rows(cot_ref[i].astype(F32), LH) * live
                enter(i, x, cot, fields[0][i].astype(F32))

        def after():
            for i in range(LB):
                out, grad = leave(i)
                block_ref[i] = out[:HL]
                packs[0][i] = grad.astype(BF)
            add_sums()

    before()
    feed_chunks(n2, cots, c1_ref, wts, out_acc, gn_acc, gw, gc1)
    after()

    @pl.when(step == pl.num_programs(0) - 1)
    def _():
        if not high:
            store = pltpu.make_async_copy(gw, keep_out, sem)
            store.start()
            store.wait()
        else:
            mine = lax.rem(own, 2)
            store = pltpu.make_async_copy(gw.at[mine], keep_out, sem)
            store.start()

            def low(c, _):
                rows = pl.ds(pl.multiple_of(c * FC, FC), FC)
                give_out[rows, :] = gw[1 - mine, rows, :].astype(BF)
                return 0

            lax.fori_loop(0, NC, low, 0)
            store.wait()


def feed(high, own, live, samples, cotan, fields, vectors, bias_hidden, weights, earlier):
    planes, tall = (2 * HB, PW) if high else (LB, LH)
    tokens = planes * tall
    if high:
        steps = HALF // HB
        wide, packed, packed_shape = WIDE_BLOCK, PACKED_BLOCK, PACKED
    else:
        steps = WL // LB
        wide = pl.BlockSpec((LB, HL, D), lambda i: (i, 0, 0))
        packed = pl.BlockSpec((LB, LH, D), lambda i: (i, 0, 0))
        packed_shape = (WL, LH, D)
    count = len(fields)
    return pl.pallas_call(
        functools.partial(feed_kernel, high),
        grid=(steps,),
        in_specs=[SM, SM, wide, wide]
        + [packed] * count
        + [VM, VM, ANY, ANY]
        + ([ANY, VM, VM] if high else []),
        out_specs=[wide] + [packed] * count + ([ANY, VM] if high else [ANY]) + [VM, VM],
        out_shape=[shape(samples.shape, BF)]
        + [shape(packed_shape, BF)] * count
        + ([shape((FF, D), F32), shape((FF, D), BF)] if high else [shape((2, FF, D), F32)])
        + [shape((NC, FC), F32), shape((8, D), F32)],
        scratch_shapes=[
            pltpu.VMEM((2, *weights[0].shape), BF),
            pltpu.SemaphoreType.DMA((2,)),
            pltpu.VMEM((2, FF, D), F32),
            pltpu.SemaphoreType.DMA,
            pltpu.VMEM((tokens, D), F32),
            pltpu.VMEM((planes, tall, D), BF),
            pltpu.VMEM((planes, tall, D), BF),
            pltpu.VMEM((tokens, D), F32),
            pltpu.VMEM((tokens, D), F32),
            pltpu.VMEM((HB, SPLIT, PW, PAIR), BF),
        ],
        compiler_params=params(),
        name="feed_hi" if high else "feed_lo",
        cost_estimate=cost(210 if high else 70),
    )(own, live, samples, cotan, *fields, vectors, bias_hidden, *weights, *earlier)


def eye_of(size):
    return lax.broadcasted_iota(jnp.int32, (size, size), 0) == lax.broadcasted_iota(
        jnp.int32, (size, size), 1
    )


def mul(left, right):
    return jnp.dot(left, right, precision=highest, preferred_element_type=F32)


def split_three(values):
    top = values.astype(BF)
    rest = values - top.astype(F32)
    middle = rest.astype(BF)
    return top, middle, (rest - middle.astype(F32)).astype(BF)


TILE = 384


def mul_parts(left, right_ref, parts, full, out, finish=None):
    size = right_ref.shape[0]
    rows = left.shape[0]
    tile = TILE if rows % TILE == 0 else rows

    def cut(i, _):
        at = pl.ds(pl.multiple_of(i * TILE, TILE), TILE)
        for n, part in enumerate(split_three(right_ref[at, :])):
            parts[n, at, :] = part
        return 0

    lax.fori_loop(0, size // TILE, cut, 0)

    def one(i, _):
        at = pl.ds(pl.multiple_of(i * tile, tile), tile)
        top, middle, low = split_three(left[at, :])
        total = dot(lanes(middle, top), parts[0:2].reshape(2 * size, size))
        if full:
            total = total + dot(lanes(low, middle, top), parts[...].reshape(3 * size, size))
        total = total + dot(top, parts[0])
        out[at, :] = total if finish is None else finish(at, total)
        return 0

    lax.fori_loop(0, rows // tile, one, 0)


def newton_kernel(g_ref, x_ref, y_ref, gram, poly, hold, parts, once, twice):
    size = g_ref.shape[0]
    trace = jnp.sum(jnp.where(eye_of(size), g_ref[...], 0.0), keepdims=True)
    scale = 1.0 / (jnp.sqrt(trace) + 1e-07)
    gram[...] = g_ref[...] * (scale * scale)
    y_ref[...] = x_ref[...] * scale

    def turn(full):
        def polynomial(at, square):
            rows = at.start + lax.broadcasted_iota(jnp.int32, (TILE, size), 0)
            diagonal = rows == lax.broadcasted_iota(jnp.int32, (TILE, size), 1)
            return jnp.where(diagonal, newton_a, 0.0) + newton_b * gram[at, :] + newton_c * square

        mul_parts(gram, gram, parts, full, poly, polynomial)
        mul_parts(gram, poly, parts, full, hold)
        mul_parts(y_ref, poly, parts, full, once)
        y_ref[...] = once[...]
        mul_parts(poly, hold, parts, full, gram)

    turn(True)

    def later(_, carry):
        turn(False)
        return carry

    lax.fori_loop(1, NEWTON_STEPS - 1, later, 0)
    mul_parts(y_ref, gram, parts, False, once)
    mul_parts(once, gram, parts, False, twice)
    y_ref[...] = newton_a * y_ref[...] + newton_b * once[...] + newton_c * twice[...]


def newton_one(gram, rows):
    return pl.pallas_call(
        newton_kernel,
        in_specs=[VM] * 2,
        out_specs=VM,
        out_shape=shape(rows.shape, F32),
        scratch_shapes=[pltpu.VMEM((D, D), F32)] * 3
        + [pltpu.VMEM((3, D, D), BF)]
        + [pltpu.VMEM(rows.shape, F32)] * 2,
        compiler_params=params(),
        name="newton",
        cost_estimate=cost(60),
    )(gram, rows)


SWAP = [(0, 1), (1, 0)]


def choose(first, when_first, when_second):
    return jnp.where(first, when_first, when_second)


def both_rows(first, of_first, of_second):
    keep = choose(first, of_first, of_second)
    other = lax.ppermute(choose(first, of_second, of_first), "sc", SWAP)
    return jnp.concatenate(
        [choose(first, keep, other), choose(first, other, keep)], axis=0
    )


def own_rows(first, rows):
    upper, lower = jnp.split(rows, 2, axis=0)
    keep = choose(first, upper, lower)
    other = lax.ppermute(choose(first, lower, upper), "sc", SWAP)
    return choose(first, keep, other), choose(first, other, keep)


def newton_small_kernel(x_ref, y_ref):
    y_ref[...] = newton_rows(x_ref[...])


def newton_small(values):
    return pl.pallas_call(
        newton_small_kernel,
        in_specs=[VM],
        out_specs=VM,
        out_shape=shape(values.shape, F32),
        name="newton_small",
    )(values)


def place(dp, sp):
    return (dp, sp // 2, lax.rem(sp, 2))


def greet(count):
    dp, sp = lax.axis_index("dp"), lax.axis_index("sy") * 2 + lax.axis_index("sc")
    barrier = pltpu.get_barrier_semaphore()
    for o in range(1, count):
        pl.semaphore_signal(
            barrier, inc=1, device_id=place(lax.rem(dp + o, count), sp),
            device_id_type=pl.DeviceIdType.MESH,
        )
    for j in range(1, SPLIT):
        pl.semaphore_signal(
            barrier, inc=1, device_id=place(dp, sp ^ j), device_id_type=pl.DeviceIdType.MESH
        )
    pl.semaphore_wait(barrier, count - 1 + SPLIT - 1)
    return dp, sp


def remote_copy(source, target, out_sem, in_sem, device):
    return pltpu.make_async_remote_copy(
        src_ref=source, dst_ref=target, send_sem=out_sem, recv_sem=in_sem, device_id=device,
        device_id_type=pl.DeviceIdType.MESH,
    )


def send(source, target, out_sem, in_sem, device):
    copy = remote_copy(source, target, out_sem, in_sem, device)
    copy.start()
    return copy


def spread_out(count, dp, sp, jobs):
    copies = []
    for buf, sems in jobs:
        here = buf.at[sp, dp]
        for o in range(1, count):
            to = place(lax.rem(dp + o, count), sp)
            copies.append(send(here, here, sems[0].at[o], sems[1].at[o], to))
    for copy in copies:
        copy.wait()
    copies = []
    for buf, sems in jobs:
        for j in range(1, SPLIT):
            here = buf.at[sp]
            copies.append(send(here, here, sems[2].at[j], sems[3].at[j], place(dp, sp ^ j)))
    for copy in copies:
        copy.wait()


def gather_kernel(count, vec_ref, spec_ref, vec_out, bias, lead, wu, wv, w1, buf, sbuf, *sems):
    height, cols = vec_ref.shape
    rows = spec_ref.shape[0]
    dp, sp = greet(count)
    buf[sp, dp] = jnp.zeros(buf.shape[2:], F32)
    buf[sp, dp, :height, :cols] = vec_ref[...]
    sbuf[sp, dp] = jnp.zeros(sbuf.shape[2:], BF)
    sbuf[sp, dp, :, :BS] = spec_ref[...].astype(BF)
    spread_out(count, dp, sp, [(buf, sems[:4]), (sbuf, sems[4:])])
    for ref in (wu, wv, w1):
        ref[...] = jnp.zeros_like(ref)
    for i in range(count * SPLIT):
        vec_out[:height, i * cols : (i + 1) * cols] = buf[i % SPLIT, i // SPLIT, :height, :cols]
    for g in range(SPLIT):
        cut = slice(g * GD, (g + 1) * GD)
        for layer in range(2):
            row = 9 + 2 * layer
            bias[g, layer : layer + 1, :GD] = vec_out[row : row + 1, cut]
            bias[g, layer : layer + 1, GD:] = vec_out[row + 1 : row + 2, cut]
            for part in (slice(GD), slice(GD, PAIR)):
                lead[g, layer : layer + 1, part] = vec_out[layer : layer + 1, cut]
    for i in range(count * SPLIT):
        value = sbuf[i % SPLIT, i // SPLIT][:, :BS]
        cell, off = divmod(i * rows, BS)
        layer, part, g, b = cell // 16, (cell // 8) % 2, (cell % 8) // 2, cell % 2
        re = slice(b * BS + off, b * BS + off + rows)
        im = slice(GD + b * BS + off, GD + b * BS + off + rows)
        to_re, to_im = slice(b * BS, (b + 1) * BS), slice(GD + b * BS, GD + (b + 1) * BS)
        if layer == 0 and part == 0:
            wu[g, re, to_re] = value
            wv[g, re, to_im] = value
        elif layer == 0:
            wu[g, re, to_im] = value
            wv[g, re, to_re] = -value
        elif part == 0:
            w1[g, re, to_re] = value
            w1[g, im, to_im] = value
        else:
            w1[g, re, to_im] = value
            w1[g, im, to_re] = -value


def dma_sems(*counts):
    return [pltpu.SemaphoreType.DMA((n,)) for n in counts]


def remote(number):
    return pltpu.CompilerParams(
        vmem_limit_bytes=VMEM_LIMIT, collective_id=number, has_side_effects=True
    )


def gather_small(count, vectors, spectral):
    return pl.pallas_call(
        functools.partial(gather_kernel, count),
        in_specs=[VM] * 2,
        out_specs=[VM] * 6,
        out_shape=[
            shape((16, D), F32),
            shape((SPLIT, 2, PAIR), F32),
            shape((SPLIT, 2, PAIR), F32),
            shape((SPLIT, GD, PAIR), BF),
            shape((SPLIT, GD, PAIR), BF),
            shape((SPLIT, PAIR, PAIR), BF),
        ],
        scratch_shapes=[
            pltpu.VMEM((SPLIT, count, 16, 128), F32),
            pltpu.VMEM((SPLIT, count, spectral.shape[0], 128), BF),
        ]
        + dma_sems(count, count, SPLIT, SPLIT) * 2,
        compiler_params=remote(0),
        name="gather_small",
        cost_estimate=cost(70),
    )(vectors, spectral)


def scatter_near(dp, sp, x_ref, land, sems):
    return [
        remote_copy(
            x_ref.at[:, sp ^ j], land.at[j - 1], sems[0].at[j], sems[1].at[j], place(dp, sp ^ j)
        )
        for j in range(1, SPLIT)
    ]


def scatter_far(count, dp, sp, total, land_two, sems):
    copies = []
    for o in range(1, count):
        to = lax.rem(dp + o, count)
        copies.append(
            remote_copy(
                total.at[to], land_two.at[o - 1], sems[2].at[o], sems[3].at[o], place(to, sp)
            )
        )
    return copies


def scatter_total(count, dp, total, land_two):
    result = total[dp]
    for o in range(1, count):
        result = result + land_two[o - 1]
    return result


def scatter_scratch(count, rows, width):
    return [
        pltpu.VMEM((SPLIT - 1, count, rows, width), F32),
        pltpu.VMEM((count, rows, width), F32),
        pltpu.VMEM((count, rows, width), F32),
    ] + dma_sems(SPLIT, SPLIT, count, count)


def spec_kernel(count, x_ref, out_ref, land, total, land_two, *sems):
    dp, sp = greet(count)
    copies = []
    for o in range(1, count):
        to = lax.rem(dp + o, count)
        copies.append(
            send(x_ref.at[to], land.at[o - 1], sems[0].at[o], sems[1].at[o], place(to, sp))
        )
    for copy in copies:
        copy.wait()
    value = x_ref[dp]
    for o in range(1, count):
        value = value + land[o - 1]
    total[...] = value
    copies = []
    for j in range(1, SPLIT):
        source = total.at[sp ^ j]
        copies.append(
            send(source, land_two.at[j - 1], sems[2].at[j], sems[3].at[j], place(dp, sp ^ j))
        )
    for copy in copies:
        copy.wait()
    out_ref[...] = (total[sp] + land_two[0]) + (land_two[1] + land_two[2])


def scatter_spec(count, grads):
    rows = 4 * NB * BS // (count * SPLIT)
    return pl.pallas_call(
        functools.partial(spec_kernel, count),
        in_specs=[VM],
        out_specs=VM,
        out_shape=shape((rows, BS), F32),
        scratch_shapes=[
            pltpu.VMEM((count - 1, SPLIT, rows, BS), F32),
            pltpu.VMEM((SPLIT, rows, BS), F32),
            pltpu.VMEM((SPLIT - 1, rows, BS), F32),
        ]
        + dma_sems(count, count, SPLIT, SPLIT),
        compiler_params=remote(4),
        name="scatter_spec",
        cost_estimate=cost(25),
    )(grads.reshape(count, SPLIT, rows, BS))


def newton_rows(values):
    size = 1.0 / (jnp.sqrt(jnp.sum(values * values, keepdims=True)) + 1e-07)
    values = values * size
    for _ in range(NEWTON_STEPS):
        gram = lax.dot_general(
            values, values, (((0,), (0,)), ((), ())), precision=highest, preferred_element_type=F32
        )
        once = mul(values, gram)
        values = newton_a * values + newton_b * once + newton_c * mul(once, gram)
    return values


def vectors_kernel(
    count, gv_lo, gv_hi, gv, gc1, ge_lo, ge, vec_ref, first_ref, second_ref,
    red_spec, spec_ref, moment_ref,
    new_vec, new_first, new_second, new_spec, new_moment,
    full, esum, x_ref, land, total, land_two, *sems,
):
    height, cols = vec_ref.shape
    dp, sp = greet(count)
    full[...] = jnp.zeros_like(full)
    full[0:2, :] = gv_lo[...] + gv_hi[...]
    full[2:5, :] = gv[0:3, :]
    full[5:9, :] = gc1[...]
    esum[...] = ge_lo[...]
    esum[sp] += ge[...]
    for g in range(SPLIT):
        cut = slice(g * GD, (g + 1) * GD)
        for layer in range(2):
            row = 9 + 2 * layer
            full[row : row + 1, cut] = esum[g, layer : layer + 1, :GD]
            full[row + 1 : row + 2, cut] = esum[g, layer : layer + 1, GD:]
    x_ref[...] = jnp.zeros_like(x_ref)
    for i in range(count * SPLIT):
        x_ref[i // SPLIT, i % SPLIT, :, :cols] = full[:, i * cols : (i + 1) * cols]
    copies = scatter_near(dp, sp, x_ref, land, sems)
    for copy in copies:
        copy.start()
    moment = momentum * moment_ref[...] + red_spec[...]
    new_moment[...] = moment
    push = red_spec[...] + momentum * moment
    if red_spec.shape[0] == BS:
        new_spec[...] = spec_ref[...] * (1.0 - muon_rate * decay) - muon_rate * newton_rows(push)
    else:
        new_spec[...] = push
    for copy in copies:
        copy.wait()
    total[...] = (x_ref[:, sp] + land[0]) + (land[1] + land[2])
    copies = scatter_far(count, dp, sp, total, land_two, sems)
    for copy in copies:
        copy.start()
    for copy in copies:
        copy.wait()
    grad = scatter_total(count, dp, total, land_two)[:height, :cols]
    first = beta_one * first_ref[...] + (1.0 - beta_one) * grad
    second = beta_two * second_ref[...] + (1.0 - beta_two) * grad * grad
    new_first[...] = first
    new_second[...] = second
    first_hat = first / (1.0 - beta_one**STEP)
    second_hat = second / (1.0 - beta_two**STEP)
    new_vec[...] = vec_ref[...] * (1.0 - adam_rate * decay) - adam_rate * first_hat / (
        jnp.sqrt(second_hat) + 1e-08
    )


def update_small(count, pieces, vectors, first, second, red_spec, spectral, moment):
    return pl.pallas_call(
        functools.partial(vectors_kernel, count),
        in_specs=[VM] * 12,
        out_specs=[VM] * 5,
        out_shape=[shape(vectors.shape, F32)] * 3 + [shape(red_spec.shape, F32)] * 2,
        scratch_shapes=[
            pltpu.VMEM((16, D), F32),
            pltpu.VMEM((SPLIT, 2, PAIR), F32),
            pltpu.VMEM((count, SPLIT, 16, 128), F32),
        ]
        + scatter_scratch(count, 16, 128),
        compiler_params=remote(2),
        name="update_small",
        cost_estimate=cost(15),
    )(*pieces, vectors, first, second, red_spec, spectral, moment)


def norm_back_kernel(own_ref, x_ref, m0, m1, m2, m3, f0, f1, f2, f3, vec_ref, grad_ref, gvec, fs, ms):
    @pl.when(pl.program_id(0) == 0)
    def _():
        gvec[...] = jnp.zeros_like(gvec)

    own = own_ref[0]
    gain = vec_ref[0:1, :]

    for i in range(HB):
        for j, (m, f) in enumerate(((m0, f0), (m1, f1), (m2, f2), (m3, f3))):
            ms[i, own ^ j] = m[i]
            fs[i, own ^ j] = f[i]
    sums = []
    for i in range(HB):
        for part, (direct, field) in enumerate(zip(unpack_pair(ms.at[i]), unpack_pair(fs.at[i]))):
            direct, field = direct[:OWN], field[:OWN]
            norm, scale = normed(x_ref[part, i].astype(F32))
            grad = field + direct
            sums.append((jnp.sum(grad * norm, axis=0, keepdims=True), jnp.sum(grad, axis=0, keepdims=True)))
            value = direct + norm_back(grad, norm, scale, gain)
            for c in range(6):
                at = pl.ds(i * (6 * OWN) + c, OWN, stride=6)
                grad_ref[part, at, 0, :] = value[:, c * 128 : (c + 1) * 128]
    gvec[0:1, :] += sum(a for a, b in sums)
    gvec[1:2, :] += sum(b for a, b in sums)


def norm_backward(own, samples, direct, fields, vectors):
    return pl.pallas_call(
        norm_back_kernel,
        grid=(HALF // HB,),
        in_specs=[SM, WIDE_BLOCK] + [PACKED_BLOCK] * (2 * SPLIT) + [VM],
        out_specs=[pl.BlockSpec((2, HB * OWN * 6, 1, 128), lambda i: (0, i, 0, 0)), VM],
        out_shape=[shape((2, HALF * OWN * 6, 1, 128), F32), shape((2, D), F32)],
        scratch_shapes=[pltpu.VMEM((HB, SPLIT, PW, PAIR), BF)] * 2,
        compiler_params=params(),
        name="norm_backward",
        cost_estimate=cost(30),
    )(own, samples, *direct, *fields, vectors)


def reduce_kernel(
    bits, keep, give, moment, new_moment, direction, gram,
    acc, land, red, load_sem, give_sems, *scratch,
):
    half = moment.shape[0] // 2
    dp, sy, sc = (lax.axis_index(name) for name in ("dp", "sy", "sc"))
    swap = (dp, sy, 1 - sc)
    partners = [(dp, 1 - sy, sc)] + [(dp ^ (1 << b), sy, sc) for b in range(bits - 1)]
    mine = [sy] + [lax.rem(dp // (1 << b), 2) for b in range(bits - 1)]
    barrier = pltpu.get_barrier_semaphore()
    for device in [swap] + partners:
        pl.semaphore_signal(barrier, inc=1, device_id=device, device_id_type=pl.DeviceIdType.MESH)
    load = pltpu.make_async_copy(keep, acc, load_sem)
    load.start()
    pl.semaphore_wait(barrier, bits + 1)
    halves = [
        send(give.at[t], land.at[t], give_sems.at[2 * t], give_sems.at[2 * t + 1], swap)
        for t in range(2)
    ]
    load.wait()

    def join_half(t):
        halves[t].wait()

        def join(o, _):
            acc[t, o] = acc[t, o] + land[t, o].astype(F32)
            return 0

        lax.fori_loop(0, 2**bits, join, 0)

    streams = []
    for t in range(2):
        order = list(range(1, bits)) + [0]
        if t == 1:
            order[0], order[1] = order[1], order[0]
        streams.append(order)
    left = [list(range(bits)), list(range(bits))]
    current = [lambda block, t=t: acc.at[t, block] for t in range(2)]
    for stage in range(bits):
        count = 2 ** (bits - 1 - stage)
        copies = []
        for t in range(2):
            outgoing, incoming, _sum, sems = scratch[(stage * 2 + t) * 4 : (stage * 2 + t) * 4 + 4]
            bit = streams[t][stage]
            step = 1 << left[t].index(bit)
            side = mine[bit]
            if stage == 0:
                join_half(t)

            def cast(o, _, t=t, outgoing=outgoing, step=step, side=side):
                block = (o // step) * (2 * step) + (1 - side) * step + lax.rem(o, step)
                outgoing[o] = current[t](block)[...].astype(BF)
                return 0

            lax.fori_loop(0, count, cast, 0)
            copies.append(send(outgoing, incoming, sems.at[0], sems.at[1], partners[bit]))
        following = []
        for t in range(2):
            outgoing, incoming, total, sems = scratch[(stage * 2 + t) * 4 : (stage * 2 + t) * 4 + 4]
            bit = streams[t][stage]
            step = 1 << left[t].index(bit)
            side = mine[bit]
            left[t].remove(bit)
            copies[t].wait()

            def add(o, _, t=t, incoming=incoming, total=total, step=step, side=side):
                block = (o // step) * (2 * step) + side * step + lax.rem(o, step)
                total[o] = current[t](block)[...] + incoming[o].astype(F32)
                return 0

            lax.fori_loop(0, count, add, 0)
            following.append(lambda block, total=total: total.at[block])
        current = following
    for t in range(2):
        red[t * half : (t + 1) * half, :] = current[t](0)[...]
    new = momentum * moment[...] + red[...]
    new_moment[...] = new
    pushed = red[...] + momentum * new
    direction[...] = pushed
    top, middle, low = split_three(pushed)
    gram[...] = (
        (dot_tn(middle, middle) + dot_tn(top, low) + dot_tn(low, top))
        + (dot_tn(top, middle) + dot_tn(middle, top))
    ) + dot_tn(top, top)


def reduce_feed(count, keep, give, moment):
    rows = moment.shape[0]
    blocks = FF // rows
    bits = blocks.bit_length() - 1
    whole = (2, blocks, rows // 2, D)
    scratch = []
    for stage in range(bits):
        for _ in range(2):
            part = (2 ** (bits - 1 - stage), rows // 2, D)
            scratch += [pltpu.VMEM(part, BF), pltpu.VMEM(part, BF), pltpu.VMEM(part, F32)] + dma_sems(2)
    return pl.pallas_call(
        functools.partial(reduce_kernel, bits),
        in_specs=[ANY, ANY, VM],
        out_specs=[VM] * 3,
        out_shape=[shape((rows, D), F32)] * 2 + [shape((D, D), F32)],
        scratch_shapes=[
            pltpu.VMEM(whole, F32),
            pltpu.VMEM(whole, BF),
            pltpu.VMEM((rows, D), F32),
            pltpu.SemaphoreType.DMA,
        ]
        + dma_sems(4)
        + scratch,
        compiler_params=pltpu.CompilerParams(
            vmem_limit_bytes=VMEM_LIMIT, collective_id=1, has_side_effects=True
        ),
        name="reduce_feed",
        cost_estimate=cost(80),
    )(keep.reshape(whole), give.reshape(whole), moment)


def after(values, earlier):
    return lax.optimization_barrier((values, earlier))[0]


def body(
    count, samples_hi, samples_lo, cotan_hi, cotan_lo, live_slots, spectral_w, vectors, weight_in,
    weight_out, moment_spec, moment_in, moment_out, adam_first, adam_second,
):
    axes = ("dp", *SP)
    chips = ("dp", "sy")
    sp = lax.axis_index(SP)
    first = lax.axis_index("sc") == 0
    own = sp.astype(jnp.int32).reshape(1)
    wide, tall, wide_lo, tall_lo = (t.astype(BF) for t in tables())
    tabs = (wide, np.swapaxes(wide, 1, 2), tall, tall.T)
    tabs_lo = (wide_lo, wide_lo.T, tall_lo, tall_lo.T)
    tabs = tuple(jnp.asarray(np.ascontiguousarray(t)) for t in tabs)
    tabs_lo = tuple(jnp.asarray(np.ascontiguousarray(t)) for t in tabs_lo)

    own_width = weight_in.shape[1]
    split_hi = samples_hi.reshape(2, HALF, OWN, D)
    split_cot = cotan_hi.reshape(2, HALF, OWN, D)
    one_lo = samples_lo.reshape(HL, WL, D).transpose(1, 0, 2)
    one_cot = cotan_lo.reshape(HL, WL, D).transpose(1, 0, 2)

    moment = both_rows(first, moment_in.T, moment_out)
    piece = jnp.stack([weight_in.T.astype(BF), weight_out.astype(BF)])
    here = lax.all_gather(piece, chips, axis=0)
    packed = norm_packed(own, split_hi)
    vec, bias, lead, *weights = gather_small(count, *after((vectors, spectral_w), packed))
    bias_hidden = vec[5:9].reshape(2 * count, 2, own_width).transpose(1, 0, 2).reshape(NC, FC)
    slabs = after(exchange(packed), vec)
    slabs, here = after((slabs, here), (slabs[1], here))
    feed_weights = (here, lax.ppermute(here, "sc", SWAP))
    fields, four = filter_forward(own, slabs, tabs, weights, bias, lead)
    lo_after = after(one_lo, fields)
    fields = exchange(fields)
    field_lo, four_lo = filter_forward_lo(lo_after, vec, tabs_lo, weights, bias)
    block_lo, gm_lo, gw, gc1, gv = feed(
        False, own, live_slots, one_lo, one_cot, [field_lo], vec, bias_hidden, feed_weights, ()
    )
    block_hi, p0, p1, p2, p3, keep, give, gc1, gv = feed(
        True, own, live_slots, split_hi, split_cot, fields, vec, bias_hidden, feed_weights,
        (gw, gc1, gv),
    )
    packs = [p0, p1, p2, p3]
    grad_slabs = exchange(packs)
    new_moment, direction, gram = reduce_feed(count, keep, give, moment)
    gram = lax.psum(gram, chips)
    gm_lo, grad_slabs = after((gm_lo, grad_slabs), (direction, grad_slabs[1]))
    grad_lo, gspec, ge_lo, gv_lo = filter_backward_lo(
        one_lo, gm_lo, four_lo, vec, tabs_lo, weights, bias
    )
    back, gspec, ge = filter_backward(own, grad_slabs, four, tabs, weights, bias, gspec)
    red_spec = scatter_spec(count, gspec)
    back, gram = after((back, gram), red_spec)
    back = exchange(back)
    orth = newton_one(gram, direction)
    back = after(back, orth)
    grad_hi, gv_hi = norm_backward(own, split_hi, packs, back, vec)
    gc1 = gc1.reshape(2, 2 * count, own_width).transpose(1, 0, 2).reshape(4, D)
    new_vectors, new_adam_first, new_adam_second, new_spectral, new_moment_spec = update_small(
        count, (gv_lo, gv_hi, gv, gc1, ge_lo, ge), vectors, adam_first, adam_second,
        red_spec, spectral_w, moment_spec,
    )
    new_moment_in, new_moment_out = own_rows(first, new_moment)
    orth_in, orth_out = own_rows(first, orth)

    keep_share = 1.0 - muon_rate * decay
    new_weight_in = weight_in * keep_share - muon_rate * orth_in.T
    new_weight_out = weight_out * keep_share - muon_rate * math.sqrt(max(1.0, FF / D)) * orth_out
    rows = moment_spec.shape[0]
    if rows != BS:
        gathered = lax.all_gather(new_spectral, SP, axis=0, tiled=True)
        orth_spec = lax.dynamic_slice_in_dim(newton_small(gathered), sp * rows, rows, 0)
        new_spectral = spectral_w * keep_share - muon_rate * orth_spec
    return (
        block_hi.reshape(samples_hi.shape),
        block_lo.transpose(1, 0, 2).reshape(samples_lo.shape),
        grad_hi.reshape(samples_hi.shape),
        grad_lo.reshape(samples_lo.shape),
        new_spectral,
        new_weight_in,
        new_weight_out,
        new_moment_spec,
        new_moment_in.T,
        new_moment_out,
        new_vectors,
        new_adam_first,
        new_adam_second,
    )


def solution(mesh):
    count = mesh.shape["dp"]
    fine = jax.sharding.Mesh(mesh.devices.reshape(count, 2, 2), ("dp", *SP))
    both = ("dp", *SP)
    hi = P("dp", None, SP, None)
    lo = P(both, None, None, None)
    rows = P(both, None)
    cols = P(None, both)
    return jax.shard_map(
        functools.partial(body, count),
        mesh=fine,
        in_specs=(hi, lo, hi, lo, P(both), rows, cols, cols, rows, rows, cols, rows, cols, cols),
        out_specs=(hi, lo, hi, lo, rows, cols, rows, rows, cols, rows, cols, cols, cols),
        check_vma=False,
    )
```
